128 devices in a mesh: seq: 4 (over z), tm: 32 (over y, x, core).
Axes of the slice: x: 4, y: 4, z: 4, core: 2. Of those that a mesh axis runs over, the one named last changes fastest.
Arguments:
- inputs: float32 [4, 8192, 64], P('seq', 'tm'), may hold values from -6 to 6
- guess: float32 [4, 8192, 64], P('seq', 'tm'), may hold values from -0.9 to 0.9
- cotangent: float32 [4, 8192, 64], P('seq', 'tm'), may hold values from -0.4 to 0.4
- w_input: float32 [64, 192], replicated, may hold values from -0.75 to 0.75
- w_hidden: float32 [64, 192], replicated, may hold values from -0.75 to 0.75
- bias: float32 [256], replicated, may hold values from -2 to 13, as said below
Outputs:
- new_states: float32 [4, 8192, 64], P('seq', 'tm')
- adjoint: float32 [4, 8192, 64], P('seq', 'tm')
- grad_input: float32 [64, 192], replicated
- grad_hidden: float32 [64, 192], replicated
- grad_bias: float32 [256], replicated
The draws below stay inside these ranges and needn't reach their ends.
Inputs may be any that keep to these rules, and one draw needn't show every extreme that they name: `bias`: gate biases as laid out in the meaning.
All inputs are finite; a program needn't handle non-finite values.
Results may differ from the reference program's by a relative error of at most 0.00075.
Values sent between devices are 32-bit elements; how exact they have to be, the bound alone decides.
No kernel may reach another device: no remote copies, remote signals or barrier semaphores. Data moves between devices by JAX's collectives and lax.ppermute only.
A program may use at most 128 MiB of HBM per device.

```python
import math
import jax
import jax.numpy as jnp
from jax import lax

D = 64
H = 64
SEQS = 4
SEQLEN = 8192


def draw_bias(key, part):
    keys = jax.random.split(key, 6)
    reset_part = jnp.clip(0.5 * jax.random.normal(keys[0], (H,), jnp.float32), -2.0, 2.0)
    slow_share = 0.5
    slow = jax.random.bernoulli(keys[1], slow_share, (H,))
    leak = jnp.exp(jax.random.uniform(keys[2], (H,), jnp.float32, jnp.log(0.5), jnp.log(3.0)))
    slow_bias = jnp.log(2.0 * SEQLEN / leak)
    fast_bias = jax.random.uniform(keys[3], (H,), jnp.float32, 1.0, 3.9)
    update_part = jnp.where(slow, slow_bias, fast_bias)
    cand_part = jnp.clip(0.5 * jax.random.normal(keys[4], (H,), jnp.float32), -2.0, 2.0)
    hidden_part = jnp.clip(0.5 * jax.random.normal(keys[5], (H,), jnp.float32), -2.0, 2.0)
    return jnp.concatenate([reset_part, update_part, cand_part, hidden_part]).astype(jnp.float32)


def levels(key, dims, cuts, smallest, top_value):
    level = 1.0
    for dim, blocks in cuts:
        draws = jax.random.uniform(jax.random.fold_in(jax.random.fold_in(key, 6), dim), (blocks,), jnp.float32, smallest / len(cuts), top_value / len(cuts))
        level = level * jnp.repeat(jnp.exp(draws), dims[dim] // blocks).reshape((-1,) + (1,) * (len(dims) - 1 - dim))
    return level


def centred(stream_key, dims, scale, bound, cuts=(), kind=jnp.bfloat16):
    gain = levels(stream_key, dims, cuts, -0.22, 0.18) if cuts else 1.0
    array = jax.random.normal(stream_key, dims, jnp.float32) * scale * gain
    return jnp.minimum(jnp.maximum(array, -bound), bound).astype(kind)


def setup_inputs(seed: int = 0) -> dict:
    key_of = jax.random.split(jax.random.key(seed), 7)
    inputs = centred(key_of[0], (SEQS, SEQLEN, D), 1.0, 6.0, ((0, 4), (1, 32)), jnp.float32)
    guess = jnp.clip(jax.random.uniform(key_of[1], (SEQS, SEQLEN, H), jnp.float32, -0.9, 0.9) * levels(key_of[1], (SEQS, SEQLEN, H), ((0, 4), (1, 32)), -0.4, 0.0), -0.9, 0.9)
    cotangent = centred(key_of[2], (SEQS, SEQLEN, H), 0.05, 0.4, ((0, 4), (1, 32)), jnp.float32)
    w_input = centred(key_of[3], (D, 3 * H), D ** -0.5, 0.75, (), jnp.float32)
    w_hidden = centred(key_of[4], (H, 3 * H), H ** -0.5, 0.75, (), jnp.float32)
    bias = draw_bias(jax.random.fold_in(key_of[6], 71), 0)
    return dict(inputs=inputs, guess=guess, cotangent=cotangent, w_input=w_input, w_hidden=w_hidden, bias=bias)


HIGHEST = lax.Precision.HIGHEST

def cell(inputs, prev, w_input, w_hidden, bias):
    width = prev.shape[-1]
    gate_in = jnp.einsum('...d,dk->...k', inputs, w_input, precision=HIGHEST) + bias[:3 * width]
    gate_hid = jnp.einsum('...j,jk->...k', prev, w_hidden, precision=HIGHEST)
    reset = jax.nn.sigmoid(gate_in[..., :width] + gate_hid[..., :width])
    update = jax.nn.sigmoid(gate_in[..., width:2 * width] + gate_hid[..., width:2 * width])
    hsum = gate_hid[..., 2 * width:] + bias[3 * width:]
    cand = jnp.tanh(gate_in[..., 2 * width:] + reset * hsum)
    value = (1.0 - update) * cand + update * prev
    return (value, (reset, update, cand, hsum))

def jacobian(prev, w_hidden, reset, update, cand, hsum):
    width = prev.shape[-1]
    w_reset = w_hidden[:, :width].T
    w_update = w_hidden[:, width:2 * width].T
    w_cand = w_hidden[:, 2 * width:].T
    squash = (1.0 - update) * (1.0 - cand * cand)
    coef_cand = squash * reset
    coef_reset = squash * hsum * reset * (1.0 - reset)
    coef_update = (prev - cand) * update * (1.0 - update)
    identity_mat = jnp.eye(width, dtype=jnp.float32)
    return coef_cand[..., :, None] * w_cand + coef_reset[..., :, None] * w_reset + coef_update[..., :, None] * w_update + update[..., :, None] * identity_mat

def reference(inputs, guess, cotangent, w_input, w_hidden, bias):
    prev = jnp.concatenate([jnp.zeros_like(guess[:, :1]), guess[:, :-1]], axis=1)
    value, parts = cell(inputs, prev, w_input, w_hidden, bias)
    series = tuple((jnp.moveaxis(a, 1, 0) for a in (prev, value, cotangent) + parts))

    def forward_step(state, items):
        prev_t, value_t, cot_t, reset, update, cand, hsum = items
        jac = jacobian(prev_t, w_hidden, reset, update, cand, hsum)
        shift = value_t - jnp.einsum('sij,sj->si', jac, prev_t, precision=HIGHEST)
        state = jnp.einsum('sij,sj->si', jac, state, precision=HIGHEST) + shift
        return (state, state)

    def backward_step(carry, items):
        prev_t, value_t, cot_t, reset, update, cand, hsum = items
        jac = jacobian(prev_t, w_hidden, reset, update, cand, hsum)
        lam = cot_t + carry
        carry = jnp.einsum('sji,sj->si', jac, lam, precision=HIGHEST)
        return (carry, lam)
    start = jnp.zeros_like(guess[:, 0])
    unused, states = lax.scan(forward_step, start, series)
    unused, lams = lax.scan(backward_step, start, series, reverse=True)
    new_states = jnp.moveaxis(states, 0, 1)
    adjoint = jnp.moveaxis(lams, 0, 1)
    unused, pullback = jax.vjp(lambda a, b, c: cell(inputs, prev, a, b, c)[0], w_input, w_hidden, bias)
    grad_a, grad_b, grad_c = pullback(adjoint)
    scale = 1.0 / math.sqrt(SEQS * SEQLEN)
    return (new_states, adjoint, grad_a * scale, grad_b * scale, grad_c * scale)
```

```python
import math

import jax
import jax.numpy as jnp
from jax import lax
from jax.experimental import pallas as pl
from jax.experimental.pallas import tpu as pltpu
from jax.sharding import PartitionSpec as P

F32 = jnp.float32
BF16 = jnp.bfloat16
HIGHEST = lax.Precision.HIGHEST
H = 64
T = 256
RUN = 16
PAIRS = 8
DEV = 32
HALF = DEV // 2
TILE = 40
VMEM_LIMIT = 48 * 1024 * 1024


def dot(a, b, dims=((1,), (0,))):
    return lax.dot_general(a, b, (dims, ((), ())), precision=HIGHEST, preferred_element_type=F32)


def bdot(a, b):
    return jnp.dot(a, b, preferred_element_type=F32)


def iota(shape, axis):
    return lax.broadcasted_iota(jnp.int32, shape, axis)


def split(a):
    high = a.astype(BF16)
    return high, (a - high.astype(F32)).astype(BF16)


def sigmoid(a):
    return 1.0 / (1.0 + jnp.exp(-a))


def doubled(block):
    zero = jnp.zeros_like(block)
    return jnp.concatenate(
        [jnp.concatenate([block, zero], axis=1), jnp.concatenate([zero, block], axis=1)], axis=0
    )


def forward_weights(wh):
    wide = jnp.concatenate(
        [doubled(wh[:, 128:192]), doubled(wh[:, :64]), doubled(wh[:, 64:128])], axis=1
    )
    high, low = split(wide)
    return jnp.concatenate([high, high, low], axis=0)


def backward_weights(wh):
    tall = jnp.concatenate(
        [doubled(wh[:, 128:192].T), doubled(wh[:, :64].T), doubled(wh[:, 64:128].T)], axis=0
    )
    high, low = split(tall)
    return jnp.concatenate([high, high, low], axis=0)


def three(a):
    high, low = split(a)
    return jnp.concatenate([high, low, high], axis=1)


def to_row(column, offset):
    hit = iota((H, 128), 1) == iota((H, 128), 0) + offset
    return jnp.sum(jnp.where(hit, column, 0.0), axis=0, keepdims=True)


def gate_terms(gi_r, gi_z, gi_n, gh_r, gh_z, gh_n, bias_h, prev):
    reset = sigmoid(gi_r + gh_r)
    update = sigmoid(gi_z + gh_z)
    keep = sigmoid(-(gi_z + gh_z))
    hsum = gh_n + bias_h
    cand = jnp.tanh(gi_n + reset * hsum)
    squash = keep * (1.0 - cand * cand)
    p = squash * reset
    q = squash * hsum * reset * (1.0 - reset)
    w = (prev - cand) * update * keep
    shift = keep * cand - p * gh_n - q * gh_r - w * gh_z
    return squash, p, q, w, update, shift


def packed(a):
    return jnp.concatenate([a[:, :128], a[:, 128:]], axis=0).T


def combine(earlier, later):
    row, lane = iota((72, 128), 0), iota((72, 128), 1)
    product = dot(earlier[:, :H], later[:H, :])
    return (
        product
        + jnp.where((lane == H) & (row < H), earlier, 0.0)
        + jnp.where((row == H) & (lane < H), later, 0.0)
    )


def blocks_kernel(
    x_ref, g_ref, c_ref, wi_ref, wh_ref, bias_ref,
    send_ref, aug_ref, sup_ref, pk_ref, tl_ref,
    y_ref, z_ref, b_ref, lhs_ref, w_ref,
):
    wh = wh_ref[...]
    w_ref[...] = forward_weights(wh)
    guess = g_ref[...]
    prev = pltpu.roll(guess, 1, 1)
    gi = dot(wi_ref[...], x_ref[...], ((0,), (0,)))
    gh = dot(wh, prev, ((0,), (0,)))
    bias0 = jnp.broadcast_to(bias_ref[0:1, :], (128, 128)).T
    bias1 = jnp.broadcast_to(bias_ref[1:2, :], (128, 128)).T
    bias0 = jnp.concatenate([bias0, bias0], axis=1)
    bias1 = jnp.concatenate([bias1, bias1], axis=1)
    gi_r = gi[:64] + bias0[:64]
    gi_z = gi[64:128] + bias0[64:]
    gi_n = gi[128:] + bias1[:64]
    squash, p, q, w, u, shift = gate_terms(
        gi_r, gi_z, gi_n, gh[:64], gh[64:128], gh[128:], bias1[64:], prev
    )
    tl_ref[0], tl_ref[1], tl_ref[2], tl_ref[3] = squash, p, q, w
    first = iota((H, T), 1) == 0
    pk_ref[0] = packed(jnp.where(first, 0.0, p))
    pk_ref[1] = packed(jnp.where(first, 0.0, q))
    pk_ref[2] = packed(jnp.where(first, 0.0, w))
    pk_ref[3] = packed(jnp.where(first, 1.0, u))
    pk_ref[4] = packed(jnp.where(first, 0.0, shift))
    pk_ref[5] = packed(c_ref[...])

    lane64 = iota((H, 128), 1)
    low64 = lane64 < H
    eye2 = jnp.where((lane64 == iota((H, 128), 0)) | (lane64 == iota((H, 128), 0) + H), 1.0, 0.0)
    wn2 = jnp.concatenate([wh[:, 128:192], wh[:, 128:192]], axis=1)
    wr2 = jnp.concatenate([wh[:, :64], wh[:, :64]], axis=1)
    wz2 = jnp.concatenate([wh[:, 64:128], wh[:, 64:128]], axis=1)

    def rows(k, step):
        return pk_ref[k, pl.ds(step, PAIRS, stride=RUN), :]

    def put(c, value, cot):
        y_ref[c] = value
        high, low = split(value)
        lhs_ref[c * H:(c + 1) * H, 0:128] = high
        lhs_ref[c * H:(c + 1) * H, 128:256] = low
        lhs_ref[c * H:(c + 1) * H, 256:384] = high
        return value * cot

    def put_b(value):
        b_ref[...] = value
        lhs_ref[512:528, :] = three(jnp.concatenate([value, jnp.zeros_like(value)], axis=0))

    p0, q0, w0, u0, s0, c0 = [rows(k, 0) for k in range(6)]
    for c in range(PAIRS):
        value = (
            p0[c:c + 1] * wn2 + q0[c:c + 1] * wr2 + w0[c:c + 1] * wz2 + u0[c:c + 1] * eye2
        )
        z_ref[c] = put(c, value, c0[c:c + 1])
    put_b(s0)

    def step(l, carry):
        p1, q1, w1, u1, s1, c1 = [rows(k, l) for k in range(6)]
        prod = bdot(lhs_ref[...], w_ref[...])
        for c in range(PAIRS):
            part = prod[c * H:(c + 1) * H]
            value = (
                u1[c:c + 1] * y_ref[c] + p1[c:c + 1] * part[:, :128]
                + q1[c:c + 1] * part[:, 128:256] + w1[c:c + 1] * part[:, 256:]
            )
            z_ref[c] += put(c, value, c1[c:c + 1])
        part = prod[512:520]
        put_b(u1 * b_ref[...] + p1 * part[:, :128] + q1 * part[:, 128:256] + w1 * part[:, 256:] + s1)
        return carry

    lax.fori_loop(1, RUN, step, 0)

    low8 = iota((8, 128), 1) < H
    top8 = iota((8, 128), 0) == 0
    bs = b_ref[...]
    for c in range(PAIRS):
        y = y_ref[c]
        z = z_ref[c]
        offs = jnp.broadcast_to(bs[c:c + 1], (8, 128))
        for part in range(2):
            if part:
                y, z, offs = pltpu.roll(y, H, 1), pltpu.roll(z, H, 1), pltpu.roll(offs, H, 1)
            col = jnp.sum(jnp.where(low64, z, 0.0), axis=1, keepdims=True)
            n = c + part * PAIRS
            aug_ref[n, 0:64, :] = jnp.where(low64, y, jnp.where(lane64 == H, col, 0.0))
            aug_ref[n, 64:72, :] = jnp.where(low8 & top8, offs, 0.0)
    sups = []
    for k in range(4):
        left = combine(aug_ref[4 * k], aug_ref[4 * k + 1])
        right = combine(aug_ref[4 * k + 2], aug_ref[4 * k + 3])
        sups.append(combine(left, right))
        sup_ref[k] = sups[-1]
    total = combine(combine(sups[0], sups[1]), combine(sups[2], sups[3]))

    low32 = iota((32, 128), 1) < H
    body = jnp.where(low32, total[:32], pltpu.roll(total[32:64], H, 1))
    col = jnp.sum(jnp.where(lane64 == H, total[:64], 0.0), axis=1, keepdims=True)
    row_bc = jnp.where(low8[:1], total[64:65], 0.0) + to_row(col, H)
    last = jnp.sum(jnp.where(lane64 == 127, guess[:, 128:], 0.0), axis=1, keepdims=True)

    def head(a):
        return jnp.sum(jnp.where(lane64 == 0, a[:, :128], 0.0), axis=1, keepdims=True)

    row_gr = to_row(last, 0) + to_row(head(gi_r), H)
    row_zn = to_row(head(gi_z), 0) + to_row(head(gi_n), H)
    row8 = iota((8, 128), 0)
    tail = jnp.where(row8 == 0, row_bc, jnp.where(row8 == 1, row_gr, jnp.where(row8 == 2, row_zn, 0.0)))
    for k in range(DEV):
        send_ref[k, 0:32, :] = body
        send_ref[k, 32:40, :] = tail


def apply_kernel(
    me_ref, r_ref, aug_ref, sup_ref, pk_ref, tl_ref, x_ref, g_ref, wh_ref, bias_ref,
    state_ref, adj_ref, grad_ref,
    w_ref, wt_ref, lhs_ref, z_ref, d_ref, row_ref, bnd_ref, st_ref, lam_ref,
):
    me = me_ref[0]
    wh = wh_ref[...]
    w_ref[...] = forward_weights(wh)
    wt_ref[...] = backward_weights(wh)
    bias_h = bias_ref[1:2, 64:]

    bc = r_ref[:, 32, :]
    gr = r_ref[:, 33, :]
    zn = r_ref[:, 34, :]
    prev = jnp.where(iota((DEV, H), 0) == DEV - 1, 0.0, gr[:, :H])
    gr_next = pltpu.roll(gr, DEV - 1, 0)
    zn_next = pltpu.roll(zn, DEV - 1, 0)
    gh = dot(prev, wh)
    terms = gate_terms(
        gr_next[:, H:], zn_next[:, :H], zn_next[:, H:],
        gh[:, :64], gh[:, 64:128], gh[:, 128:], bias_h, prev,
    )
    for k in range(6):
        bnd_ref[k] = jnp.concatenate([terms[k], terms[k]], axis=1)
    bnd_ref[6] = jnp.concatenate([prev, prev], axis=1)
    row_ref[...] = bc

    def pair(a):
        return jnp.concatenate([a[:HALF], a[HALF:]], axis=1)

    p, q, w, u, shift = [pair(terms[k]) for k in (1, 2, 3, 4, 5)]
    lane64 = iota((H, 128), 1)
    row64 = iota((H, 128), 0)
    low32 = iota((32, 128), 1) < H
    for k in range(HALF):
        a, b = r_ref[k, 0:32, :], r_ref[k + HALF, 0:32, :]
        top = jnp.where(low32, a, pltpu.roll(b, H, 1))
        bottom = jnp.where(low32, pltpu.roll(a, H, 1), b)
        value = jnp.concatenate([top, bottom], axis=0)
        z_ref[k] = value
        lhs_ref[k * H:(k + 1) * H, :] = three(value)
    offs = pair(bc[:, :H])
    lhs_ref[HALF * H:, :] = three(offs)
    prod = bdot(lhs_ref[...], w_ref[...])
    for k in range(HALF):
        part = prod[k * H:(k + 1) * H]
        z_ref[k] = (
            u[k:k + 1] * z_ref[k] + p[k:k + 1] * part[:, :128]
            + q[k:k + 1] * part[:, 128:256] + w[k:k + 1] * part[:, 256:]
        )
    part = prod[HALF * H:]
    d_ref[...] = u * offs + p * part[:, :128] + q * part[:, 128:256] + w * part[:, 256:] + shift

    lane1 = iota((1, 128), 1)
    eye_a = lane64 == row64
    eye_b = lane64 == row64 + H

    def fwd(eye, base):
        def lap(k, x):
            col = jnp.sum(jnp.where(eye, x, 0.0), axis=1, keepdims=True)
            return jnp.sum(col * z_ref[k - base], axis=0, keepdims=True) + d_ref[pl.ds(k - base, 1), :]
        return lap

    x = bnd_ref[5, DEV - 1:DEV, :]
    x = lax.fori_loop(0, jnp.minimum(me, HALF), fwd(eye_a, 0), x)
    x = lax.fori_loop(HALF, me, fwd(eye_b, HALF), pltpu.roll(x, H, 1))
    x = pltpu.roll(x, H, 1)

    def bwd(eye, base, turn, keep):
        def lap(i, lam):
            k = base - i
            col = jnp.sum(z_ref[k % HALF] * lam, axis=1, keepdims=True)
            extra = row_ref[pl.ds(k, 1), :]
            if turn:
                extra = pltpu.roll(extra, H, 1)
            return jnp.sum(jnp.where(eye, col, 0.0), axis=0, keepdims=True) + jnp.where(keep, extra, 0.0)
        return lap

    lam = jnp.where(lane1 >= H, row_ref[DEV - 1:DEV, :], 0.0)
    lam = lax.fori_loop(
        0, DEV - 1 - jnp.maximum(me + 1, HALF), bwd(eye_b, DEV - 2, False, lane1 >= H), lam
    )
    lam = lax.fori_loop(
        0, jnp.maximum(HALF - 1 - me, 0), bwd(eye_a, HALF - 1, True, lane1 < H), pltpu.roll(lam, H, 1)
    )
    row_terms = [bnd_ref[k, pl.ds(me, 1), :] for k in range(6)]
    lam8 = jnp.broadcast_to(lam, (8, 128))[:, :H]
    wide = jnp.concatenate([lam8 * row_terms[k][:, :H] for k in (1, 2, 3)], axis=1)
    tall = jnp.concatenate([wh[:, 128:192].T, wh[:, :64].T, wh[:, 64:128].T], axis=0)
    carry = (dot(wide, tall) + lam8 * row_terms[4][:, :H])[0:1]
    carry = jnp.where(me == DEV - 1, 0.0, carry)
    carry = jnp.concatenate([carry, jnp.zeros_like(carry)], axis=1)

    row72 = iota((72, 128), 0)
    eye72 = iota((72, 128), 1) == row72
    one = lane1 == H

    def ahead(maps, x):
        col = jnp.sum(jnp.where(eye72, x, 0.0), axis=1, keepdims=True)
        return jnp.where(one, 1.0, jnp.sum(col * maps, axis=0, keepdims=True))

    def back(maps, lam):
        col = jnp.sum(maps[:H] * lam, axis=1, keepdims=True)
        return jnp.where(one, 1.0, jnp.sum(jnp.where(eye_a, col, 0.0), axis=0, keepdims=True))

    starts = [jnp.where(one, 1.0, x)]
    for k in range(3):
        starts.append(ahead(sup_ref[k], starts[-1]))
    ends = [jnp.where(one, 1.0, carry)]
    for k in (3, 2, 1):
        ends.append(back(sup_ref[k], ends[-1]))
    ends = ends[::-1]
    state_rows, carry_rows = [None] * 16, [None] * 16
    for k in range(4):
        value, lam = starts[k], ends[k]
        for j in range(4):
            state_rows[4 * k + j] = value
            carry_rows[4 * k + 3 - j] = lam
            if j < 3:
                value = ahead(aug_ref[4 * k + j], value)
                lam = back(aug_ref[4 * k + 3 - j], lam)

    def gather(items):
        left = jnp.concatenate(items[:8], axis=0)
        right = jnp.concatenate(items[8:], axis=0)
        return jnp.where(iota((8, 128), 1) < H, left, pltpu.roll(right, H, 1))

    def rows(k, step):
        return pk_ref[k, pl.ds(step, PAIRS, stride=RUN), :]

    def pad(a):
        return jnp.concatenate([a, jnp.zeros_like(a)], axis=0)

    def lap(i, both):
        state, kappa = both
        j = RUN - 1 - i
        prod = bdot(three(pad(state)), w_ref[...])[:8]
        lam = rows(5, j) + kappa
        lam_ref[pl.ds(j, PAIRS, stride=RUN), :] = lam
        mixed = jnp.concatenate([lam * rows(0, j), lam * rows(1, j), lam * rows(2, j)], axis=1)
        kappa = bdot(three(pad(mixed)), wt_ref[...])[:8] + lam * rows(3, j)
        state = (
            rows(3, i) * state + rows(0, i) * prod[:, :128] + rows(1, i) * prod[:, 128:256]
            + rows(2, i) * prod[:, 256:] + rows(4, i)
        )
        st_ref[pl.ds(i, PAIRS, stride=RUN), :] = state
        return state, kappa

    lax.fori_loop(0, RUN, lap, (gather(state_rows), gather(carry_rows)))
    states = st_ref[...].T
    state_ref[:, :128] = states[:H]
    state_ref[:, 128:] = states[H:]
    lams = lam_ref[...].T
    lams = jnp.concatenate([lams[:H], lams[H:]], axis=1)
    adj_ref[...] = lams

    before = (me + DEV - 1) % DEV
    first = iota((H, T), 1) == 0

    def with_first(a, k):
        col = jnp.sum(jnp.where(eye_a, bnd_ref[k, pl.ds(before, 1), :], 0.0), axis=1, keepdims=True)
        return jnp.where(first, col, a)

    squash, p, q, w = [with_first(tl_ref[k], k) for k in range(4)]
    prev = with_first(pltpu.roll(g_ref[...], 1, 1), 6)
    left = jnp.concatenate([x_ref[...], prev, jnp.ones((8, T), F32)], axis=0)
    right = jnp.concatenate([lams * q, lams * w, lams * squash, lams * p], axis=0)
    sums = dot(left, right, ((1,), (1,)))
    grad_ref[0:64, :] = sums[:64, :128]
    grad_ref[64:128, :] = sums[64:128, :128]
    grad_ref[128:192, :] = jnp.where(lane64 < H, sums[:64, 128:], sums[64:128, 128:])
    row8 = iota((8, 128), 0)
    grad_ref[192:200, :] = jnp.where(
        row8 == 0, sums[128:136, :128], jnp.where(row8 == 1, sums[128:136, 128:], 0.0)
    )
    grad_ref[200:, :] = jnp.zeros((56, 128), F32)


def shape(*dims):
    return jax.ShapeDtypeStruct(dims, F32)


def per_device(inputs, guess, cotangent, w_input, w_hidden, bias):
    x = jnp.swapaxes(inputs[0], 0, 1)
    g = jnp.swapaxes(guess[0], 0, 1)
    c = jnp.swapaxes(cotangent[0], 0, 1)
    bias2 = bias.reshape(2, 128)
    vmem = pl.BlockSpec(memory_space=pltpu.VMEM)
    params = pltpu.CompilerParams(vmem_limit_bytes=VMEM_LIMIT)
    send, aug, sup, pk, tl = pl.pallas_call(
        blocks_kernel,
        out_shape=(
            shape(DEV, TILE, 128), shape(16, 72, 128), shape(4, 72, 128),
            shape(6, 128, 128), shape(4, H, T),
        ),
        in_specs=[vmem] * 6,
        out_specs=[vmem] * 5,
        scratch_shapes=[
            pltpu.VMEM((PAIRS, H, 128), F32),
            pltpu.VMEM((PAIRS, H, 128), F32),
            pltpu.VMEM((8, 128), F32),
            pltpu.VMEM((528, 384), BF16),
            pltpu.VMEM((384, 384), BF16),
        ],
        compiler_params=params,
        name="blocks",
    )(x, g, c, w_input, w_hidden, bias2)
    received = lax.all_to_all(send, "tm", 0, 0)
    me = lax.axis_index("tm").astype(jnp.int32).reshape(1)
    states, adjoint, grads = pl.pallas_call(
        apply_kernel,
        out_shape=(shape(H, T), shape(H, T), shape(256, 128)),
        in_specs=[pl.BlockSpec(memory_space=pltpu.SMEM)] + [vmem] * 9,
        out_specs=[vmem] * 3,
        scratch_shapes=[
            pltpu.VMEM((384, 384), BF16),
            pltpu.VMEM((1152, 128), BF16),
            pltpu.VMEM((HALF * H + 16, 384), BF16),
            pltpu.VMEM((HALF, H, 128), F32),
            pltpu.VMEM((HALF, 128), F32),
            pltpu.VMEM((DEV, 128), F32),
            pltpu.VMEM((7, DEV, 128), F32),
            pltpu.VMEM((128, 128), F32),
            pltpu.VMEM((128, 128), F32),
        ],
        compiler_params=params,
        name="apply",
    )(me, received, aug, sup, pk, tl, x, g, w_hidden, bias2)
    axes = ("seq", "tm")
    count = lax.axis_size("seq") * lax.axis_size("tm")
    pieces = lax.all_to_all(grads.reshape(count, 2, 128), axes, 0, 0)
    scale = 1.0 / math.sqrt(lax.axis_size("seq") * lax.axis_size("tm") * T)
    mine = jnp.sum(pieces, axis=0) * scale
    whole = lax.all_to_all(jnp.broadcast_to(mine[None], (count, 2, 128)), axes, 0, 0)
    whole = whole.reshape(256, 128)
    grad_input = jnp.concatenate([whole[0:64], whole[128:192, :64]], axis=1)
    grad_hidden = jnp.concatenate([whole[64:128], whole[128:192, 64:]], axis=1)
    grad_bias = whole[192:194].reshape(256)
    return (
        jnp.swapaxes(states, 0, 1)[None], jnp.swapaxes(adjoint, 0, 1)[None],
        grad_input, grad_hidden, grad_bias,
    )


def solution(mesh):
    return jax.shard_map(
        per_device,
        mesh=mesh,
        in_specs=(P("seq", "tm", None), P("seq", "tm", None), P("seq", "tm", None), P(), P(), P()),
        out_specs=(P("seq", "tm", None), P("seq", "tm", None), P(), P(), P()),
        check_vma=False,
    )
```

```python
import math

import jax
import jax.numpy as jnp
from jax import lax
from jax.experimental import pallas as pl
from jax.experimental.pallas import tpu as pltpu
from jax.sharding import PartitionSpec as P

F32 = jnp.float32
BF16 = jnp.bfloat16
HIGHEST = lax.Precision.HIGHEST
H = 64
T = 256
RUN = 16
PAIRS = 8
DEV = 32
HALF = DEV // 2
TILE = 40
GROUP = 2
VMEM_LIMIT = 48 * 1024 * 1024


def dot(a, b, dims=((1,), (0,))):
    return lax.dot_general(a, b, (dims, ((), ())), precision=HIGHEST, preferred_element_type=F32)


def bdot(a, b):
    return jnp.dot(a, b, preferred_element_type=F32)


def iota(shape, axis):
    return lax.broadcasted_iota(jnp.int32, shape, axis)


def split(a):
    high = a.astype(BF16)
    return high, (a - high.astype(F32)).astype(BF16)


def sigmoid(a):
    return 1.0 / (1.0 + jnp.exp(-a))


def doubled(block):
    zero = jnp.zeros_like(block)
    return jnp.concatenate(
        [jnp.concatenate([block, zero], axis=1), jnp.concatenate([zero, block], axis=1)], axis=0
    )


def forward_weights(wh):
    wide = jnp.concatenate(
        [doubled(wh[:, 128:192]), doubled(wh[:, :64]), doubled(wh[:, 64:128])], axis=1
    )
    high, low = split(wide)
    return jnp.concatenate([high, high, low], axis=0)


def side_weights(wh):
    n, r, z = [split(doubled(wh[:, k:k + H])) for k in (128, 0, 64)]
    zero = jnp.zeros((128, 128), BF16)
    top = jnp.concatenate([n[0], r[0], z[0], n[1]], axis=1)
    bottom = jnp.concatenate([n[0], r[0], z[0], zero], axis=1)
    return jnp.concatenate([top, bottom], axis=0), jnp.concatenate([r[1], z[1]], axis=1)


def halves(value):
    return jnp.concatenate(split(value), axis=1)


def gates_of(first, second):
    return (
        first[:, :128] + first[:, 384:], first[:, 128:256] + second[:, :128],
        first[:, 256:384] + second[:, 128:],
    )


def backward_weights(wh):
    tall = jnp.concatenate(
        [doubled(wh[:, 128:192].T), doubled(wh[:, :64].T), doubled(wh[:, 64:128].T)], axis=0
    )
    high, low = split(tall)
    return jnp.concatenate([high, high, low], axis=0)


def three(a):
    high, low = split(a)
    return jnp.concatenate([high, low, high], axis=1)


def to_row(column, offset):
    hit = iota((H, 128), 1) == iota((H, 128), 0) + offset
    return jnp.sum(jnp.where(hit, column, 0.0), axis=0, keepdims=True)


def gate_terms(gi_r, gi_z, gi_n, gh_r, gh_z, gh_n, bias_h, prev):
    reset = sigmoid(gi_r + gh_r)
    update = sigmoid(gi_z + gh_z)
    keep = sigmoid(-(gi_z + gh_z))
    hsum = gh_n + bias_h
    cand = jnp.tanh(gi_n + reset * hsum)
    squash = keep * (1.0 - cand * cand)
    p = squash * reset
    q = squash * hsum * reset * (1.0 - reset)
    w = (prev - cand) * update * keep
    shift = keep * cand - p * gh_n - q * gh_r - w * gh_z
    return squash, p, q, w, update, shift


def packed(a):
    return jnp.concatenate([a[:, :128], a[:, 128:]], axis=0).T


def combine(earlier, later):
    row, lane = iota((72, 128), 0), iota((72, 128), 1)
    product = dot(earlier[:, :H], later[:H, :])
    return (
        product
        + jnp.where((lane == H) & (row < H), earlier, 0.0)
        + jnp.where((row == H) & (lane < H), later, 0.0)
    )


def fetch(pairs, sems):
    copies = [pltpu.make_async_copy(a, b, sems.at[k]) for k, (a, b) in enumerate(pairs)]
    for copy in copies:
        copy.start()
    return copies


def blocks_kernel(
    x_hbm, g_hbm, c_hbm, wi_hbm, wh_hbm, bias_hbm,
    send_ref, aug_ref, sup_ref, pk_ref, tl_ref,
    y_ref, z_ref, b_ref, lhs_ref, w1_ref, w2_ref,
    x_ref, g_ref, c_ref, wi_ref, wh_ref, bias_ref, sems,
):
    for copy in fetch(
        [(wh_hbm, wh_ref), (g_hbm, g_ref), (wi_hbm, wi_ref), (x_hbm, x_ref), (bias_hbm, bias_ref),
         (c_hbm, c_ref)], sems,
    ):
        copy.wait()
    wh = wh_ref[...]
    w1_ref[...], w2_ref[...] = side_weights(wh)
    guess = g_ref[...]
    prev = pltpu.roll(guess, 1, 1)
    gi = dot(wi_ref[...], x_ref[...], ((0,), (0,)))
    gh = dot(wh, prev, ((0,), (0,)))
    bias0 = jnp.broadcast_to(bias_ref[0:1, :], (128, 128)).T
    bias1 = jnp.broadcast_to(bias_ref[1:2, :], (128, 128)).T
    bias0 = jnp.concatenate([bias0, bias0], axis=1)
    bias1 = jnp.concatenate([bias1, bias1], axis=1)
    gi_r = gi[:64] + bias0[:64]
    gi_z = gi[64:128] + bias0[64:]
    gi_n = gi[128:] + bias1[:64]
    squash, p, q, w, u, shift = gate_terms(
        gi_r, gi_z, gi_n, gh[:64], gh[64:128], gh[128:], bias1[64:], prev
    )
    tl_ref[0], tl_ref[1], tl_ref[2], tl_ref[3] = squash, p, q, w
    first = iota((H, T), 1) == 0
    pk_ref[0] = packed(jnp.where(first, 0.0, p))
    pk_ref[1] = packed(jnp.where(first, 0.0, q))
    pk_ref[2] = packed(jnp.where(first, 0.0, w))
    pk_ref[3] = packed(jnp.where(first, 1.0, u))
    pk_ref[4] = packed(jnp.where(first, 0.0, shift))
    pk_ref[5] = packed(c_ref[...])

    lane64 = iota((H, 128), 1)
    low64 = lane64 < H
    eye2 = jnp.where((lane64 == iota((H, 128), 0)) | (lane64 == iota((H, 128), 0) + H), 1.0, 0.0)
    wn2 = jnp.concatenate([wh[:, 128:192], wh[:, 128:192]], axis=1)
    wr2 = jnp.concatenate([wh[:, :64], wh[:, :64]], axis=1)
    wz2 = jnp.concatenate([wh[:, 64:128], wh[:, 64:128]], axis=1)

    def rows(k, step):
        return pk_ref[k, pl.ds(step, PAIRS, stride=RUN), :]

    def put(c, value, cot):
        y_ref[c] = value
        lhs_ref[c * H:(c + 1) * H, :] = halves(value)
        return value * cot

    def put_b(value):
        b_ref[...] = value
        lhs_ref[512:528, :] = halves(jnp.concatenate([value, jnp.zeros_like(value)], axis=0))

    p0, q0, w0, u0, s0, c0 = [rows(k, 0) for k in range(6)]
    for c in range(PAIRS):
        value = (
            p0[c:c + 1] * wn2 + q0[c:c + 1] * wr2 + w0[c:c + 1] * wz2 + u0[c:c + 1] * eye2
        )
        z_ref[c] = put(c, value, c0[c:c + 1])
    put_b(s0)

    def step(l, carry):
        p1, q1, w1, u1, s1, c1 = [rows(k, l) for k in range(6)]
        for c in range(PAIRS):
            if c % GROUP == 0:
                lhs = lhs_ref[c * H:(c + GROUP) * H, :]
                first, second = bdot(lhs, w1_ref[...]), bdot(lhs[:, :128], w2_ref[...])
            part = slice((c % GROUP) * H, (c % GROUP + 1) * H)
            n, r, z = gates_of(first[part], second[part])
            value = (
                u1[c:c + 1] * y_ref[c] + p1[c:c + 1] * n + q1[c:c + 1] * r + w1[c:c + 1] * z
            )
            z_ref[c] += put(c, value, c1[c:c + 1])
        lhs = lhs_ref[512:528, :]
        first, second = bdot(lhs, w1_ref[...]), bdot(lhs[:, :128], w2_ref[...])
        n, r, z = gates_of(first[:8], second[:8])
        put_b(u1 * b_ref[...] + p1 * n + q1 * r + w1 * z + s1)
        return carry

    lax.fori_loop(1, RUN, step, 0, unroll=True)

    low8 = iota((8, 128), 1) < H
    top8 = iota((8, 128), 0) == 0
    bs = b_ref[...]
    for c in range(PAIRS):
        y = y_ref[c]
        z = z_ref[c]
        offs = jnp.broadcast_to(bs[c:c + 1], (8, 128))
        for part in range(2):
            if part:
                y, z, offs = pltpu.roll(y, H, 1), pltpu.roll(z, H, 1), pltpu.roll(offs, H, 1)
            col = jnp.sum(jnp.where(low64, z, 0.0), axis=1, keepdims=True)
            n = c + part * PAIRS
            aug_ref[n, 0:64, :] = jnp.where(low64, y, jnp.where(lane64 == H, col, 0.0))
            aug_ref[n, 64:72, :] = jnp.where(low8 & top8, offs, 0.0)
    sups = []
    for k in range(4):
        left = combine(aug_ref[4 * k], aug_ref[4 * k + 1])
        right = combine(aug_ref[4 * k + 2], aug_ref[4 * k + 3])
        sups.append(combine(left, right))
        sup_ref[k] = sups[-1]
    total = combine(combine(sups[0], sups[1]), combine(sups[2], sups[3]))

    low32 = iota((32, 128), 1) < H
    body = jnp.where(low32, total[:32], pltpu.roll(total[32:64], H, 1))
    col = jnp.sum(jnp.where(lane64 == H, total[:64], 0.0), axis=1, keepdims=True)
    row_bc = jnp.where(low8[:1], total[64:65], 0.0) + to_row(col, H)
    last = jnp.sum(jnp.where(lane64 == 127, guess[:, 128:], 0.0), axis=1, keepdims=True)

    def head(a):
        return jnp.sum(jnp.where(lane64 == 0, a[:, :128], 0.0), axis=1, keepdims=True)

    row_gr = to_row(last, 0) + to_row(head(gi_r), H)
    row_zn = to_row(head(gi_z), 0) + to_row(head(gi_n), H)
    row8 = iota((8, 128), 0)
    tail = jnp.where(row8 == 0, row_bc, jnp.where(row8 == 1, row_gr, jnp.where(row8 == 2, row_zn, 0.0)))
    for k in range(HALF):
        send_ref[k, 0:32, :] = body
        send_ref[k, 32:40, :] = tail


def apply_kernel(
    me_ref, own_ref, other_ref, aug_ref, sup_ref, pk_ref, tl_ref, x_hbm, g_hbm, wh_hbm, bias_hbm,
    state_ref, adj_ref, grad_ref,
    w_ref, wt_ref, lhs_ref, z_ref, d_ref, row_ref, bnd_ref, st_ref, lam_ref,
    x_ref, g_ref, wh_ref, bias_ref, sems,
):
    copies = fetch([(wh_hbm, wh_ref), (bias_hbm, bias_ref), (g_hbm, g_ref), (x_hbm, x_ref)], sems)
    me = me_ref[0]
    core = me % 2
    for k in range(3):
        row_ref[k, pl.ds(core, HALF, stride=2), :] = own_ref[:, 32 + k, :]
        row_ref[k, pl.ds(1 - core, HALF, stride=2), :] = other_ref[:, 32 + k, :]
    for copy in copies:
        copy.wait()
    wh = wh_ref[...]
    w_ref[...] = forward_weights(wh)
    wt_ref[...] = backward_weights(wh)
    bias_h = bias_ref[1:2, 64:]

    bc, gr, zn = row_ref[0], row_ref[1], row_ref[2]
    prev = jnp.where(iota((DEV, H), 0) == DEV - 1, 0.0, gr[:, :H])
    gr_next = pltpu.roll(gr, DEV - 1, 0)
    zn_next = pltpu.roll(zn, DEV - 1, 0)
    gh = dot(prev, wh)
    terms = gate_terms(
        gr_next[:, H:], zn_next[:, :H], zn_next[:, H:],
        gh[:, :64], gh[:, 64:128], gh[:, 128:], bias_h, prev,
    )
    for k in range(6):
        bnd_ref[k] = jnp.concatenate([terms[k], terms[k]], axis=1)
    bnd_ref[6] = jnp.concatenate([prev, prev], axis=1)

    def pair(a):
        return jnp.concatenate([a[:HALF], a[HALF:]], axis=1)

    p, q, w, u, shift = [pair(terms[k]) for k in (1, 2, 3, 4, 5)]
    lane64 = iota((H, 128), 1)
    row64 = iota((H, 128), 0)
    low32 = iota((32, 128), 1) < H
    for ref, side in ((own_ref, core), (other_ref, 1 - core)):
        for k in range(HALF // 2):
            a, b = ref[k, 0:32, :], ref[k + HALF // 2, 0:32, :]
            top = jnp.where(low32, a, pltpu.roll(b, H, 1))
            bottom = jnp.where(low32, pltpu.roll(a, H, 1), b)
            value = jnp.concatenate([top, bottom], axis=0)
            z_ref[2 * k + side] = value
            start = pl.multiple_of((2 * k + side) * H, H)
            lhs_ref[pl.ds(start, H), :] = three(value)
    offs = pair(bc[:, :H])
    lhs_ref[HALF * H:, :] = three(offs)
    prod = bdot(lhs_ref[...], w_ref[...])
    for k in range(HALF):
        part = prod[k * H:(k + 1) * H]
        z_ref[k] = (
            u[k:k + 1] * z_ref[k] + p[k:k + 1] * part[:, :128]
            + q[k:k + 1] * part[:, 128:256] + w[k:k + 1] * part[:, 256:]
        )
    part = prod[HALF * H:]
    d_ref[...] = u * offs + p * part[:, :128] + q * part[:, 128:256] + w * part[:, 256:] + shift

    lane1 = iota((1, 128), 1)
    eye_a = lane64 == row64
    eye_b = lane64 == row64 + H

    def fwd(eye, base):
        def lap(k, x):
            col = jnp.sum(jnp.where(eye, x, 0.0), axis=1, keepdims=True)
            return jnp.sum(col * z_ref[k - base], axis=0, keepdims=True) + d_ref[pl.ds(k - base, 1), :]
        return lap

    x = bnd_ref[5, DEV - 1:DEV, :]
    x = lax.fori_loop(0, jnp.minimum(me, HALF), fwd(eye_a, 0), x)
    x = lax.fori_loop(HALF, me, fwd(eye_b, HALF), pltpu.roll(x, H, 1))
    x = pltpu.roll(x, H, 1)

    def bwd(eye, base, turn, keep):
        def lap(i, lam):
            k = base - i
            col = jnp.sum(z_ref[k % HALF] * lam, axis=1, keepdims=True)
            extra = row_ref[0, pl.ds(k, 1), :]
            if turn:
                extra = pltpu.roll(extra, H, 1)
            return jnp.sum(jnp.where(eye, col, 0.0), axis=0, keepdims=True) + jnp.where(keep, extra, 0.0)
        return lap

    lam = jnp.where(lane1 >= H, row_ref[0, DEV - 1:DEV, :], 0.0)
    lam = lax.fori_loop(
        0, DEV - 1 - jnp.maximum(me + 1, HALF), bwd(eye_b, DEV - 2, False, lane1 >= H), lam
    )
    lam = lax.fori_loop(
        0, jnp.maximum(HALF - 1 - me, 0), bwd(eye_a, HALF - 1, True, lane1 < H), pltpu.roll(lam, H, 1)
    )
    row_terms = [bnd_ref[k, pl.ds(me, 1), :] for k in range(6)]
    lam8 = jnp.broadcast_to(lam, (8, 128))[:, :H]
    wide = jnp.concatenate([lam8 * row_terms[k][:, :H] for k in (1, 2, 3)], axis=1)
    tall = jnp.concatenate([wh[:, 128:192].T, wh[:, :64].T, wh[:, 64:128].T], axis=0)
    carry = (dot(wide, tall) + lam8 * row_terms[4][:, :H])[0:1]
    carry = jnp.where(me == DEV - 1, 0.0, carry)
    carry = jnp.concatenate([carry, jnp.zeros_like(carry)], axis=1)

    row72 = iota((72, 128), 0)
    eye72 = iota((72, 128), 1) == row72
    one = lane1 == H

    def ahead(maps, x):
        col = jnp.sum(jnp.where(eye72, x, 0.0), axis=1, keepdims=True)
        return jnp.where(one, 1.0, jnp.sum(col * maps, axis=0, keepdims=True))

    def back(maps, lam):
        col = jnp.sum(maps[:H] * lam, axis=1, keepdims=True)
        return jnp.where(one, 1.0, jnp.sum(jnp.where(eye_a, col, 0.0), axis=0, keepdims=True))

    starts = [jnp.where(one, 1.0, x)]
    for k in range(3):
        starts.append(ahead(sup_ref[k], starts[-1]))
    ends = [jnp.where(one, 1.0, carry)]
    for k in (3, 2, 1):
        ends.append(back(sup_ref[k], ends[-1]))
    ends = ends[::-1]
    state_rows, carry_rows = [None] * 16, [None] * 16
    for k in range(4):
        value, lam = starts[k], ends[k]
        for j in range(4):
            state_rows[4 * k + j] = value
            carry_rows[4 * k + 3 - j] = lam
            if j < 3:
                value = ahead(aug_ref[4 * k + j], value)
                lam = back(aug_ref[4 * k + 3 - j], lam)

    def gather(items):
        left = jnp.concatenate(items[:8], axis=0)
        right = jnp.concatenate(items[8:], axis=0)
        return jnp.where(iota((8, 128), 1) < H, left, pltpu.roll(right, H, 1))

    def rows(k, step):
        return pk_ref[k, pl.ds(step, PAIRS, stride=RUN), :]

    def pad(a):
        return jnp.concatenate([a, jnp.zeros_like(a)], axis=0)

    def lap(i, both):
        state, kappa = both
        j = RUN - 1 - i
        prod = bdot(three(pad(state)), w_ref[...])[:8]
        lam = rows(5, j) + kappa
        lam_ref[pl.ds(j, PAIRS, stride=RUN), :] = lam
        mixed = jnp.concatenate([lam * rows(0, j), lam * rows(1, j), lam * rows(2, j)], axis=1)
        kappa = bdot(three(pad(mixed)), wt_ref[...])[:8] + lam * rows(3, j)
        state = (
            rows(3, i) * state + rows(0, i) * prod[:, :128] + rows(1, i) * prod[:, 128:256]
            + rows(2, i) * prod[:, 256:] + rows(4, i)
        )
        st_ref[pl.ds(i, PAIRS, stride=RUN), :] = state
        return state, kappa

    lax.fori_loop(0, RUN, lap, (gather(state_rows), gather(carry_rows)))
    states = st_ref[...].T
    state_ref[:, :128] = states[:H]
    state_ref[:, 128:] = states[H:]
    lams = lam_ref[...].T
    lams = jnp.concatenate([lams[:H], lams[H:]], axis=1)
    adj_ref[...] = lams

    before = (me + DEV - 1) % DEV
    first = iota((H, T), 1) == 0

    def with_first(a, k):
        col = jnp.sum(jnp.where(eye_a, bnd_ref[k, pl.ds(before, 1), :], 0.0), axis=1, keepdims=True)
        return jnp.where(first, col, a)

    squash, p, q, w = [with_first(tl_ref[k], k) for k in range(4)]
    prev = with_first(pltpu.roll(g_ref[...], 1, 1), 6)
    left = jnp.concatenate([x_ref[...], prev, jnp.ones((8, T), F32)], axis=0)
    right = jnp.concatenate([lams * q, lams * w, lams * squash, lams * p], axis=0)
    sums = dot(left, right, ((1,), (1,)))
    grad_ref[0:64, :] = sums[:64, :128]
    grad_ref[64:128, :] = sums[64:128, :128]
    grad_ref[128:192, :] = jnp.where(lane64 < H, sums[:64, 128:], sums[64:128, 128:])
    row8 = iota((8, 128), 0)
    grad_ref[192:200, :] = jnp.where(
        row8 == 0, sums[128:136, :128], jnp.where(row8 == 1, sums[128:136, 128:], 0.0)
    )
    grad_ref[200:, :] = jnp.zeros((56, 128), F32)


def shape(*dims):
    return jax.ShapeDtypeStruct(dims, F32)


def per_device(inputs, guess, cotangent, w_input, w_hidden, bias):
    x = jnp.swapaxes(inputs[0], 0, 1)
    g = jnp.swapaxes(guess[0], 0, 1)
    c = jnp.swapaxes(cotangent[0], 0, 1)
    bias2 = bias.reshape(2, 128)
    x, g, c, w_input, w_hidden, bias2 = [
        pltpu.with_memory_space_constraint(a, pltpu.HBM)
        for a in (x, g, c, w_input, w_hidden, bias2)
    ]
    vmem = pl.BlockSpec(memory_space=pltpu.VMEM)
    hbm = pl.BlockSpec(memory_space=pltpu.HBM)
    wide = [pltpu.VMEM((H, T), F32)] * 3
    params = pltpu.CompilerParams(vmem_limit_bytes=VMEM_LIMIT)
    send, aug, sup, pk, tl = pl.pallas_call(
        blocks_kernel,
        out_shape=(
            shape(HALF, TILE, 128), shape(16, 72, 128), shape(4, 72, 128),
            shape(6, 128, 128), shape(4, H, T),
        ),
        in_specs=[hbm] * 6,
        out_specs=[vmem] * 5,
        scratch_shapes=[
            pltpu.VMEM((PAIRS, H, 128), F32),
            pltpu.VMEM((PAIRS, H, 128), F32),
            pltpu.VMEM((8, 128), F32),
            pltpu.VMEM((528, 256), BF16),
            pltpu.VMEM((256, 512), BF16),
            pltpu.VMEM((128, 256), BF16),
        ] + wide + [
            pltpu.VMEM((H, 192), F32),
            pltpu.VMEM((H, 192), F32),
            pltpu.VMEM((2, 128), F32),
            pltpu.SemaphoreType.DMA((6,)),
        ],
        compiler_params=params,
        name="blocks",
    )(x, g, c, w_input, w_hidden, bias2)
    groups = [[2 * k + core for k in range(HALF)] for core in range(2)]
    received = lax.all_to_all(send, "tm", 0, 0, axis_index_groups=groups)
    other = lax.ppermute(received, "tm", [(k, k ^ 1) for k in range(DEV)])
    me = lax.axis_index("tm").astype(jnp.int32).reshape(1)
    states, adjoint, grads = pl.pallas_call(
        apply_kernel,
        out_shape=(shape(H, T), shape(H, T), shape(256, 128)),
        in_specs=[pl.BlockSpec(memory_space=pltpu.SMEM)] + [vmem] * 6 + [hbm] * 4,
        out_specs=[vmem] * 3,
        scratch_shapes=[
            pltpu.VMEM((384, 384), BF16),
            pltpu.VMEM((1152, 128), BF16),
            pltpu.VMEM((HALF * H + 16, 384), BF16),
            pltpu.VMEM((HALF, H, 128), F32),
            pltpu.VMEM((HALF, 128), F32),
            pltpu.VMEM((3, DEV, 128), F32),
            pltpu.VMEM((7, DEV, 128), F32),
            pltpu.VMEM((128, 128), F32),
            pltpu.VMEM((128, 128), F32),
        ] + wide[:2] + [
            pltpu.VMEM((H, 192), F32),
            pltpu.VMEM((2, 128), F32),
            pltpu.SemaphoreType.DMA((4,)),
        ],
        compiler_params=params,
        name="apply",
    )(me, received, other, aug, sup, pk, tl, x, g, w_hidden, bias2)
    axes = ("seq", "tm")
    count = lax.axis_size("seq") * lax.axis_size("tm")
    pieces = lax.all_to_all(grads.reshape(count, 2, 128), axes, 0, 0)
    scale = 1.0 / math.sqrt(lax.axis_size("seq") * lax.axis_size("tm") * T)
    mine = jnp.sum(pieces, axis=0) * scale
    whole = lax.all_to_all(jnp.broadcast_to(mine[None], (count, 2, 128)), axes, 0, 0)
    whole = whole.reshape(256, 128)
    grad_input = jnp.concatenate([whole[0:64], whole[128:192, :64]], axis=1)
    grad_hidden = jnp.concatenate([whole[64:128], whole[128:192, 64:]], axis=1)
    grad_bias = whole[192:194].reshape(256)
    return (
        jnp.swapaxes(states, 0, 1)[None], jnp.swapaxes(adjoint, 0, 1)[None],
        grad_input, grad_hidden, grad_bias,
    )


def solution(mesh):
    return jax.shard_map(
        per_device,
        mesh=mesh,
        in_specs=(P("seq", "tm", None), P("seq", "tm", None), P("seq", "tm", None), P(), P(), P()),
        out_specs=(P("seq", "tm", None), P("seq", "tm", None), P(), P(), P()),
        check_vma=False,
    )
```

```python
import math

import jax
import jax.numpy as jnp
from jax import lax
from jax.experimental import pallas as pl
from jax.experimental.pallas import tpu as pltpu
from jax.sharding import PartitionSpec as P

F32 = jnp.float32
BF16 = jnp.bfloat16
HIGHEST = lax.Precision.HIGHEST
H = 64
T = 256
RUN = 16
PAIRS = 8
DEV = 32
HALF = DEV // 2
TILE = 40
GROUP = 2
VMEM_LIMIT = 48 * 1024 * 1024


def dot(a, b, dims=((1,), (0,))):
    return lax.dot_general(a, b, (dims, ((), ())), precision=HIGHEST, preferred_element_type=F32)


def bdot(a, b):
    return jnp.dot(a, b, preferred_element_type=F32)


def iota(shape, axis):
    return lax.broadcasted_iota(jnp.int32, shape, axis)


def split(a):
    high = a.astype(BF16)
    return high, (a - high.astype(F32)).astype(BF16)


def sigmoid(a):
    return 1.0 / (1.0 + jnp.exp(-a))


def doubled(block):
    zero = jnp.zeros_like(block)
    return jnp.concatenate(
        [jnp.concatenate([block, zero], axis=1), jnp.concatenate([zero, block], axis=1)], axis=0
    )


def side_weights(wh):
    n, r, z = [split(doubled(wh[:, k:k + H])) for k in (128, 0, 64)]
    zero = jnp.zeros((128, 128), BF16)
    top = jnp.concatenate([n[0], r[0], z[0], n[1]], axis=1)
    bottom = jnp.concatenate([n[0], r[0], z[0], zero], axis=1)
    return jnp.concatenate([top, bottom], axis=0), jnp.concatenate([r[1], z[1]], axis=1)


def halves(value):
    return jnp.concatenate(split(value), axis=1)


def gates_of(first, second):
    return (
        first[:, :128] + first[:, 384:], first[:, 128:256] + second[:, :128],
        first[:, 256:384] + second[:, 128:],
    )


def backward_weights(wh):
    tall = jnp.concatenate([doubled(wh[:, k:k + H].T) for k in (128, 0, 64)], axis=0)
    return jnp.concatenate(split(tall), axis=1)


def stacked(value):
    high = value.astype(BF16).astype(F32)
    return jnp.concatenate([high, value - high], axis=0).astype(BF16)


def narrow_gates(value, w1_ref, w2_ref):
    rows = value.shape[0]
    weights = jnp.concatenate([w1_ref[:128, :], w2_ref[...]], axis=1)
    out = bdot(stacked(value), weights)
    high, low = out[:rows], out[rows:]
    n = high[:, :128] + high[:, 384:512] + low[:, :128]
    r = high[:, 128:256] + high[:, 512:640] + low[:, 128:256]
    z = high[:, 256:384] + high[:, 640:] + low[:, 256:384]
    return n, r, z


def pulled(mixed, wt_ref):
    rows = mixed.shape[0]
    out = bdot(stacked(mixed), wt_ref[...])
    return out[:rows, :128] + out[rows:, :128] + out[:rows, 128:]


def to_row(column, offset):
    hit = iota((H, 128), 1) == iota((H, 128), 0) + offset
    return jnp.sum(jnp.where(hit, column, 0.0), axis=0, keepdims=True)


def gate_terms(gi_r, gi_z, gi_n, gh_r, gh_z, gh_n, bias_h, prev):
    reset = sigmoid(gi_r + gh_r)
    update = sigmoid(gi_z + gh_z)
    keep = sigmoid(-(gi_z + gh_z))
    hsum = gh_n + bias_h
    cand = jnp.tanh(gi_n + reset * hsum)
    squash = keep * (1.0 - cand * cand)
    p = squash * reset
    q = squash * hsum * reset * (1.0 - reset)
    w = (prev - cand) * update * keep
    shift = keep * cand - p * gh_n - q * gh_r - w * gh_z
    return squash, p, q, w, update, shift


def packed(a):
    return jnp.concatenate([a[:, :128], a[:, 128:]], axis=0).T


def combine(earlier, later):
    row, lane = iota((72, 128), 0), iota((72, 128), 1)
    product = dot(earlier[:, :H], later[:H, :])
    return (
        product
        + jnp.where((lane == H) & (row < H), earlier, 0.0)
        + jnp.where((row == H) & (lane < H), later, 0.0)
    )


def fetch(pairs, sems):
    copies = [pltpu.make_async_copy(a, b, sems.at[k]) for k, (a, b) in enumerate(pairs)]
    for copy in copies:
        copy.start()
    return copies


def blocks_kernel(
    x_hbm, g_hbm, c_hbm, wi_hbm, wh_hbm, bias_hbm,
    send_ref, aug_ref, sup_ref, pk_ref, tl_ref, w1_ref, w2_ref, wt_ref, hb_ref,
    y_ref, z_ref, b_ref, lhs_ref,
    x_ref, g_ref, c_ref, wi_ref, wh_ref, bias_ref, sems,
):
    for copy in fetch(
        [(wh_hbm, wh_ref), (g_hbm, g_ref), (wi_hbm, wi_ref), (x_hbm, x_ref), (bias_hbm, bias_ref),
         (c_hbm, c_ref)], sems,
    ):
        copy.wait()
    wh = wh_ref[...]
    w1_ref[...], w2_ref[...] = side_weights(wh)
    wt_ref[...] = backward_weights(wh)
    hb = jnp.broadcast_to(bias_ref[1:2, :], (8, 128))
    hb_ref[...] = jnp.where(iota((8, 128), 1) < H, pltpu.roll(hb, H, 1), hb)
    guess = g_ref[...]
    prev = pltpu.roll(guess, 1, 1)
    gi = dot(wi_ref[...], x_ref[...], ((0,), (0,)))
    gh = dot(wh, prev, ((0,), (0,)))
    bias0 = jnp.broadcast_to(bias_ref[0:1, :], (128, 128)).T
    bias1 = jnp.broadcast_to(bias_ref[1:2, :], (128, 128)).T
    bias0 = jnp.concatenate([bias0, bias0], axis=1)
    bias1 = jnp.concatenate([bias1, bias1], axis=1)
    gi_r = gi[:64] + bias0[:64]
    gi_z = gi[64:128] + bias0[64:]
    gi_n = gi[128:] + bias1[:64]
    squash, p, q, w, u, shift = gate_terms(
        gi_r, gi_z, gi_n, gh[:64], gh[64:128], gh[128:], bias1[64:], prev
    )
    tl_ref[0], tl_ref[1], tl_ref[2], tl_ref[3] = squash, p, q, w
    first = iota((H, T), 1) == 0
    pk_ref[0] = packed(jnp.where(first, 0.0, p))
    pk_ref[1] = packed(jnp.where(first, 0.0, q))
    pk_ref[2] = packed(jnp.where(first, 0.0, w))
    pk_ref[3] = packed(jnp.where(first, 1.0, u))
    pk_ref[4] = packed(jnp.where(first, 0.0, shift))
    pk_ref[5] = packed(c_ref[...])

    lane64 = iota((H, 128), 1)
    low64 = lane64 < H
    eye2 = jnp.where((lane64 == iota((H, 128), 0)) | (lane64 == iota((H, 128), 0) + H), 1.0, 0.0)
    wn2 = jnp.concatenate([wh[:, 128:192], wh[:, 128:192]], axis=1)
    wr2 = jnp.concatenate([wh[:, :64], wh[:, :64]], axis=1)
    wz2 = jnp.concatenate([wh[:, 64:128], wh[:, 64:128]], axis=1)

    def rows(k, step):
        return pk_ref[k, pl.ds(step, PAIRS, stride=RUN), :]

    def put(c, value, cot):
        y_ref[c] = value
        lhs_ref[c * H:(c + 1) * H, :] = halves(value)
        return value * cot

    def put_b(value):
        b_ref[...] = value
        lhs_ref[512:528, :] = halves(jnp.concatenate([value, jnp.zeros_like(value)], axis=0))

    p0, q0, w0, u0, s0, c0 = [rows(k, 0) for k in range(6)]
    for c in range(PAIRS):
        value = (
            p0[c:c + 1] * wn2 + q0[c:c + 1] * wr2 + w0[c:c + 1] * wz2 + u0[c:c + 1] * eye2
        )
        z_ref[c] = put(c, value, c0[c:c + 1])
    put_b(s0)

    def step(l, carry):
        p1, q1, w1, u1, s1, c1 = [rows(k, l) for k in range(6)]
        for c in range(PAIRS):
            if c % GROUP == 0:
                lhs = lhs_ref[c * H:(c + GROUP) * H, :]
                first, second = bdot(lhs, w1_ref[...]), bdot(lhs[:, :128], w2_ref[...])
            part = slice((c % GROUP) * H, (c % GROUP + 1) * H)
            n, r, z = gates_of(first[part], second[part])
            value = (
                u1[c:c + 1] * y_ref[c] + p1[c:c + 1] * n + q1[c:c + 1] * r + w1[c:c + 1] * z
            )
            z_ref[c] += put(c, value, c1[c:c + 1])
        lhs = lhs_ref[512:528, :]
        first, second = bdot(lhs, w1_ref[...]), bdot(lhs[:, :128], w2_ref[...])
        n, r, z = gates_of(first[:8], second[:8])
        put_b(u1 * b_ref[...] + p1 * n + q1 * r + w1 * z + s1)
        return carry

    lax.fori_loop(1, RUN, step, 0, unroll=True)

    low8 = iota((8, 128), 1) < H
    top8 = iota((8, 128), 0) == 0
    bs = b_ref[...]
    for c in range(PAIRS):
        y = y_ref[c]
        z = z_ref[c]
        offs = jnp.broadcast_to(bs[c:c + 1], (8, 128))
        for part in range(2):
            if part:
                y, z, offs = pltpu.roll(y, H, 1), pltpu.roll(z, H, 1), pltpu.roll(offs, H, 1)
            col = jnp.sum(jnp.where(low64, z, 0.0), axis=1, keepdims=True)
            n = c + part * PAIRS
            aug_ref[n, 0:64, :] = jnp.where(low64, y, jnp.where(lane64 == H, col, 0.0))
            aug_ref[n, 64:72, :] = jnp.where(low8 & top8, offs, 0.0)
    sups = []
    for k in range(4):
        left = combine(aug_ref[4 * k], aug_ref[4 * k + 1])
        right = combine(aug_ref[4 * k + 2], aug_ref[4 * k + 3])
        sups.append(combine(left, right))
        sup_ref[k] = sups[-1]
    total = combine(combine(sups[0], sups[1]), combine(sups[2], sups[3]))

    low32 = iota((32, 128), 1) < H
    body = jnp.where(low32, total[:32], pltpu.roll(total[32:64], H, 1))
    col = jnp.sum(jnp.where(lane64 == H, total[:64], 0.0), axis=1, keepdims=True)
    row_bc = jnp.where(low8[:1], total[64:65], 0.0) + to_row(col, H)
    last = jnp.sum(jnp.where(lane64 == 127, guess[:, 128:], 0.0), axis=1, keepdims=True)

    def head(a):
        return jnp.sum(jnp.where(lane64 == 0, a[:, :128], 0.0), axis=1, keepdims=True)

    row_gr = to_row(last, 0) + to_row(head(gi_r), H)
    row_zn = to_row(head(gi_z), 0) + to_row(head(gi_n), H)
    row8 = iota((8, 128), 0)
    tail = jnp.where(row8 == 0, row_bc, jnp.where(row8 == 1, row_gr, jnp.where(row8 == 2, row_zn, 0.0)))
    for k in range(HALF):
        send_ref[k, 0:32, :] = body
        send_ref[k, 32:40, :] = tail


def apply_kernel(
    me_ref, own_ref, other_ref, aug_ref, sup_ref, pk_ref, tl_ref, w1_ref, w2_ref, wt_ref, hb_ref,
    x_hbm, g_hbm,
    state_ref, adj_ref, grad_ref,
    lhs_ref, z_ref, zt_ref, row_ref, bnd_ref, st_ref, lam_ref, x_ref, g_ref, sems,
):
    copies = fetch([(g_hbm, g_ref), (x_hbm, x_ref)], sems)
    me = me_ref[0]
    core = me % 2
    for k in range(3):
        row_ref[k, pl.ds(core, HALF, stride=2), :] = own_ref[:, 32 + k, :]
        row_ref[k, pl.ds(1 - core, HALF, stride=2), :] = other_ref[:, 32 + k, :]
    bc, gr, zn = row_ref[0], row_ref[1], row_ref[2]
    low16 = iota((HALF, 128), 1) < H

    def pair_low(a):
        return jnp.where(low16, a[:HALF], pltpu.roll(a[HALF:], H, 1))

    def pair_high(a):
        return jnp.where(low16, pltpu.roll(a[:HALF], H, 1), a[HALF:])

    gr_next = pltpu.roll(gr, DEV - 1, 0)
    zn_next = pltpu.roll(zn, DEV - 1, 0)
    prev = jnp.where((iota((HALF, 128), 0) == HALF - 1) & ~low16, 0.0, pair_low(gr))
    n, r, z = narrow_gates(prev, w1_ref, w2_ref)
    terms = gate_terms(
        pair_high(gr_next), pair_low(zn_next), pair_high(zn_next), r, z, n, hb_ref[0:1, :], prev
    )
    for k in range(6):
        bnd_ref[k] = terms[k]
    bnd_ref[6] = prev
    squash, p, q, w, u, shift = terms

    lane64 = iota((H, 128), 1)
    row64 = iota((H, 128), 0)
    low32 = iota((32, 128), 1) < H
    for ref, side in ((own_ref, core), (other_ref, 1 - core)):
        for k in range(HALF // 2):
            a, b = ref[k, 0:32, :], ref[k + HALF // 2, 0:32, :]
            top = jnp.where(low32, a, pltpu.roll(b, H, 1))
            bottom = jnp.where(low32, pltpu.roll(a, H, 1), b)
            value = jnp.concatenate([top, bottom], axis=0)
            z_ref[2 * k + side] = value
            start = pl.multiple_of((2 * k + side) * H, H)
            lhs_ref[pl.ds(start, H), :] = halves(value)
    offs = pair_low(bc)
    lhs_ref[HALF * H:, :] = halves(offs)
    for k in range(HALF):
        if k % GROUP == 0:
            lhs = lhs_ref[k * H:(k + GROUP) * H, :]
            first, second = bdot(lhs, w1_ref[...]), bdot(lhs[:, :128], w2_ref[...])
        part = slice((k % GROUP) * H, (k % GROUP + 1) * H)
        n, r, z = gates_of(first[part], second[part])
        value = u[k:k + 1] * z_ref[k] + p[k:k + 1] * n + q[k:k + 1] * r + w[k:k + 1] * z
        z_ref[k] = value
        if k % 2:
            zt_ref[k // 2] = jnp.concatenate([value, pltpu.roll(value, H, 1)], axis=0).T[:H]
    lhs = lhs_ref[HALF * H:, :]
    n, r, z = gates_of(bdot(lhs, w1_ref[...]), bdot(lhs[:, :128], w2_ref[...]))
    fwd_rows = u * offs + p * n + q * r + w * z + shift
    bwd_rows = pair_high(bc)
    empty = jnp.zeros((128 - HALF, 128), F32)
    fwd_cols = jnp.concatenate([fwd_rows, empty], axis=0).T
    bwd_cols = jnp.concatenate([bwd_rows, empty], axis=0).T

    lane1 = iota((1, 128), 1)
    low1 = lane1 < H
    eye_a = lane64 == row64
    eye_b = lane64 == row64 + H
    shift_last = shift[HALF - 1:HALF, :]
    x_col = jnp.sum(jnp.where(eye_b, shift_last, 0.0), axis=1, keepdims=True)
    lam_row = jnp.where(low1, 0.0, bwd_rows[HALF - 1:HALF, :])
    zero_col, zero_row = jnp.zeros((H, 1), F32), jnp.zeros((1, 128), F32)
    x_keep = jnp.where(me == 0, x_col, zero_col)
    lam_keep = zero_col
    x_rows, lam_rows = zero_row, jnp.where(me + 1 == DEV - 1, lam_row, zero_row)

    def half(k, row):
        return jnp.where(low1, row, 0.0) if k < HALF else jnp.where(low1, 0.0, row)

    def side_cols(cols, k):
        return jnp.where(lane64 == k % HALF, cols[:H] if k < HALF else cols[H:], 0.0)

    for i in range(DEV - 1):
        k, m = i, i % HALF
        if k % 2 == 0:
            x_row = half(k, jnp.sum(x_col * z_ref[m], axis=0, keepdims=True) + fwd_rows[m:m + 1])
            x_rows = jnp.where(me == k + 1, x_row, x_rows)
        else:
            x_col = jnp.sum(zt_ref[m // 2] * x_row + side_cols(fwd_cols, k), axis=1, keepdims=True)
            x_keep = jnp.where(me == k + 1, x_col, x_keep)
        k = DEV - 2 - i
        m = k % HALF
        if k % 2 == 0:
            lam_col = jnp.sum(z_ref[m] * lam_row + side_cols(bwd_cols, k), axis=1, keepdims=True)
            lam_keep = jnp.where(me + 1 == k, lam_col, lam_keep)
        else:
            lam_row = half(
                k, jnp.sum(lam_col * zt_ref[m // 2], axis=0, keepdims=True) + bwd_rows[m:m + 1]
            )
            lam_rows = jnp.where(me + 1 == k, lam_row, lam_rows)

    def settled(rows, column):
        row = jnp.where(low1, rows, 0.0) + jnp.where(low1, pltpu.roll(rows, H, 1), 0.0)
        return row + jnp.sum(jnp.where(eye_a, column, 0.0), axis=0, keepdims=True)

    x = settled(x_rows, x_keep)
    lam = settled(lam_rows, lam_keep)

    def boundary(k, index):
        row = bnd_ref[k, pl.ds(index % HALF, 1), :]
        return jnp.where(low1, jnp.where(index >= HALF, pltpu.roll(row, H, 1), row), 0.0)

    lam8 = jnp.broadcast_to(lam, (8, 128))
    mixed = jnp.concatenate([lam8 * boundary(k, me) for k in (1, 2, 3)], axis=1)
    carry = (pulled(mixed, wt_ref) + lam8 * boundary(4, me))[0:1]

    row72 = iota((72, 128), 0)
    eye72 = iota((72, 128), 1) == row72
    one = lane1 == H

    def ahead(maps, x):
        col = jnp.sum(jnp.where(eye72, x, 0.0), axis=1, keepdims=True)
        return jnp.where(one, 1.0, jnp.sum(col * maps, axis=0, keepdims=True))

    def back(maps, lam):
        col = jnp.sum(maps[:H] * lam, axis=1, keepdims=True)
        return jnp.where(one, 1.0, jnp.sum(jnp.where(eye_a, col, 0.0), axis=0, keepdims=True))

    starts = [jnp.where(one, 1.0, x)]
    for k in range(3):
        starts.append(ahead(sup_ref[k], starts[-1]))
    ends = [jnp.where(one, 1.0, carry)]
    for k in (3, 2, 1):
        ends.append(back(sup_ref[k], ends[-1]))
    ends = ends[::-1]
    state_rows, carry_rows = [None] * 16, [None] * 16
    for k in range(4):
        value, lam = starts[k], ends[k]
        for j in range(4):
            state_rows[4 * k + j] = value
            carry_rows[4 * k + 3 - j] = lam
            if j < 3:
                value = ahead(aug_ref[4 * k + j], value)
                lam = back(aug_ref[4 * k + 3 - j], lam)

    def gather(items):
        left = jnp.concatenate(items[:8], axis=0)
        right = jnp.concatenate(items[8:], axis=0)
        return jnp.where(iota((8, 128), 1) < H, left, pltpu.roll(right, H, 1))

    def rows(k, step):
        return pk_ref[k, pl.ds(step, PAIRS, stride=RUN), :]

    state, kappa = gather(state_rows), gather(carry_rows)
    for i in range(RUN):
        j = RUN - 1 - i
        n, r, z = narrow_gates(state, w1_ref, w2_ref)
        lam = rows(5, j) + kappa
        lam_ref[pl.ds(j, PAIRS, stride=RUN), :] = lam
        mixed = jnp.concatenate([lam * rows(0, j), lam * rows(1, j), lam * rows(2, j)], axis=1)
        kappa = pulled(mixed, wt_ref) + lam * rows(3, j)
        state = rows(3, i) * state + rows(0, i) * n + rows(1, i) * r + rows(2, i) * z + rows(4, i)
        st_ref[pl.ds(i, PAIRS, stride=RUN), :] = state

    states = st_ref[...].T
    state_ref[:, :128] = states[:H]
    state_ref[:, 128:] = states[H:]
    lams = lam_ref[...].T
    lams = jnp.concatenate([lams[:H], lams[H:]], axis=1)
    adj_ref[...] = lams

    before = (me + DEV - 1) % DEV
    first = iota((H, T), 1) == 0

    def with_first(a, k):
        col = jnp.sum(jnp.where(eye_a, boundary(k, before), 0.0), axis=1, keepdims=True)
        return jnp.where(first, col, a)

    for copy in copies:
        copy.wait()
    squash, p, q, w = [with_first(tl_ref[k], k) for k in range(4)]
    prev = with_first(pltpu.roll(g_ref[...], 1, 1), 6)
    left = jnp.concatenate([x_ref[...], prev, jnp.ones((8, T), F32)], axis=0)
    right = jnp.concatenate([lams * q, lams * w, lams * squash, lams * p], axis=0)
    sums = dot(left, right, ((1,), (1,)))
    grad_ref[0:64, :] = sums[:64, :128]
    grad_ref[64:128, :] = sums[64:128, :128]
    grad_ref[128:192, :] = jnp.where(lane64 < H, sums[:64, 128:], sums[64:128, 128:])
    row8 = iota((8, 128), 0)
    grad_ref[192:200, :] = jnp.where(
        row8 == 0, sums[128:136, :128], jnp.where(row8 == 1, sums[128:136, 128:], 0.0)
    )
    grad_ref[200:, :] = jnp.zeros((56, 128), F32)


def shape(*dims):
    return jax.ShapeDtypeStruct(dims, F32)


def per_device(inputs, guess, cotangent, w_input, w_hidden, bias):
    x = jnp.swapaxes(inputs[0], 0, 1)
    g = jnp.swapaxes(guess[0], 0, 1)
    c = jnp.swapaxes(cotangent[0], 0, 1)
    bias2 = bias.reshape(2, 128)
    x, g, c, w_input, w_hidden, bias2 = [
        pltpu.with_memory_space_constraint(a, pltpu.HBM)
        for a in (x, g, c, w_input, w_hidden, bias2)
    ]
    vmem = pl.BlockSpec(memory_space=pltpu.VMEM)
    hbm = pl.BlockSpec(memory_space=pltpu.HBM)
    wide = [pltpu.VMEM((H, T), F32)] * 3
    params = pltpu.CompilerParams(vmem_limit_bytes=VMEM_LIMIT)
    send, *kept = pl.pallas_call(
        blocks_kernel,
        out_shape=(
            shape(HALF, TILE, 128), shape(16, 72, 128), shape(4, 72, 128),
            shape(6, 128, 128), shape(4, H, T),
            jax.ShapeDtypeStruct((256, 512), BF16), jax.ShapeDtypeStruct((128, 256), BF16),
            jax.ShapeDtypeStruct((384, 256), BF16), shape(8, 128),
        ),
        in_specs=[hbm] * 6,
        out_specs=[vmem] * 9,
        scratch_shapes=[
            pltpu.VMEM((PAIRS, H, 128), F32),
            pltpu.VMEM((PAIRS, H, 128), F32),
            pltpu.VMEM((8, 128), F32),
            pltpu.VMEM((528, 256), BF16),
        ] + wide + [
            pltpu.VMEM((H, 192), F32),
            pltpu.VMEM((H, 192), F32),
            pltpu.VMEM((2, 128), F32),
            pltpu.SemaphoreType.DMA((6,)),
        ],
        compiler_params=params,
        name="blocks",
    )(x, g, c, w_input, w_hidden, bias2)
    groups = [[2 * k + core for k in range(HALF)] for core in range(2)]
    received = lax.all_to_all(send, "tm", 0, 0, axis_index_groups=groups)
    other = lax.ppermute(received, "tm", [(k, k ^ 1) for k in range(DEV)])
    me = lax.axis_index("tm").astype(jnp.int32).reshape(1)
    states, adjoint, grads = pl.pallas_call(
        apply_kernel,
        out_shape=(shape(H, T), shape(H, T), shape(256, 128)),
        in_specs=[pl.BlockSpec(memory_space=pltpu.SMEM)] + [vmem] * 10 + [hbm] * 2,
        out_specs=[vmem] * 3,
        scratch_shapes=[
            pltpu.VMEM((HALF * H + 16, 256), BF16),
            pltpu.VMEM((HALF, H, 128), F32),
            pltpu.VMEM((HALF // 2, H, 128), F32),
            pltpu.VMEM((3, DEV, 128), F32),
            pltpu.VMEM((7, HALF, 128), F32),
            pltpu.VMEM((128, 128), F32),
            pltpu.VMEM((128, 128), F32),
        ] + wide[:2] + [pltpu.SemaphoreType.DMA((2,))],
        compiler_params=params,
        name="apply",
    )(me, received, other, *kept, x, g)
    axes = ("seq", "tm")
    count = lax.axis_size("seq") * lax.axis_size("tm")
    pieces = lax.all_to_all(grads.reshape(count, 2, 128), axes, 0, 0)
    scale = 1.0 / math.sqrt(lax.axis_size("seq") * lax.axis_size("tm") * T)
    mine = jnp.sum(pieces, axis=0) * scale
    whole = lax.all_to_all(jnp.broadcast_to(mine[None], (count, 2, 128)), axes, 0, 0)
    whole = whole.reshape(256, 128)
    grad_input = jnp.concatenate([whole[0:64], whole[128:192, :64]], axis=1)
    grad_hidden = jnp.concatenate([whole[64:128], whole[128:192, 64:]], axis=1)
    grad_bias = whole[192:194].reshape(256)
    return (
        jnp.swapaxes(states, 0, 1)[None], jnp.swapaxes(adjoint, 0, 1)[None],
        grad_input, grad_hidden, grad_bias,
    )


def solution(mesh):
    return jax.shard_map(
        per_device,
        mesh=mesh,
        in_specs=(P("seq", "tm", None), P("seq", "tm", None), P("seq", "tm", None), P(), P(), P()),
        out_specs=(P("seq", "tm", None), P("seq", "tm", None), P(), P(), P()),
        check_vma=False,
    )
```

```python
import functools
import math

import jax
import jax.numpy as jnp
from jax import lax
from jax.experimental import pallas as pl
from jax.experimental.pallas import tpu as pltpu
from jax.sharding import PartitionSpec as P

F32 = jnp.float32
BF16 = jnp.bfloat16
HIGHEST = lax.Precision.HIGHEST
H = 64
T = 256
RUN = 16
PAIRS = 8
DEV = 32
HALF = DEV // 2
TILE = 40
GROUP = 2
PART = 104
VMEM_LIMIT = 48 * 1024 * 1024


def dot(a, b, dims=((1,), (0,))):
    return lax.dot_general(a, b, (dims, ((), ())), precision=HIGHEST, preferred_element_type=F32)


def bdot(a, b):
    return jnp.dot(a, b, preferred_element_type=F32)


def iota(shape, axis):
    return lax.broadcasted_iota(jnp.int32, shape, axis)


def split(a):
    high = a.astype(BF16)
    return high, (a - high.astype(F32)).astype(BF16)


def sigmoid(a):
    return 1.0 / (1.0 + jnp.exp(-a))


def doubled(block):
    zero = jnp.zeros_like(block)
    return jnp.concatenate(
        [jnp.concatenate([block, zero], axis=1), jnp.concatenate([zero, block], axis=1)], axis=0
    )


def side_weights(wh):
    n, r, z = [split(doubled(wh[:, k:k + H])) for k in (128, 0, 64)]
    zero = jnp.zeros((128, 128), BF16)
    top = jnp.concatenate([n[0], r[0], z[0], n[1]], axis=1)
    bottom = jnp.concatenate([n[0], r[0], z[0], zero], axis=1)
    return jnp.concatenate([top, bottom], axis=0), jnp.concatenate([r[1], z[1]], axis=1)


def halves(value):
    return jnp.concatenate(split(value), axis=1)


def gates_of(first, second):
    return (
        first[:, :128] + first[:, 384:], first[:, 128:256] + second[:, :128],
        first[:, 256:384] + second[:, 128:],
    )


def backward_weights(wh):
    tall = jnp.concatenate([doubled(wh[:, k:k + H].T) for k in (128, 0, 64)], axis=0)
    return jnp.concatenate(split(tall), axis=1)


def stacked(value):
    high = value.astype(BF16).astype(F32)
    return jnp.concatenate([high, value - high], axis=0).astype(BF16)


def narrow_gates(value, w1_ref, w2_ref):
    rows = value.shape[0]
    weights = jnp.concatenate([w1_ref[:128, :], w2_ref[...]], axis=1)
    out = bdot(stacked(value), weights)
    high, low = out[:rows], out[rows:]
    n = high[:, :128] + high[:, 384:512] + low[:, :128]
    r = high[:, 128:256] + high[:, 512:640] + low[:, 128:256]
    z = high[:, 256:384] + high[:, 640:] + low[:, 256:384]
    return n, r, z


def pulled(mixed, wt_ref):
    rows = mixed.shape[0]
    out = bdot(stacked(mixed), wt_ref[...])
    return out[:rows, :128] + out[rows:, :128] + out[:rows, 128:]


def to_row(column, offset):
    hit = iota((H, 128), 1) == iota((H, 128), 0) + offset
    return jnp.sum(jnp.where(hit, column, 0.0), axis=0, keepdims=True)


def gate_terms(gi_r, gi_z, gi_n, gh_r, gh_z, gh_n, bias_h, prev):
    reset = sigmoid(gi_r + gh_r)
    update = sigmoid(gi_z + gh_z)
    keep = sigmoid(-(gi_z + gh_z))
    hsum = gh_n + bias_h
    cand = jnp.tanh(gi_n + reset * hsum)
    squash = keep * (1.0 - cand * cand)
    p = squash * reset
    q = squash * hsum * reset * (1.0 - reset)
    w = (prev - cand) * update * keep
    shift = keep * cand - p * gh_n - q * gh_r - w * gh_z
    return squash, p, q, w, update, shift


def packed(a):
    return jnp.concatenate([a[:, :128], a[:, 128:]], axis=0).T


def combine(earlier, later):
    row, lane = iota((72, 128), 0), iota((72, 128), 1)
    product = dot(earlier[:, :H], later[:H, :])
    return (
        product
        + jnp.where((lane == H) & (row < H), earlier, 0.0)
        + jnp.where((row == H) & (lane < H), later, 0.0)
    )


def fetch(pairs, sems):
    copies = [pltpu.make_async_copy(a, b, sems.at[k]) for k, (a, b) in enumerate(pairs)]
    for copy in copies:
        copy.start()
    return copies


def blocks_kernel(
    x_hbm, g_hbm, c_hbm, wi_hbm, wh_hbm, bias_hbm,
    send_ref, aug_ref, sup_ref, pk_ref, tl_ref, w1_ref, w2_ref, wt_ref, hb_ref,
    y_ref, z_ref, b_ref, lhs_ref,
    x_ref, g_ref, c_ref, wi_ref, wh_ref, bias_ref, sems,
):
    for copy in fetch(
        [(wh_hbm, wh_ref), (g_hbm, g_ref), (wi_hbm, wi_ref), (x_hbm, x_ref), (bias_hbm, bias_ref),
         (c_hbm, c_ref)], sems,
    ):
        copy.wait()
    wh = wh_ref[...]
    w1_ref[...], w2_ref[...] = side_weights(wh)
    wt_ref[...] = backward_weights(wh)
    hb = jnp.broadcast_to(bias_ref[1:2, :], (8, 128))
    hb_ref[...] = jnp.where(iota((8, 128), 1) < H, pltpu.roll(hb, H, 1), hb)
    guess = g_ref[...]
    prev = pltpu.roll(guess, 1, 1)
    gi = dot(wi_ref[...], x_ref[...], ((0,), (0,)))
    gh = dot(wh, prev, ((0,), (0,)))
    bias0 = jnp.broadcast_to(bias_ref[0:1, :], (128, 128)).T
    bias1 = jnp.broadcast_to(bias_ref[1:2, :], (128, 128)).T
    bias0 = jnp.concatenate([bias0, bias0], axis=1)
    bias1 = jnp.concatenate([bias1, bias1], axis=1)
    gi_r = gi[:64] + bias0[:64]
    gi_z = gi[64:128] + bias0[64:]
    gi_n = gi[128:] + bias1[:64]
    squash, p, q, w, u, shift = gate_terms(
        gi_r, gi_z, gi_n, gh[:64], gh[64:128], gh[128:], bias1[64:], prev
    )
    tl_ref[0], tl_ref[1], tl_ref[2], tl_ref[3] = squash, p, q, w
    first = iota((H, T), 1) == 0
    pk_ref[0] = packed(jnp.where(first, 0.0, p))
    pk_ref[1] = packed(jnp.where(first, 0.0, q))
    pk_ref[2] = packed(jnp.where(first, 0.0, w))
    pk_ref[3] = packed(jnp.where(first, 1.0, u))
    pk_ref[4] = packed(jnp.where(first, 0.0, shift))
    pk_ref[5] = packed(c_ref[...])

    lane64 = iota((H, 128), 1)
    low64 = lane64 < H
    eye2 = jnp.where((lane64 == iota((H, 128), 0)) | (lane64 == iota((H, 128), 0) + H), 1.0, 0.0)
    wn2 = jnp.concatenate([wh[:, 128:192], wh[:, 128:192]], axis=1)
    wr2 = jnp.concatenate([wh[:, :64], wh[:, :64]], axis=1)
    wz2 = jnp.concatenate([wh[:, 64:128], wh[:, 64:128]], axis=1)

    def rows(k, step):
        return pk_ref[k, pl.ds(step, PAIRS, stride=RUN), :]

    def put(c, value, cot):
        y_ref[c] = value
        lhs_ref[c * H:(c + 1) * H, :] = halves(value)
        return value * cot

    def put_b(value):
        b_ref[...] = value
        lhs_ref[512:528, :] = halves(jnp.concatenate([value, jnp.zeros_like(value)], axis=0))

    p0, q0, w0, u0, s0, c0 = [rows(k, 0) for k in range(6)]
    for c in range(PAIRS):
        value = (
            p0[c:c + 1] * wn2 + q0[c:c + 1] * wr2 + w0[c:c + 1] * wz2 + u0[c:c + 1] * eye2
        )
        z_ref[c] = put(c, value, c0[c:c + 1])
    put_b(s0)

    def step(l, carry):
        p1, q1, w1, u1, s1, c1 = [rows(k, l) for k in range(6)]
        for c in range(PAIRS):
            if c % GROUP == 0:
                lhs = lhs_ref[c * H:(c + GROUP) * H, :]
                first, second = bdot(lhs, w1_ref[...]), bdot(lhs[:, :128], w2_ref[...])
            part = slice((c % GROUP) * H, (c % GROUP + 1) * H)
            n, r, z = gates_of(first[part], second[part])
            value = (
                u1[c:c + 1] * y_ref[c] + p1[c:c + 1] * n + q1[c:c + 1] * r + w1[c:c + 1] * z
            )
            z_ref[c] += put(c, value, c1[c:c + 1])
        lhs = lhs_ref[512:528, :]
        first, second = bdot(lhs, w1_ref[...]), bdot(lhs[:, :128], w2_ref[...])
        n, r, z = gates_of(first[:8], second[:8])
        put_b(u1 * b_ref[...] + p1 * n + q1 * r + w1 * z + s1)
        return carry

    lax.fori_loop(1, RUN, step, 0, unroll=True)

    low8 = iota((8, 128), 1) < H
    top8 = iota((8, 128), 0) == 0
    bs = b_ref[...]
    for c in range(PAIRS):
        y = y_ref[c]
        z = z_ref[c]
        offs = jnp.broadcast_to(bs[c:c + 1], (8, 128))
        for part in range(2):
            if part:
                y, z, offs = pltpu.roll(y, H, 1), pltpu.roll(z, H, 1), pltpu.roll(offs, H, 1)
            col = jnp.sum(jnp.where(low64, z, 0.0), axis=1, keepdims=True)
            n = c + part * PAIRS
            aug_ref[n, 0:64, :] = jnp.where(low64, y, jnp.where(lane64 == H, col, 0.0))
            aug_ref[n, 64:72, :] = jnp.where(low8 & top8, offs, 0.0)
    sups = []
    for k in range(4):
        left = combine(aug_ref[4 * k], aug_ref[4 * k + 1])
        right = combine(aug_ref[4 * k + 2], aug_ref[4 * k + 3])
        sups.append(combine(left, right))
        sup_ref[k] = sups[-1]
    total = combine(combine(sups[0], sups[1]), combine(sups[2], sups[3]))

    low32 = iota((32, 128), 1) < H
    body = jnp.where(low32, total[:32], pltpu.roll(total[32:64], H, 1))
    col = jnp.sum(jnp.where(lane64 == H, total[:64], 0.0), axis=1, keepdims=True)
    row_bc = jnp.where(low8[:1], total[64:65], 0.0) + to_row(col, H)
    last = jnp.sum(jnp.where(lane64 == 127, guess[:, 128:], 0.0), axis=1, keepdims=True)

    def head(a):
        return jnp.sum(jnp.where(lane64 == 0, a[:, :128], 0.0), axis=1, keepdims=True)

    row_gr = to_row(last, 0) + to_row(head(gi_r), H)
    row_zn = to_row(head(gi_z), 0) + to_row(head(gi_n), H)
    row8 = iota((8, 128), 0)
    tail = jnp.where(row8 == 0, row_bc, jnp.where(row8 == 1, row_gr, jnp.where(row8 == 2, row_zn, 0.0)))
    for k in range(HALF):
        send_ref[k, 0:32, :] = body
        send_ref[k, 32:40, :] = tail


def apply_kernel(
    me_ref, own_ref, other_ref, aug_ref, sup_ref, pk_ref, tl_ref, w1_ref, w2_ref, wt_ref, hb_ref,
    x_hbm, g_hbm,
    state_hbm, adj_hbm, keep_ref, give_ref,
    lhs_ref, z_ref, zt_ref, row_ref, bnd_ref, st_ref, lam_ref, x_ref, g_ref, sems,
    state_ref, adj_ref, out_sems,
):
    copies = fetch([(g_hbm, g_ref), (x_hbm, x_ref)], sems)
    me = me_ref[0]
    core = me % 2
    for k in range(3):
        row_ref[k, pl.ds(core, HALF, stride=2), :] = own_ref[:, 32 + k, :]
        row_ref[k, pl.ds(1 - core, HALF, stride=2), :] = other_ref[:, 32 + k, :]
    bc, gr, zn = row_ref[0], row_ref[1], row_ref[2]
    low16 = iota((HALF, 128), 1) < H

    def pair_low(a):
        return jnp.where(low16, a[:HALF], pltpu.roll(a[HALF:], H, 1))

    def pair_high(a):
        return jnp.where(low16, pltpu.roll(a[:HALF], H, 1), a[HALF:])

    gr_next = pltpu.roll(gr, DEV - 1, 0)
    zn_next = pltpu.roll(zn, DEV - 1, 0)
    prev = jnp.where((iota((HALF, 128), 0) == HALF - 1) & ~low16, 0.0, pair_low(gr))
    n, r, z = narrow_gates(prev, w1_ref, w2_ref)
    terms = gate_terms(
        pair_high(gr_next), pair_low(zn_next), pair_high(zn_next), r, z, n, hb_ref[0:1, :], prev
    )
    for k in range(6):
        bnd_ref[k] = terms[k]
    bnd_ref[6] = prev
    squash, p, q, w, u, shift = terms

    lane64 = iota((H, 128), 1)
    row64 = iota((H, 128), 0)
    low32 = iota((32, 128), 1) < H
    for ref, side in ((own_ref, core), (other_ref, 1 - core)):
        for k in range(HALF // 2):
            a, b = ref[k, 0:32, :], ref[k + HALF // 2, 0:32, :]
            top = jnp.where(low32, a, pltpu.roll(b, H, 1))
            bottom = jnp.where(low32, pltpu.roll(a, H, 1), b)
            value = jnp.concatenate([top, bottom], axis=0)
            z_ref[2 * k + side] = value
            start = pl.multiple_of((2 * k + side) * H, H)
            lhs_ref[pl.ds(start, H), :] = halves(value)
    offs = pair_low(bc)
    lhs_ref[HALF * H:, :] = halves(offs)
    for k in range(HALF):
        if k % GROUP == 0:
            lhs = lhs_ref[k * H:(k + GROUP) * H, :]
            first, second = bdot(lhs, w1_ref[...]), bdot(lhs[:, :128], w2_ref[...])
        part = slice((k % GROUP) * H, (k % GROUP + 1) * H)
        n, r, z = gates_of(first[part], second[part])
        value = u[k:k + 1] * z_ref[k] + p[k:k + 1] * n + q[k:k + 1] * r + w[k:k + 1] * z
        z_ref[k] = value
        if k % 2:
            zt_ref[k // 2] = jnp.concatenate([value, pltpu.roll(value, H, 1)], axis=0).T[:H]
    lhs = lhs_ref[HALF * H:, :]
    n, r, z = gates_of(bdot(lhs, w1_ref[...]), bdot(lhs[:, :128], w2_ref[...]))
    fwd_rows = u * offs + p * n + q * r + w * z + shift
    bwd_rows = pair_high(bc)
    empty = jnp.zeros((128 - HALF, 128), F32)
    fwd_cols = jnp.concatenate([fwd_rows, empty], axis=0).T
    bwd_cols = jnp.concatenate([bwd_rows, empty], axis=0).T

    lane1 = iota((1, 128), 1)
    low1 = lane1 < H
    eye_a = lane64 == row64
    eye_b = lane64 == row64 + H
    shift_last = shift[HALF - 1:HALF, :]
    x_col = jnp.sum(jnp.where(eye_b, shift_last, 0.0), axis=1, keepdims=True)
    lam_row = jnp.where(low1, 0.0, bwd_rows[HALF - 1:HALF, :])
    zero_col, zero_row = jnp.zeros((H, 1), F32), jnp.zeros((1, 128), F32)
    x_keep = jnp.where(me == 0, x_col, zero_col)
    lam_keep = zero_col
    x_rows, lam_rows = zero_row, jnp.where(me + 1 == DEV - 1, lam_row, zero_row)

    def half(k, row):
        return jnp.where(low1, row, 0.0) if k < HALF else jnp.where(low1, 0.0, row)

    def side_cols(cols, k):
        return jnp.where(lane64 == k % HALF, cols[:H] if k < HALF else cols[H:], 0.0)

    for i in range(DEV - 1):
        k, m = i, i % HALF
        if k % 2 == 0:
            x_row = half(k, jnp.sum(x_col * z_ref[m], axis=0, keepdims=True) + fwd_rows[m:m + 1])
            x_rows = jnp.where(me == k + 1, x_row, x_rows)
        else:
            x_col = jnp.sum(zt_ref[m // 2] * x_row + side_cols(fwd_cols, k), axis=1, keepdims=True)
            x_keep = jnp.where(me == k + 1, x_col, x_keep)
        k = DEV - 2 - i
        m = k % HALF
        if k % 2 == 0:
            lam_col = jnp.sum(z_ref[m] * lam_row + side_cols(bwd_cols, k), axis=1, keepdims=True)
            lam_keep = jnp.where(me + 1 == k, lam_col, lam_keep)
        else:
            lam_row = half(
                k, jnp.sum(lam_col * zt_ref[m // 2], axis=0, keepdims=True) + bwd_rows[m:m + 1]
            )
            lam_rows = jnp.where(me + 1 == k, lam_row, lam_rows)

    def settled(rows, column):
        row = jnp.where(low1, rows, 0.0) + jnp.where(low1, pltpu.roll(rows, H, 1), 0.0)
        return row + jnp.sum(jnp.where(eye_a, column, 0.0), axis=0, keepdims=True)

    x = settled(x_rows, x_keep)
    lam = settled(lam_rows, lam_keep)

    def boundary(k, index):
        row = bnd_ref[k, pl.ds(index % HALF, 1), :]
        return jnp.where(low1, jnp.where(index >= HALF, pltpu.roll(row, H, 1), row), 0.0)

    lam8 = jnp.broadcast_to(lam, (8, 128))
    mixed = jnp.concatenate([lam8 * boundary(k, me) for k in (1, 2, 3)], axis=1)
    carry = (pulled(mixed, wt_ref) + lam8 * boundary(4, me))[0:1]

    row72 = iota((72, 128), 0)
    eye72 = iota((72, 128), 1) == row72
    one = lane1 == H

    def ahead(maps, x):
        col = jnp.sum(jnp.where(eye72, x, 0.0), axis=1, keepdims=True)
        return jnp.where(one, 1.0, jnp.sum(col * maps, axis=0, keepdims=True))

    def back(maps, lam):
        col = jnp.sum(maps[:H] * lam, axis=1, keepdims=True)
        return jnp.where(one, 1.0, jnp.sum(jnp.where(eye_a, col, 0.0), axis=0, keepdims=True))

    starts = [jnp.where(one, 1.0, x)]
    for k in range(3):
        starts.append(ahead(sup_ref[k], starts[-1]))
    ends = [jnp.where(one, 1.0, carry)]
    for k in (3, 2, 1):
        ends.append(back(sup_ref[k], ends[-1]))
    ends = ends[::-1]
    state_rows, carry_rows = [None] * 16, [None] * 16
    for k in range(4):
        value, lam = starts[k], ends[k]
        for j in range(4):
            state_rows[4 * k + j] = value
            carry_rows[4 * k + 3 - j] = lam
            if j < 3:
                value = ahead(aug_ref[4 * k + j], value)
                lam = back(aug_ref[4 * k + 3 - j], lam)

    def gather(items):
        left = jnp.concatenate(items[:8], axis=0)
        right = jnp.concatenate(items[8:], axis=0)
        return jnp.where(iota((8, 128), 1) < H, left, pltpu.roll(right, H, 1))

    def rows(k, step):
        return pk_ref[k, pl.ds(step, PAIRS, stride=RUN), :]

    state, kappa = gather(state_rows), gather(carry_rows)
    for i in range(RUN):
        j = RUN - 1 - i
        n, r, z = narrow_gates(state, w1_ref, w2_ref)
        lam = rows(5, j) + kappa
        lam_ref[pl.ds(j, PAIRS, stride=RUN), :] = lam
        mixed = jnp.concatenate([lam * rows(0, j), lam * rows(1, j), lam * rows(2, j)], axis=1)
        kappa = pulled(mixed, wt_ref) + lam * rows(3, j)
        state = rows(3, i) * state + rows(0, i) * n + rows(1, i) * r + rows(2, i) * z + rows(4, i)
        st_ref[pl.ds(i, PAIRS, stride=RUN), :] = state

    states = st_ref[...].T
    state_ref[:, :128] = states[:H]
    state_ref[:, 128:] = states[H:]
    lams = lam_ref[...].T
    lams = jnp.concatenate([lams[:H], lams[H:]], axis=1)
    adj_ref[...] = lams
    results = fetch([(state_ref, state_hbm), (adj_ref, adj_hbm)], out_sems)

    before = (me + DEV - 1) % DEV
    first = iota((H, T), 1) == 0

    def with_first(a, k):
        col = jnp.sum(jnp.where(eye_a, boundary(k, before), 0.0), axis=1, keepdims=True)
        return jnp.where(first, col, a)

    for copy in copies:
        copy.wait()
    squash, p, q, w = [with_first(tl_ref[k], k) for k in range(4)]
    prev = with_first(pltpu.roll(g_ref[...], 1, 1), 6)
    left = jnp.concatenate([x_ref[...], prev, jnp.ones((8, T), F32)], axis=0)
    right = jnp.concatenate([lams * q, lams * w, lams * squash, lams * p], axis=0)
    sums = dot(left, right, ((1,), (1,)))
    row8 = iota((8, 128), 0)
    biases = jnp.where(
        row8 == 0, sums[128:136, :128], jnp.where(row8 == 1, sums[128:136, 128:], 0.0)
    )
    last = jnp.where(lane64 < H, sums[:64, 128:], sums[64:128, 128:])
    first_half = sums[:PART, :128]
    second_half = jnp.concatenate([sums[PART:128, :128], last, biases, jnp.zeros((8, 128), F32)], axis=0)
    keep_ref[...] = jnp.where(core == 0, first_half, second_half)
    give_ref[...] = jnp.where(core == 0, second_half, first_half)
    for copy in results:
        copy.wait()


def finish_kernel(me_ref, own_ref, other_ref, gin_ref, ghid_ref, gbias_ref, *, scale):
    core = me_ref[0] % 2
    own, other = own_ref[...] * scale, other_ref[...] * scale
    whole = jnp.concatenate(
        [jnp.where(core == 0, own, other), jnp.where(core == 0, other, own)], axis=0
    )
    gin_ref[:, :128] = whole[:64]
    gin_ref[:, 128:] = whole[128:192, :64]
    ghid_ref[:, :128] = whole[64:128]
    ghid_ref[:, 128:] = whole[128:192, 64:]
    gbias_ref[...] = whole[192:194]


def shape(*dims):
    return jax.ShapeDtypeStruct(dims, F32)


def swapped(a):
    return lax.ppermute(a, "tm", [(k, k ^ 1) for k in range(DEV)])


def grouped(members):
    found = {}
    for z in range(4):
        for y in range(4):
            for x in range(4):
                for core in range(2):
                    place = z * DEV + y * 8 + x * 2 + core
                    found.setdefault(members(z, y, x, core), []).append(place)
    return list(found.values())


AROUND = grouped(lambda z, y, x, core: (z, y // 2, core))
ACROSS = grouped(lambda z, y, x, core: (y % 2, x, core))


def per_device(inputs, guess, cotangent, w_input, w_hidden, bias):
    x = jnp.swapaxes(inputs[0], 0, 1)
    g = jnp.swapaxes(guess[0], 0, 1)
    c = jnp.swapaxes(cotangent[0], 0, 1)
    bias2 = bias.reshape(2, 128)
    x, g, c, w_input, w_hidden, bias2 = [
        pltpu.with_memory_space_constraint(a, pltpu.HBM)
        for a in (x, g, c, w_input, w_hidden, bias2)
    ]
    vmem = pl.BlockSpec(memory_space=pltpu.VMEM)
    hbm = pl.BlockSpec(memory_space=pltpu.HBM)
    smem = pl.BlockSpec(memory_space=pltpu.SMEM)
    wide = [pltpu.VMEM((H, T), F32)] * 3
    params = pltpu.CompilerParams(vmem_limit_bytes=VMEM_LIMIT)
    send, *kept = pl.pallas_call(
        blocks_kernel,
        out_shape=(
            shape(HALF, TILE, 128), shape(16, 72, 128), shape(4, 72, 128),
            shape(6, 128, 128), shape(4, H, T),
            jax.ShapeDtypeStruct((256, 512), BF16), jax.ShapeDtypeStruct((128, 256), BF16),
            jax.ShapeDtypeStruct((384, 256), BF16), shape(8, 128),
        ),
        in_specs=[hbm] * 6,
        out_specs=[vmem] * 9,
        scratch_shapes=[
            pltpu.VMEM((PAIRS, H, 128), F32),
            pltpu.VMEM((PAIRS, H, 128), F32),
            pltpu.VMEM((8, 128), F32),
            pltpu.VMEM((528, 256), BF16),
        ] + wide + [
            pltpu.VMEM((H, 192), F32),
            pltpu.VMEM((H, 192), F32),
            pltpu.VMEM((2, 128), F32),
            pltpu.SemaphoreType.DMA((6,)),
        ],
        compiler_params=params,
        name="blocks",
    )(x, g, c, w_input, w_hidden, bias2)
    groups = [[2 * k + core for k in range(HALF)] for core in range(2)]
    received = lax.all_to_all(send, "tm", 0, 0, axis_index_groups=groups)
    other = swapped(received)
    me = lax.axis_index("tm").astype(jnp.int32).reshape(1)
    states, adjoint, part, give = pl.pallas_call(
        apply_kernel,
        out_shape=(shape(H, T), shape(H, T), shape(PART, 128), shape(PART, 128)),
        in_specs=[smem] + [vmem] * 10 + [hbm] * 2,
        out_specs=[hbm] * 2 + [vmem] * 2,
        scratch_shapes=[
            pltpu.VMEM((HALF * H + 16, 256), BF16),
            pltpu.VMEM((HALF, H, 128), F32),
            pltpu.VMEM((HALF // 2, H, 128), F32),
            pltpu.VMEM((3, DEV, 128), F32),
            pltpu.VMEM((7, HALF, 128), F32),
            pltpu.VMEM((128, 128), F32),
            pltpu.VMEM((128, 128), F32),
        ] + wide[:2] + [pltpu.SemaphoreType.DMA((2,))] + wide[:2] + [pltpu.SemaphoreType.DMA((2,))],
        compiler_params=params,
        name="apply",
    )(me, received, other, *kept, x, g)
    part = part + swapped(give)
    axes = ("seq", "tm")
    for group in (AROUND, ACROSS):
        copies = jnp.broadcast_to(part[None], (8, PART, 128))
        part = jnp.sum(lax.all_to_all(copies, axes, 0, 0, axis_index_groups=group), axis=0)
    scale = 1.0 / math.sqrt(lax.axis_size("seq") * lax.axis_size("tm") * T)
    grad_input, grad_hidden, grad_bias = pl.pallas_call(
        functools.partial(finish_kernel, scale=scale),
        out_shape=(shape(H, 192), shape(H, 192), shape(2, 128)),
        in_specs=[smem, vmem, vmem],
        out_specs=[vmem] * 3,
        compiler_params=params,
        name="finish",
    )(me, part, swapped(part))
    grad_bias = grad_bias.reshape(256)
    return (
        jnp.swapaxes(states, 0, 1)[None], jnp.swapaxes(adjoint, 0, 1)[None],
        grad_input, grad_hidden, grad_bias,
    )


def solution(mesh):
    return jax.shard_map(
        per_device,
        mesh=mesh,
        in_specs=(P("seq", "tm", None), P("seq", "tm", None), P("seq", "tm", None), P(), P(), P()),
        out_specs=(P("seq", "tm", None), P("seq", "tm", None), P(), P(), P()),
        check_vma=False,
    )
```

```python
import functools
import math

import jax
import jax.numpy as jnp
from jax import lax
from jax.experimental import pallas as pl
from jax.experimental.pallas import tpu as pltpu
from jax.sharding import PartitionSpec as P

F32 = jnp.float32
BF16 = jnp.bfloat16
HIGHEST = lax.Precision.HIGHEST
H = 64
T = 256
RUN = 16
PAIRS = 8
DEV = 32
HALF = DEV // 2
TILE = 40
GROUP = 2
PART = 104
VMEM_LIMIT = 48 * 1024 * 1024


def dot(a, b, dims=((1,), (0,))):
    return lax.dot_general(a, b, (dims, ((), ())), precision=HIGHEST, preferred_element_type=F32)


def bdot(a, b):
    return jnp.dot(a, b, preferred_element_type=F32)


def iota(shape, axis):
    return lax.broadcasted_iota(jnp.int32, shape, axis)


def split(a):
    high = a.astype(BF16)
    return high, (a - high.astype(F32)).astype(BF16)


def sigmoid(a):
    return 1.0 / (1.0 + jnp.exp(-a))


def doubled(block):
    zero = jnp.zeros_like(block)
    return jnp.concatenate(
        [jnp.concatenate([block, zero], axis=1), jnp.concatenate([zero, block], axis=1)], axis=0
    )


def side_weights(wh):
    n, r, z = [split(doubled(wh[:, k:k + H])) for k in (128, 0, 64)]
    zero = jnp.zeros((128, 128), BF16)
    top = jnp.concatenate([n[0], r[0], z[0], n[1]], axis=1)
    bottom = jnp.concatenate([n[0], r[0], z[0], zero], axis=1)
    return jnp.concatenate([top, bottom], axis=0), jnp.concatenate([r[1], z[1]], axis=1)


def halves(value):
    return jnp.concatenate(split(value), axis=1)


def gates_of(first, second):
    return (
        first[:, :128] + first[:, 384:], first[:, 128:256] + second[:, :128],
        first[:, 256:384] + second[:, 128:],
    )


def backward_weights(wh):
    tall = jnp.concatenate([doubled(wh[:, k:k + H].T) for k in (128, 0, 64)], axis=0)
    return jnp.concatenate(split(tall), axis=1)


def stacked(value):
    high = value.astype(BF16).astype(F32)
    return jnp.concatenate([high, value - high], axis=0).astype(BF16)


def narrow_gates(value, w1_ref, w2_ref):
    rows = value.shape[0]
    weights = jnp.concatenate([w1_ref[:128, :], w2_ref[...]], axis=1)
    out = bdot(stacked(value), weights)
    high, low = out[:rows], out[rows:]
    n = high[:, :128] + high[:, 384:512] + low[:, :128]
    r = high[:, 128:256] + high[:, 512:640] + low[:, 128:256]
    z = high[:, 256:384] + high[:, 640:] + low[:, 256:384]
    return n, r, z


def pulled(mixed, wt_ref):
    rows = mixed.shape[0]
    out = bdot(stacked(mixed), wt_ref[...])
    return out[:rows, :128] + out[rows:, :128] + out[:rows, 128:]


def to_row(column, offset):
    hit = iota((H, 128), 1) == iota((H, 128), 0) + offset
    return jnp.sum(jnp.where(hit, column, 0.0), axis=0, keepdims=True)


def gate_terms(gi_r, gi_z, gi_n, gh_r, gh_z, gh_n, bias_h, prev):
    reset = sigmoid(gi_r + gh_r)
    update = sigmoid(gi_z + gh_z)
    keep = sigmoid(-(gi_z + gh_z))
    hsum = gh_n + bias_h
    cand = jnp.tanh(gi_n + reset * hsum)
    squash = keep * (1.0 - cand * cand)
    p = squash * reset
    q = squash * hsum * reset * (1.0 - reset)
    w = (prev - cand) * update * keep
    shift = keep * cand - p * gh_n - q * gh_r - w * gh_z
    return squash, p, q, w, update, shift


def packed(a):
    return jnp.concatenate([a[:, :128], a[:, 128:]], axis=0).T


def combine(earlier, later):
    row, lane = iota((72, 128), 0), iota((72, 128), 1)
    out = bdot(stacked(earlier[:, :H]), jnp.concatenate(split(later[:H, :]), axis=1))
    product = out[:72, :128] + out[72:, :128] + out[:72, 128:]
    return (
        product
        + jnp.where((lane == H) & (row < H), earlier, 0.0)
        + jnp.where((row == H) & (lane < H), later, 0.0)
    )


def fetch(pairs, sems):
    copies = [pltpu.make_async_copy(a, b, sems.at[k]) for k, (a, b) in enumerate(pairs)]
    for copy in copies:
        copy.start()
    return copies


def blocks_kernel(
    x_hbm, g_hbm, c_hbm, wi_hbm, wh_hbm, bias_hbm,
    send_ref, aug_ref, sup_ref, pk_ref, tl_ref, w1_ref, w2_ref, wt_ref, hb_ref,
    y_ref, z_ref, b_ref, lhs_ref,
    x_ref, g_ref, c_ref, wi_ref, wh_ref, bias_ref, sems,
):
    for copy in fetch(
        [(wh_hbm, wh_ref), (g_hbm, g_ref), (wi_hbm, wi_ref), (x_hbm, x_ref), (bias_hbm, bias_ref),
         (c_hbm, c_ref)], sems,
    ):
        copy.wait()
    wh = wh_ref[...]
    w1_ref[...], w2_ref[...] = side_weights(wh)
    wt_ref[...] = backward_weights(wh)
    hb = jnp.broadcast_to(bias_ref[1:2, :], (8, 128))
    hb_ref[...] = jnp.where(iota((8, 128), 1) < H, pltpu.roll(hb, H, 1), hb)
    guess = g_ref[...]
    prev = pltpu.roll(guess, 1, 1)
    gi = dot(wi_ref[...], x_ref[...], ((0,), (0,)))
    gh = dot(wh, prev, ((0,), (0,)))
    bias0 = jnp.broadcast_to(bias_ref[0:1, :], (128, 128)).T
    bias1 = jnp.broadcast_to(bias_ref[1:2, :], (128, 128)).T
    bias0 = jnp.concatenate([bias0, bias0], axis=1)
    bias1 = jnp.concatenate([bias1, bias1], axis=1)
    gi_r = gi[:64] + bias0[:64]
    gi_z = gi[64:128] + bias0[64:]
    gi_n = gi[128:] + bias1[:64]
    squash, p, q, w, u, shift = gate_terms(
        gi_r, gi_z, gi_n, gh[:64], gh[64:128], gh[128:], bias1[64:], prev
    )
    tl_ref[0], tl_ref[1], tl_ref[2], tl_ref[3] = squash, p, q, w
    first = iota((H, T), 1) == 0
    pk_ref[0] = packed(jnp.where(first, 0.0, p))
    pk_ref[1] = packed(jnp.where(first, 0.0, q))
    pk_ref[2] = packed(jnp.where(first, 0.0, w))
    pk_ref[3] = packed(jnp.where(first, 1.0, u))
    pk_ref[4] = packed(jnp.where(first, 0.0, shift))
    pk_ref[5] = packed(c_ref[...])

    lane64 = iota((H, 128), 1)
    low64 = lane64 < H
    eye2 = jnp.where((lane64 == iota((H, 128), 0)) | (lane64 == iota((H, 128), 0) + H), 1.0, 0.0)
    wn2 = jnp.concatenate([wh[:, 128:192], wh[:, 128:192]], axis=1)
    wr2 = jnp.concatenate([wh[:, :64], wh[:, :64]], axis=1)
    wz2 = jnp.concatenate([wh[:, 64:128], wh[:, 64:128]], axis=1)

    def rows(k, step):
        return pk_ref[k, pl.ds(step, PAIRS, stride=RUN), :]

    def put(c, value, cot):
        y_ref[c] = value
        lhs_ref[c * H:(c + 1) * H, :] = halves(value)
        return value * cot

    def put_b(value):
        b_ref[...] = value
        lhs_ref[512:528, :] = halves(jnp.concatenate([value, jnp.zeros_like(value)], axis=0))

    p0, q0, w0, u0, s0, c0 = [rows(k, 0) for k in range(6)]
    for c in range(PAIRS):
        value = (
            p0[c:c + 1] * wn2 + q0[c:c + 1] * wr2 + w0[c:c + 1] * wz2 + u0[c:c + 1] * eye2
        )
        z_ref[c] = put(c, value, c0[c:c + 1])
    put_b(s0)

    def step(l, carry):
        p1, q1, w1, u1, s1, c1 = [rows(k, l) for k in range(6)]
        for c in range(PAIRS):
            if c % GROUP == 0:
                lhs = lhs_ref[c * H:(c + GROUP) * H, :]
                first, second = bdot(lhs, w1_ref[...]), bdot(lhs[:, :128], w2_ref[...])
            part = slice((c % GROUP) * H, (c % GROUP + 1) * H)
            n, r, z = gates_of(first[part], second[part])
            value = (
                u1[c:c + 1] * y_ref[c] + p1[c:c + 1] * n + q1[c:c + 1] * r + w1[c:c + 1] * z
            )
            z_ref[c] += put(c, value, c1[c:c + 1])
        lhs = lhs_ref[512:528, :]
        first, second = bdot(lhs, w1_ref[...]), bdot(lhs[:, :128], w2_ref[...])
        n, r, z = gates_of(first[:8], second[:8])
        put_b(u1 * b_ref[...] + p1 * n + q1 * r + w1 * z + s1)
        return carry

    lax.fori_loop(1, RUN, step, 0, unroll=True)

    low8 = iota((8, 128), 1) < H
    top8 = iota((8, 128), 0) == 0
    bs = b_ref[...]
    for c in range(PAIRS):
        y = y_ref[c]
        z = z_ref[c]
        offs = jnp.broadcast_to(bs[c:c + 1], (8, 128))
        for part in range(2):
            if part:
                y, z, offs = pltpu.roll(y, H, 1), pltpu.roll(z, H, 1), pltpu.roll(offs, H, 1)
            col = jnp.sum(jnp.where(low64, z, 0.0), axis=1, keepdims=True)
            n = c + part * PAIRS
            aug_ref[n, 0:64, :] = jnp.where(low64, y, jnp.where(lane64 == H, col, 0.0))
            aug_ref[n, 64:72, :] = jnp.where(low8 & top8, offs, 0.0)
    sups = []
    for k in range(4):
        left = combine(aug_ref[4 * k], aug_ref[4 * k + 1])
        right = combine(aug_ref[4 * k + 2], aug_ref[4 * k + 3])
        sups.append(combine(left, right))
        sup_ref[k] = sups[-1]
    total = combine(combine(sups[0], sups[1]), combine(sups[2], sups[3]))

    low32 = iota((32, 128), 1) < H
    body = jnp.where(low32, total[:32], pltpu.roll(total[32:64], H, 1))
    col = jnp.sum(jnp.where(lane64 == H, total[:64], 0.0), axis=1, keepdims=True)
    row_bc = jnp.where(low8[:1], total[64:65], 0.0) + to_row(col, H)
    last = jnp.sum(jnp.where(lane64 == 127, guess[:, 128:], 0.0), axis=1, keepdims=True)

    def head(a):
        return jnp.sum(jnp.where(lane64 == 0, a[:, :128], 0.0), axis=1, keepdims=True)

    row_gr = to_row(last, 0) + to_row(head(gi_r), H)
    row_zn = to_row(head(gi_z), 0) + to_row(head(gi_n), H)
    row8 = iota((8, 128), 0)
    tail = jnp.where(row8 == 0, row_bc, jnp.where(row8 == 1, row_gr, jnp.where(row8 == 2, row_zn, 0.0)))
    for k in range(HALF):
        send_ref[k, 0:32, :] = body
        send_ref[k, 32:40, :] = tail


def apply_kernel(
    me_ref, own_ref, other_ref, aug_ref, sup_ref, pk_ref, tl_ref, w1_ref, w2_ref, wt_ref, hb_ref,
    x_hbm, g_hbm,
    state_hbm, adj_hbm, keep_ref, give_ref,
    lhs_ref, z_ref, zt_ref, row_ref, bnd_ref, st_ref, lam_ref, x_ref, g_ref, sems,
    state_ref, adj_ref, out_sems,
):
    copies = fetch([(g_hbm, g_ref), (x_hbm, x_ref)], sems)
    me = me_ref[0]
    core = me % 2
    for k in range(3):
        row_ref[k, pl.ds(core, HALF, stride=2), :] = own_ref[:, 32 + k, :]
        row_ref[k, pl.ds(1 - core, HALF, stride=2), :] = other_ref[:, 32 + k, :]
    bc, gr, zn = row_ref[0], row_ref[1], row_ref[2]
    low16 = iota((HALF, 128), 1) < H

    def pair_low(a):
        return jnp.where(low16, a[:HALF], pltpu.roll(a[HALF:], H, 1))

    def pair_high(a):
        return jnp.where(low16, pltpu.roll(a[:HALF], H, 1), a[HALF:])

    gr_next = pltpu.roll(gr, DEV - 1, 0)
    zn_next = pltpu.roll(zn, DEV - 1, 0)
    prev = jnp.where((iota((HALF, 128), 0) == HALF - 1) & ~low16, 0.0, pair_low(gr))
    n, r, z = narrow_gates(prev, w1_ref, w2_ref)
    terms = gate_terms(
        pair_high(gr_next), pair_low(zn_next), pair_high(zn_next), r, z, n, hb_ref[0:1, :], prev
    )
    for k in range(6):
        bnd_ref[k] = terms[k]
    bnd_ref[6] = prev
    squash, p, q, w, u, shift = terms

    lane64 = iota((H, 128), 1)
    row64 = iota((H, 128), 0)
    low32 = iota((32, 128), 1) < H
    for ref, side in ((own_ref, core), (other_ref, 1 - core)):
        for k in range(HALF // 2):
            a, b = ref[k, 0:32, :], ref[k + HALF // 2, 0:32, :]
            top = jnp.where(low32, a, pltpu.roll(b, H, 1))
            bottom = jnp.where(low32, pltpu.roll(a, H, 1), b)
            value = jnp.concatenate([top, bottom], axis=0)
            z_ref[2 * k + side] = value
            start = pl.multiple_of((2 * k + side) * H, H)
            lhs_ref[pl.ds(start, H), :] = halves(value)
    offs = pair_low(bc)
    lhs_ref[HALF * H:, :] = halves(offs)
    for k in range(HALF):
        if k % GROUP == 0:
            lhs = lhs_ref[k * H:(k + GROUP) * H, :]
            first, second = bdot(lhs, w1_ref[...]), bdot(lhs[:, :128], w2_ref[...])
        part = slice((k % GROUP) * H, (k % GROUP + 1) * H)
        n, r, z = gates_of(first[part], second[part])
        value = u[k:k + 1] * z_ref[k] + p[k:k + 1] * n + q[k:k + 1] * r + w[k:k + 1] * z
        z_ref[k] = value
        if k % 2:
            zt_ref[k // 2] = jnp.concatenate([value, pltpu.roll(value, H, 1)], axis=0).T[:H]
    lhs = lhs_ref[HALF * H:, :]
    n, r, z = gates_of(bdot(lhs, w1_ref[...]), bdot(lhs[:, :128], w2_ref[...]))
    fwd_rows = u * offs + p * n + q * r + w * z + shift
    bwd_rows = pair_high(bc)
    empty = jnp.zeros((128 - HALF, 128), F32)
    fwd_cols = jnp.concatenate([fwd_rows, empty], axis=0).T
    bwd_cols = jnp.concatenate([bwd_rows, empty], axis=0).T

    lane1 = iota((1, 128), 1)
    low1 = lane1 < H
    eye_a = lane64 == row64
    eye_b = lane64 == row64 + H
    shift_last = shift[HALF - 1:HALF, :]
    x_col = jnp.sum(jnp.where(eye_b, shift_last, 0.0), axis=1, keepdims=True)
    lam_row = jnp.where(low1, 0.0, bwd_rows[HALF - 1:HALF, :])
    zero_col, zero_row = jnp.zeros((H, 1), F32), jnp.zeros((1, 128), F32)
    x_keep = jnp.where(me == 0, x_col, zero_col)
    lam_keep = zero_col
    x_rows, lam_rows = zero_row, jnp.where(me + 1 == DEV - 1, lam_row, zero_row)

    def half(k, row):
        return jnp.where(low1, row, 0.0) if k < HALF else jnp.where(low1, 0.0, row)

    def side_cols(cols, k):
        return jnp.where(lane64 == k % HALF, cols[:H] if k < HALF else cols[H:], 0.0)

    for i in range(DEV - 1):
        k, m = i, i % HALF
        if k % 2 == 0:
            x_row = half(k, jnp.sum(x_col * z_ref[m], axis=0, keepdims=True) + fwd_rows[m:m + 1])
            x_rows = jnp.where(me == k + 1, x_row, x_rows)
        else:
            x_col = jnp.sum(zt_ref[m // 2] * x_row + side_cols(fwd_cols, k), axis=1, keepdims=True)
            x_keep = jnp.where(me == k + 1, x_col, x_keep)
        k = DEV - 2 - i
        m = k % HALF
        if k % 2 == 0:
            lam_col = jnp.sum(z_ref[m] * lam_row + side_cols(bwd_cols, k), axis=1, keepdims=True)
            lam_keep = jnp.where(me + 1 == k, lam_col, lam_keep)
        else:
            lam_row = half(
                k, jnp.sum(lam_col * zt_ref[m // 2], axis=0, keepdims=True) + bwd_rows[m:m + 1]
            )
            lam_rows = jnp.where(me + 1 == k, lam_row, lam_rows)

    def settled(rows, column):
        row = jnp.where(low1, rows, 0.0) + jnp.where(low1, pltpu.roll(rows, H, 1), 0.0)
        return row + jnp.sum(jnp.where(eye_a, column, 0.0), axis=0, keepdims=True)

    x = settled(x_rows, x_keep)
    lam = settled(lam_rows, lam_keep)

    def boundary(k, index):
        row = bnd_ref[k, pl.ds(index % HALF, 1), :]
        return jnp.where(low1, jnp.where(index >= HALF, pltpu.roll(row, H, 1), row), 0.0)

    lam8 = jnp.broadcast_to(lam, (8, 128))
    mixed = jnp.concatenate([lam8 * boundary(k, me) for k in (1, 2, 3)], axis=1)
    carry = (pulled(mixed, wt_ref) + lam8 * boundary(4, me))[0:1]

    row72 = iota((72, 128), 0)
    eye72 = iota((72, 128), 1) == row72
    one = lane1 == H

    def ahead(maps, x):
        col = jnp.sum(jnp.where(eye72, x, 0.0), axis=1, keepdims=True)
        return jnp.where(one, 1.0, jnp.sum(col * maps, axis=0, keepdims=True))

    def back(maps, lam):
        col = jnp.sum(maps[:H] * lam, axis=1, keepdims=True)
        return jnp.where(one, 1.0, jnp.sum(jnp.where(eye_a, col, 0.0), axis=0, keepdims=True))

    starts = [jnp.where(one, 1.0, x)]
    for k in range(3):
        starts.append(ahead(sup_ref[k], starts[-1]))
    ends = [jnp.where(one, 1.0, carry)]
    for k in (3, 2, 1):
        ends.append(back(sup_ref[k], ends[-1]))
    ends = ends[::-1]
    state_rows, carry_rows = [None] * 16, [None] * 16
    for k in range(4):
        value, lam = starts[k], ends[k]
        for j in range(4):
            state_rows[4 * k + j] = value
            carry_rows[4 * k + 3 - j] = lam
            if j < 3:
                value = ahead(aug_ref[4 * k + j], value)
                lam = back(aug_ref[4 * k + 3 - j], lam)

    def gather(items):
        left = jnp.concatenate(items[:8], axis=0)
        right = jnp.concatenate(items[8:], axis=0)
        return jnp.where(iota((8, 128), 1) < H, left, pltpu.roll(right, H, 1))

    def rows(k, step):
        return pk_ref[k, pl.ds(step, PAIRS, stride=RUN), :]

    state, kappa = gather(state_rows), gather(carry_rows)
    for i in range(RUN):
        j = RUN - 1 - i
        n, r, z = narrow_gates(state, w1_ref, w2_ref)
        lam = rows(5, j) + kappa
        lam_ref[pl.ds(j, PAIRS, stride=RUN), :] = lam
        mixed = jnp.concatenate([lam * rows(0, j), lam * rows(1, j), lam * rows(2, j)], axis=1)
        kappa = pulled(mixed, wt_ref) + lam * rows(3, j)
        state = rows(3, i) * state + rows(0, i) * n + rows(1, i) * r + rows(2, i) * z + rows(4, i)
        st_ref[pl.ds(i, PAIRS, stride=RUN), :] = state

    states = st_ref[...].T
    state_ref[:, :128] = states[:H]
    state_ref[:, 128:] = states[H:]
    lams = lam_ref[...].T
    lams = jnp.concatenate([lams[:H], lams[H:]], axis=1)
    adj_ref[...] = lams
    results = fetch([(state_ref, state_hbm), (adj_ref, adj_hbm)], out_sems)

    before = (me + DEV - 1) % DEV
    first = iota((H, T), 1) == 0

    def with_first(a, k):
        col = jnp.sum(jnp.where(eye_a, boundary(k, before), 0.0), axis=1, keepdims=True)
        return jnp.where(first, col, a)

    for copy in copies:
        copy.wait()
    squash, p, q, w = [with_first(tl_ref[k], k) for k in range(4)]
    prev = with_first(pltpu.roll(g_ref[...], 1, 1), 6)
    left = jnp.concatenate([x_ref[...], prev, jnp.ones((8, T), F32)], axis=0)
    right = jnp.concatenate([lams * q, lams * w, lams * squash, lams * p], axis=0)
    sums = dot(left, right, ((1,), (1,)))
    row8 = iota((8, 128), 0)
    biases = jnp.where(
        row8 == 0, sums[128:136, :128], jnp.where(row8 == 1, sums[128:136, 128:], 0.0)
    )
    last = jnp.where(lane64 < H, sums[:64, 128:], sums[64:128, 128:])
    first_half = sums[:PART, :128]
    second_half = jnp.concatenate([sums[PART:128, :128], last, biases, jnp.zeros((8, 128), F32)], axis=0)
    keep_ref[...] = jnp.where(core == 0, first_half, second_half)
    give_ref[...] = jnp.where(core == 0, second_half, first_half)
    for copy in results:
        copy.wait()


def finish_kernel(me_ref, own_ref, other_ref, gin_ref, ghid_ref, gbias_ref, *, scale):
    core = me_ref[0] % 2
    own, other = own_ref[...] * scale, other_ref[...] * scale
    whole = jnp.concatenate(
        [jnp.where(core == 0, own, other), jnp.where(core == 0, other, own)], axis=0
    )
    gin_ref[:, :128] = whole[:64]
    gin_ref[:, 128:] = whole[128:192, :64]
    ghid_ref[:, :128] = whole[64:128]
    ghid_ref[:, 128:] = whole[128:192, 64:]
    gbias_ref[...] = whole[192:194]


def shape(*dims):
    return jax.ShapeDtypeStruct(dims, F32)


def swapped(a):
    return lax.ppermute(a, "tm", [(k, k ^ 1) for k in range(DEV)])


def grouped(members):
    found = {}
    for z in range(4):
        for y in range(4):
            for x in range(4):
                for core in range(2):
                    place = z * DEV + y * 8 + x * 2 + core
                    found.setdefault(members(z, y, x, core), []).append(place)
    return list(found.values())


AROUND = grouped(lambda z, y, x, core: (z, y // 2, core))
ACROSS = grouped(lambda z, y, x, core: (y % 2, x, core))


def per_device(inputs, guess, cotangent, w_input, w_hidden, bias):
    x = jnp.swapaxes(inputs[0], 0, 1)
    g = jnp.swapaxes(guess[0], 0, 1)
    c = jnp.swapaxes(cotangent[0], 0, 1)
    bias2 = bias.reshape(2, 128)
    x, g, c, w_input, w_hidden, bias2 = [
        pltpu.with_memory_space_constraint(a, pltpu.HBM)
        for a in (x, g, c, w_input, w_hidden, bias2)
    ]
    vmem = pl.BlockSpec(memory_space=pltpu.VMEM)
    hbm = pl.BlockSpec(memory_space=pltpu.HBM)
    smem = pl.BlockSpec(memory_space=pltpu.SMEM)
    wide = [pltpu.VMEM((H, T), F32)] * 3
    params = pltpu.CompilerParams(vmem_limit_bytes=VMEM_LIMIT)
    send, *kept = pl.pallas_call(
        blocks_kernel,
        out_shape=(
            shape(HALF, TILE, 128), shape(16, 72, 128), shape(4, 72, 128),
            shape(6, 128, 128), shape(4, H, T),
            jax.ShapeDtypeStruct((256, 512), BF16), jax.ShapeDtypeStruct((128, 256), BF16),
            jax.ShapeDtypeStruct((384, 256), BF16), shape(8, 128),
        ),
        in_specs=[hbm] * 6,
        out_specs=[vmem] * 9,
        scratch_shapes=[
            pltpu.VMEM((PAIRS, H, 128), F32),
            pltpu.VMEM((PAIRS, H, 128), F32),
            pltpu.VMEM((8, 128), F32),
            pltpu.VMEM((528, 256), BF16),
        ] + wide + [
            pltpu.VMEM((H, 192), F32),
            pltpu.VMEM((H, 192), F32),
            pltpu.VMEM((2, 128), F32),
            pltpu.SemaphoreType.DMA((6,)),
        ],
        compiler_params=params,
        name="blocks",
    )(x, g, c, w_input, w_hidden, bias2)
    groups = [[2 * k + core for k in range(HALF)] for core in range(2)]
    received = lax.all_to_all(send, "tm", 0, 0, axis_index_groups=groups)
    other = swapped(received)
    me = lax.axis_index("tm").astype(jnp.int32).reshape(1)
    states, adjoint, part, give = pl.pallas_call(
        apply_kernel,
        out_shape=(shape(H, T), shape(H, T), shape(PART, 128), shape(PART, 128)),
        in_specs=[smem] + [vmem] * 10 + [hbm] * 2,
        out_specs=[hbm] * 2 + [vmem] * 2,
        scratch_shapes=[
            pltpu.VMEM((HALF * H + 16, 256), BF16),
            pltpu.VMEM((HALF, H, 128), F32),
            pltpu.VMEM((HALF // 2, H, 128), F32),
            pltpu.VMEM((3, DEV, 128), F32),
            pltpu.VMEM((7, HALF, 128), F32),
            pltpu.VMEM((128, 128), F32),
            pltpu.VMEM((128, 128), F32),
        ] + wide[:2] + [pltpu.SemaphoreType.DMA((2,))] + wide[:2] + [pltpu.SemaphoreType.DMA((2,))],
        compiler_params=params,
        name="apply",
    )(me, received, other, *kept, x, g)
    part = part + swapped(give)
    axes = ("seq", "tm")
    for group in (AROUND, ACROSS):
        copies = jnp.broadcast_to(part[None], (8, PART, 128))
        part = jnp.sum(lax.all_to_all(copies, axes, 0, 0, axis_index_groups=group), axis=0)
    scale = 1.0 / math.sqrt(lax.axis_size("seq") * lax.axis_size("tm") * T)
    grad_input, grad_hidden, grad_bias = pl.pallas_call(
        functools.partial(finish_kernel, scale=scale),
        out_shape=(shape(H, 192), shape(H, 192), shape(2, 128)),
        in_specs=[smem, vmem, vmem],
        out_specs=[vmem] * 3,
        compiler_params=params,
        name="finish",
    )(me, part, swapped(part))
    grad_bias = grad_bias.reshape(256)
    return (
        jnp.swapaxes(states, 0, 1)[None], jnp.swapaxes(adjoint, 0, 1)[None],
        grad_input, grad_hidden, grad_bias,
    )


def solution(mesh):
    return jax.shard_map(
        per_device,
        mesh=mesh,
        in_specs=(P("seq", "tm", None), P("seq", "tm", None), P("seq", "tm", None), P(), P(), P()),
        out_specs=(P("seq", "tm", None), P("seq", "tm", None), P(), P(), P()),
        check_vma=False,
    )
```

```python
import functools
import math

import jax
import jax.numpy as jnp
from jax import lax
from jax.experimental import pallas as pl
from jax.experimental.pallas import tpu as pltpu
from jax.sharding import PartitionSpec as P

F32 = jnp.float32
BF16 = jnp.bfloat16
HIGHEST = lax.Precision.HIGHEST
H = 64
T = 256
RUN = 16
PAIRS = 8
DEV = 32
HALF = DEV // 2
TILE = 40
GROUP = 2
PART = 104
VMEM_LIMIT = 48 * 1024 * 1024


def dot(a, b, dims=((1,), (0,))):
    return lax.dot_general(a, b, (dims, ((), ())), precision=HIGHEST, preferred_element_type=F32)


def bdot(a, b):
    return jnp.dot(a, b, preferred_element_type=F32)


def iota(shape, axis):
    return lax.broadcasted_iota(jnp.int32, shape, axis)


def split(a):
    high = a.astype(BF16)
    return high, (a - high.astype(F32)).astype(BF16)


def sigmoid(a):
    return 1.0 / (1.0 + jnp.exp(-a))


def doubled(block):
    zero = jnp.zeros_like(block)
    return jnp.concatenate(
        [jnp.concatenate([block, zero], axis=1), jnp.concatenate([zero, block], axis=1)], axis=0
    )


def side_weights(wh):
    n, r, z = [split(doubled(wh[:, k:k + H])) for k in (128, 0, 64)]
    zero = jnp.zeros((128, 128), BF16)
    top = jnp.concatenate([n[0], r[0], z[0], n[1]], axis=1)
    bottom = jnp.concatenate([n[0], r[0], z[0], zero], axis=1)
    return jnp.concatenate([top, bottom], axis=0), jnp.concatenate([r[1], z[1]], axis=1)


def halves(value):
    return jnp.concatenate(split(value), axis=1)


def gates_of(first, second):
    return (
        first[:, :128] + first[:, 384:], first[:, 128:256] + second[:, :128],
        first[:, 256:384] + second[:, 128:],
    )


def backward_weights(wh):
    tall = jnp.concatenate([doubled(wh[:, k:k + H].T) for k in (128, 0, 64)], axis=0)
    return jnp.concatenate(split(tall), axis=1)


def stacked(value):
    high = value.astype(BF16).astype(F32)
    return jnp.concatenate([high, value - high], axis=0).astype(BF16)


def narrow_gates(value, w1_ref, w2_ref):
    rows = value.shape[0]
    weights = jnp.concatenate([w1_ref[:128, :], w2_ref[...]], axis=1)
    out = bdot(stacked(value), weights)
    high, low = out[:rows], out[rows:]
    n = high[:, :128] + high[:, 384:512] + low[:, :128]
    r = high[:, 128:256] + high[:, 512:640] + low[:, 128:256]
    z = high[:, 256:384] + high[:, 640:] + low[:, 256:384]
    return n, r, z


def pulled(mixed, wt_ref):
    rows = mixed.shape[0]
    out = bdot(stacked(mixed), wt_ref[...])
    return out[:rows, :128] + out[rows:, :128] + out[:rows, 128:]


def to_row(column, offset):
    hit = iota((H, 128), 1) == iota((H, 128), 0) + offset
    return jnp.sum(jnp.where(hit, column, 0.0), axis=0, keepdims=True)


def gate_terms(gi_r, gi_z, gi_n, gh_r, gh_z, gh_n, bias_h, prev):
    reset = sigmoid(gi_r + gh_r)
    update = sigmoid(gi_z + gh_z)
    keep = sigmoid(-(gi_z + gh_z))
    hsum = gh_n + bias_h
    cand = jnp.tanh(gi_n + reset * hsum)
    squash = keep * (1.0 - cand * cand)
    p = squash * reset
    q = squash * hsum * reset * (1.0 - reset)
    w = (prev - cand) * update * keep
    shift = keep * cand - p * gh_n - q * gh_r - w * gh_z
    return squash, p, q, w, update, shift


def packed(a):
    return jnp.concatenate([a[:, :128], a[:, 128:]], axis=0).T


def combine(earlier, later):
    row, lane = iota((72, 128), 0), iota((72, 128), 1)
    out = bdot(stacked(earlier[:, :H]), jnp.concatenate(split(later[:H, :]), axis=1))
    product = out[:72, :128] + out[72:, :128] + out[:72, 128:]
    return (
        product
        + jnp.where((lane == H) & (row < H), earlier, 0.0)
        + jnp.where((row == H) & (lane < H), later, 0.0)
    )


def fetch(pairs, sems):
    copies = [pltpu.make_async_copy(a, b, sems.at[k]) for k, (a, b) in enumerate(pairs)]
    for copy in copies:
        copy.start()
    return copies


def blocks_kernel(
    x_hbm, g_hbm, c_hbm, wi_hbm, wh_hbm, bias_hbm,
    send_ref, aug_ref, sup_ref, pk_ref, tl_ref, w1_ref, w2_ref, wt_ref, hb_ref,
    y_ref, z_ref, b_ref, lhs_ref,
    x_ref, g_ref, c_ref, wi_ref, wh_ref, bias_ref, sems,
):
    for copy in fetch(
        [(wh_hbm, wh_ref), (g_hbm, g_ref), (wi_hbm, wi_ref), (x_hbm, x_ref), (bias_hbm, bias_ref),
         (c_hbm, c_ref)], sems,
    ):
        copy.wait()
    wh = wh_ref[...]
    w1_ref[...], w2_ref[...] = side_weights(wh)
    wt_ref[...] = backward_weights(wh)
    hb = jnp.broadcast_to(bias_ref[1:2, :], (8, 128))
    hb_ref[...] = jnp.where(iota((8, 128), 1) < H, pltpu.roll(hb, H, 1), hb)
    guess = g_ref[...]
    prev = pltpu.roll(guess, 1, 1)
    gi = dot(wi_ref[...], x_ref[...], ((0,), (0,)))
    gh = dot(wh, prev, ((0,), (0,)))
    bias0 = jnp.broadcast_to(bias_ref[0:1, :], (128, 128)).T
    bias1 = jnp.broadcast_to(bias_ref[1:2, :], (128, 128)).T
    bias0 = jnp.concatenate([bias0, bias0], axis=1)
    bias1 = jnp.concatenate([bias1, bias1], axis=1)
    gi_r = gi[:64] + bias0[:64]
    gi_z = gi[64:128] + bias0[64:]
    gi_n = gi[128:] + bias1[:64]
    squash, p, q, w, u, shift = gate_terms(
        gi_r, gi_z, gi_n, gh[:64], gh[64:128], gh[128:], bias1[64:], prev
    )
    tl_ref[0], tl_ref[1], tl_ref[2], tl_ref[3] = squash, p, q, w
    first = iota((H, T), 1) == 0
    pk_ref[0] = packed(jnp.where(first, 0.0, p))
    pk_ref[1] = packed(jnp.where(first, 0.0, q))
    pk_ref[2] = packed(jnp.where(first, 0.0, w))
    pk_ref[3] = packed(jnp.where(first, 1.0, u))
    pk_ref[4] = packed(jnp.where(first, 0.0, shift))
    pk_ref[5] = packed(c_ref[...])

    lane64 = iota((H, 128), 1)
    low64 = lane64 < H
    eye2 = jnp.where((lane64 == iota((H, 128), 0)) | (lane64 == iota((H, 128), 0) + H), 1.0, 0.0)
    wn2 = jnp.concatenate([wh[:, 128:192], wh[:, 128:192]], axis=1)
    wr2 = jnp.concatenate([wh[:, :64], wh[:, :64]], axis=1)
    wz2 = jnp.concatenate([wh[:, 64:128], wh[:, 64:128]], axis=1)

    def rows(k, step):
        return pk_ref[k, pl.ds(step, PAIRS, stride=RUN), :]

    def put(c, value, cot):
        y_ref[c] = value
        lhs_ref[c * H:(c + 1) * H, :] = halves(value)
        return value * cot

    def put_b(value):
        b_ref[...] = value
        lhs_ref[512:528, :] = halves(jnp.concatenate([value, jnp.zeros_like(value)], axis=0))

    p0, q0, w0, u0, s0, c0 = [rows(k, 0) for k in range(6)]
    for c in range(PAIRS):
        value = (
            p0[c:c + 1] * wn2 + q0[c:c + 1] * wr2 + w0[c:c + 1] * wz2 + u0[c:c + 1] * eye2
        )
        z_ref[c] = put(c, value, c0[c:c + 1])
    put_b(s0)

    def step(l, carry):
        p1, q1, w1, u1, s1, c1 = [rows(k, l) for k in range(6)]
        for c in range(PAIRS):
            if c % GROUP == 0:
                lhs = lhs_ref[c * H:(c + GROUP) * H, :]
                first, second = bdot(lhs, w1_ref[...]), bdot(lhs[:, :128], w2_ref[...])
            part = slice((c % GROUP) * H, (c % GROUP + 1) * H)
            n, r, z = gates_of(first[part], second[part])
            value = (
                u1[c:c + 1] * y_ref[c] + p1[c:c + 1] * n + q1[c:c + 1] * r + w1[c:c + 1] * z
            )
            z_ref[c] += put(c, value, c1[c:c + 1])
        lhs = lhs_ref[512:528, :]
        first, second = bdot(lhs, w1_ref[...]), bdot(lhs[:, :128], w2_ref[...])
        n, r, z = gates_of(first[:8], second[:8])
        put_b(u1 * b_ref[...] + p1 * n + q1 * r + w1 * z + s1)
        return carry

    lax.fori_loop(1, RUN, step, 0, unroll=True)

    low8 = iota((8, 128), 1) < H
    top8 = iota((8, 128), 0) == 0
    bs = b_ref[...]
    for c in range(PAIRS):
        y = y_ref[c]
        z = z_ref[c]
        offs = jnp.broadcast_to(bs[c:c + 1], (8, 128))
        for part in range(2):
            if part:
                y, z, offs = pltpu.roll(y, H, 1), pltpu.roll(z, H, 1), pltpu.roll(offs, H, 1)
            col = jnp.sum(jnp.where(low64, z, 0.0), axis=1, keepdims=True)
            n = c + part * PAIRS
            aug_ref[n, 0:64, :] = jnp.where(low64, y, jnp.where(lane64 == H, col, 0.0))
            aug_ref[n, 64:72, :] = jnp.where(low8 & top8, offs, 0.0)
    sups = []
    for k in range(4):
        left = combine(aug_ref[4 * k], aug_ref[4 * k + 1])
        right = combine(aug_ref[4 * k + 2], aug_ref[4 * k + 3])
        sups.append(combine(left, right))
        sup_ref[k] = sups[-1]
    total = combine(combine(sups[0], sups[1]), combine(sups[2], sups[3]))

    low32 = iota((32, 128), 1) < H
    body = jnp.where(low32, total[:32], pltpu.roll(total[32:64], H, 1))
    col = jnp.sum(jnp.where(lane64 == H, total[:64], 0.0), axis=1, keepdims=True)
    row_bc = jnp.where(low8[:1], total[64:65], 0.0) + to_row(col, H)
    last = jnp.sum(jnp.where(lane64 == 127, guess[:, 128:], 0.0), axis=1, keepdims=True)

    def head(a):
        return jnp.sum(jnp.where(lane64 == 0, a[:, :128], 0.0), axis=1, keepdims=True)

    row_gr = to_row(last, 0) + to_row(head(gi_r), H)
    row_zn = to_row(head(gi_z), 0) + to_row(head(gi_n), H)
    row8 = iota((8, 128), 0)
    tail = jnp.where(row8 == 0, row_bc, jnp.where(row8 == 1, row_gr, jnp.where(row8 == 2, row_zn, 0.0)))
    for k in range(HALF):
        send_ref[k, 0:32, :] = body
        send_ref[k, 32:40, :] = tail


def apply_kernel(
    me_ref, own_ref, other_ref, aug_ref, sup_ref, pk_ref, tl_ref, w1_ref, w2_ref, wt_ref, hb_ref,
    x_hbm, g_hbm,
    state_hbm, adj_hbm, keep_ref, give_ref,
    lhs_ref, z_ref, zt_ref, row_ref, bnd_ref, st_ref, lam_ref, x_ref, g_ref, sems,
    state_ref, adj_ref, out_sems,
):
    copies = fetch([(g_hbm, g_ref), (x_hbm, x_ref)], sems)
    me = me_ref[0]
    core = me % 2
    for k in range(3):
        row_ref[k, pl.ds(core, HALF, stride=2), :] = own_ref[:, 32 + k, :]
        row_ref[k, pl.ds(1 - core, HALF, stride=2), :] = other_ref[:, 32 + k, :]
    bc, gr, zn = row_ref[0], row_ref[1], row_ref[2]
    low16 = iota((HALF, 128), 1) < H

    def pair_low(a):
        return jnp.where(low16, a[:HALF], pltpu.roll(a[HALF:], H, 1))

    def pair_high(a):
        return jnp.where(low16, pltpu.roll(a[:HALF], H, 1), a[HALF:])

    gr_next = pltpu.roll(gr, DEV - 1, 0)
    zn_next = pltpu.roll(zn, DEV - 1, 0)
    prev = jnp.where((iota((HALF, 128), 0) == HALF - 1) & ~low16, 0.0, pair_low(gr))
    n, r, z = narrow_gates(prev, w1_ref, w2_ref)
    terms = gate_terms(
        pair_high(gr_next), pair_low(zn_next), pair_high(zn_next), r, z, n, hb_ref[0:1, :], prev
    )
    for k in range(6):
        bnd_ref[k] = terms[k]
    bnd_ref[6] = prev
    squash, p, q, w, u, shift = terms

    lane64 = iota((H, 128), 1)
    row64 = iota((H, 128), 0)
    low32 = iota((32, 128), 1) < H
    for ref, side in ((own_ref, core), (other_ref, 1 - core)):
        for k in range(HALF // 2):
            a, b = ref[k, 0:32, :], ref[k + HALF // 2, 0:32, :]
            top = jnp.where(low32, a, pltpu.roll(b, H, 1))
            bottom = jnp.where(low32, pltpu.roll(a, H, 1), b)
            value = jnp.concatenate([top, bottom], axis=0)
            z_ref[2 * k + side] = value
            start = pl.multiple_of((2 * k + side) * H, H)
            lhs_ref[pl.ds(start, H), :] = halves(value)
    offs = pair_low(bc)
    lhs_ref[HALF * H:, :] = halves(offs)
    for k in range(HALF):
        if k % GROUP == 0:
            lhs = lhs_ref[k * H:(k + GROUP) * H, :]
            first, second = bdot(lhs, w1_ref[...]), bdot(lhs[:, :128], w2_ref[...])
        part = slice((k % GROUP) * H, (k % GROUP + 1) * H)
        n, r, z = gates_of(first[part], second[part])
        value = u[k:k + 1] * z_ref[k] + p[k:k + 1] * n + q[k:k + 1] * r + w[k:k + 1] * z
        z_ref[k] = value
        if k % 2:
            zt_ref[k // 2] = jnp.concatenate([value, pltpu.roll(value, H, 1)], axis=0).T[:H]
    lhs = lhs_ref[HALF * H:, :]
    n, r, z = gates_of(bdot(lhs, w1_ref[...]), bdot(lhs[:, :128], w2_ref[...]))
    fwd_rows = u * offs + p * n + q * r + w * z + shift
    bwd_rows = pair_high(bc)
    empty = jnp.zeros((128 - HALF, 128), F32)
    fwd_cols = jnp.concatenate([fwd_rows, empty], axis=0).T
    bwd_cols = jnp.concatenate([bwd_rows, empty], axis=0).T

    lane1 = iota((1, 128), 1)
    low1 = lane1 < H
    eye_a = lane64 == row64
    eye_b = lane64 == row64 + H
    shift_last = shift[HALF - 1:HALF, :]
    x_col = jnp.sum(jnp.where(eye_b, shift_last, 0.0), axis=1, keepdims=True)
    lam_row = jnp.where(low1, 0.0, bwd_rows[HALF - 1:HALF, :])
    zero_col, zero_row = jnp.zeros((H, 1), F32), jnp.zeros((1, 128), F32)
    x_keep = jnp.where(me == 0, x_col, zero_col)
    lam_keep = zero_col
    x_rows, lam_rows = zero_row, jnp.where(me + 1 == DEV - 1, lam_row, zero_row)

    def half(k, row):
        return jnp.where(low1, row, 0.0) if k < HALF else jnp.where(low1, 0.0, row)

    def side_cols(cols, k):
        return jnp.where(lane64 == k % HALF, cols[:H] if k < HALF else cols[H:], 0.0)

    for i in range(DEV - 1):
        k, m = i, i % HALF
        if k % 2 == 0:
            x_row = half(k, jnp.sum(x_col * z_ref[m], axis=0, keepdims=True) + fwd_rows[m:m + 1])
            x_rows = jnp.where(me == k + 1, x_row, x_rows)
        else:
            x_col = jnp.sum(zt_ref[m // 2] * x_row + side_cols(fwd_cols, k), axis=1, keepdims=True)
            x_keep = jnp.where(me == k + 1, x_col, x_keep)
        k = DEV - 2 - i
        m = k % HALF
        if k % 2 == 0:
            lam_col = jnp.sum(z_ref[m] * lam_row + side_cols(bwd_cols, k), axis=1, keepdims=True)
            lam_keep = jnp.where(me + 1 == k, lam_col, lam_keep)
        else:
            lam_row = half(
                k, jnp.sum(lam_col * zt_ref[m // 2], axis=0, keepdims=True) + bwd_rows[m:m + 1]
            )
            lam_rows = jnp.where(me + 1 == k, lam_row, lam_rows)

    def settled(rows, column):
        row = jnp.where(low1, rows, 0.0) + jnp.where(low1, pltpu.roll(rows, H, 1), 0.0)
        return row + jnp.sum(jnp.where(eye_a, column, 0.0), axis=0, keepdims=True)

    x = settled(x_rows, x_keep)
    lam = settled(lam_rows, lam_keep)

    def boundary(k, index):
        row = bnd_ref[k, pl.ds(index % HALF, 1), :]
        return jnp.where(low1, jnp.where(index >= HALF, pltpu.roll(row, H, 1), row), 0.0)

    lam8 = jnp.broadcast_to(lam, (8, 128))
    mixed = jnp.concatenate([lam8 * boundary(k, me) for k in (1, 2, 3)], axis=1)
    carry = (pulled(mixed, wt_ref) + lam8 * boundary(4, me))[0:1]

    row72 = iota((72, 128), 0)
    eye72 = iota((72, 128), 1) == row72
    one = lane1 == H

    def ahead(maps, x):
        col = jnp.sum(jnp.where(eye72, x, 0.0), axis=1, keepdims=True)
        return jnp.where(one, 1.0, jnp.sum(col * maps, axis=0, keepdims=True))

    def back(maps, lam):
        col = jnp.sum(maps[:H] * lam, axis=1, keepdims=True)
        return jnp.where(one, 1.0, jnp.sum(jnp.where(eye_a, col, 0.0), axis=0, keepdims=True))

    starts = [jnp.where(one, 1.0, x)]
    for k in range(3):
        starts.append(ahead(sup_ref[k], starts[-1]))
    ends = [jnp.where(one, 1.0, carry)]
    for k in (3, 2, 1):
        ends.append(back(sup_ref[k], ends[-1]))
    ends = ends[::-1]
    state_rows, carry_rows = [None] * 16, [None] * 16
    for k in range(4):
        value, lam = starts[k], ends[k]
        for j in range(4):
            state_rows[4 * k + j] = value
            carry_rows[4 * k + 3 - j] = lam
            if j < 3:
                value = ahead(aug_ref[4 * k + j], value)
                lam = back(aug_ref[4 * k + 3 - j], lam)

    def gather(items):
        left = jnp.concatenate(items[:8], axis=0)
        right = jnp.concatenate(items[8:], axis=0)
        return jnp.where(iota((8, 128), 1) < H, left, pltpu.roll(right, H, 1))

    def rows(k, step):
        return pk_ref[k, pl.ds(step, PAIRS, stride=RUN), :]

    state, kappa = gather(state_rows), gather(carry_rows)
    for i in range(RUN):
        j = RUN - 1 - i
        n, r, z = narrow_gates(state, w1_ref, w2_ref)
        lam = rows(5, j) + kappa
        lam_ref[pl.ds(j, PAIRS, stride=RUN), :] = lam
        mixed = jnp.concatenate([lam * rows(0, j), lam * rows(1, j), lam * rows(2, j)], axis=1)
        kappa = pulled(mixed, wt_ref) + lam * rows(3, j)
        state = rows(3, i) * state + rows(0, i) * n + rows(1, i) * r + rows(2, i) * z + rows(4, i)
        st_ref[pl.ds(i, PAIRS, stride=RUN), :] = state

    states = st_ref[...].T
    state_ref[:, :128] = states[:H]
    state_ref[:, 128:] = states[H:]
    lams = lam_ref[...].T
    lams = jnp.concatenate([lams[:H], lams[H:]], axis=1)
    adj_ref[...] = lams
    results = fetch([(state_ref, state_hbm), (adj_ref, adj_hbm)], out_sems)

    before = (me + DEV - 1) % DEV
    first = iota((H, T), 1) == 0

    def with_first(a, k):
        col = jnp.sum(jnp.where(eye_a, boundary(k, before), 0.0), axis=1, keepdims=True)
        return jnp.where(first, col, a)

    for copy in copies:
        copy.wait()
    squash, p, q, w = [with_first(tl_ref[k], k) for k in range(4)]
    prev = with_first(pltpu.roll(g_ref[...], 1, 1), 6)
    left = jnp.concatenate([x_ref[...], prev, jnp.ones((8, T), F32)], axis=0)
    right = jnp.concatenate([lams * q, lams * w, lams * squash, lams * p], axis=0)
    sums = dot(left, right, ((1,), (1,)))
    row8 = iota((8, 128), 0)
    biases = jnp.where(
        row8 == 0, sums[128:136, :128], jnp.where(row8 == 1, sums[128:136, 128:], 0.0)
    )
    last = jnp.where(lane64 < H, sums[:64, 128:], sums[64:128, 128:])
    first_half = sums[:PART, :128]
    second_half = jnp.concatenate([sums[PART:128, :128], last, biases, jnp.zeros((8, 128), F32)], axis=0)
    keep_ref[...] = jnp.where(core == 0, first_half, second_half)
    give_ref[...] = jnp.where(core == 0, second_half, first_half)
    for copy in results:
        copy.wait()


def finish_kernel(me_ref, own_ref, other_ref, gin_ref, ghid_ref, gbias_ref, *, scale):
    core = me_ref[0] % 2
    own, other = own_ref[...] * scale, other_ref[...] * scale
    whole = jnp.concatenate(
        [jnp.where(core == 0, own, other), jnp.where(core == 0, other, own)], axis=0
    )
    gin_ref[:, :128] = whole[:64]
    gin_ref[:, 128:] = whole[128:192, :64]
    ghid_ref[:, :128] = whole[64:128]
    ghid_ref[:, 128:] = whole[128:192, 64:]
    gbias_ref[...] = whole[192:194]


def shape(*dims):
    return jax.ShapeDtypeStruct(dims, F32)


def swapped(a):
    return lax.ppermute(a, "tm", [(k, k ^ 1) for k in range(DEV)])


def summed_by_four(a, axis, stride):
    count = lax.axis_size(axis)
    one, two, three_off = [
        lax.ppermute(a, axis, [(k, k ^ (step * stride)) for k in range(count)]) for step in (1, 2, 3)
    ]
    return lax.optimization_barrier((a + one) + (two + three_off))


def per_device(inputs, guess, cotangent, w_input, w_hidden, bias):
    x = jnp.swapaxes(inputs[0], 0, 1)
    g = jnp.swapaxes(guess[0], 0, 1)
    c = jnp.swapaxes(cotangent[0], 0, 1)
    bias2 = bias.reshape(2, 128)
    x, g, c, w_input, w_hidden, bias2 = [
        pltpu.with_memory_space_constraint(a, pltpu.HBM)
        for a in (x, g, c, w_input, w_hidden, bias2)
    ]
    vmem = pl.BlockSpec(memory_space=pltpu.VMEM)
    hbm = pl.BlockSpec(memory_space=pltpu.HBM)
    smem = pl.BlockSpec(memory_space=pltpu.SMEM)
    wide = [pltpu.VMEM((H, T), F32)] * 3
    params = pltpu.CompilerParams(vmem_limit_bytes=VMEM_LIMIT)
    send, *kept = pl.pallas_call(
        blocks_kernel,
        out_shape=(
            shape(HALF, TILE, 128), shape(16, 72, 128), shape(4, 72, 128),
            shape(6, 128, 128), shape(4, H, T),
            jax.ShapeDtypeStruct((256, 512), BF16), jax.ShapeDtypeStruct((128, 256), BF16),
            jax.ShapeDtypeStruct((384, 256), BF16), shape(8, 128),
        ),
        in_specs=[hbm] * 6,
        out_specs=[vmem] * 9,
        scratch_shapes=[
            pltpu.VMEM((PAIRS, H, 128), F32),
            pltpu.VMEM((PAIRS, H, 128), F32),
            pltpu.VMEM((8, 128), F32),
            pltpu.VMEM((528, 256), BF16),
        ] + wide + [
            pltpu.VMEM((H, 192), F32),
            pltpu.VMEM((H, 192), F32),
            pltpu.VMEM((2, 128), F32),
            pltpu.SemaphoreType.DMA((6,)),
        ],
        compiler_params=params,
        name="blocks",
    )(x, g, c, w_input, w_hidden, bias2)
    groups = [[2 * k + core for k in range(HALF)] for core in range(2)]
    received = lax.all_to_all(send, "tm", 0, 0, axis_index_groups=groups)
    other = swapped(received)
    me = lax.axis_index("tm").astype(jnp.int32).reshape(1)
    states, adjoint, part, give = pl.pallas_call(
        apply_kernel,
        out_shape=(shape(H, T), shape(H, T), shape(PART, 128), shape(PART, 128)),
        in_specs=[smem] + [vmem] * 10 + [hbm] * 2,
        out_specs=[hbm] * 2 + [vmem] * 2,
        scratch_shapes=[
            pltpu.VMEM((HALF * H + 16, 256), BF16),
            pltpu.VMEM((HALF, H, 128), F32),
            pltpu.VMEM((HALF // 2, H, 128), F32),
            pltpu.VMEM((3, DEV, 128), F32),
            pltpu.VMEM((7, HALF, 128), F32),
            pltpu.VMEM((128, 128), F32),
            pltpu.VMEM((128, 128), F32),
        ] + wide[:2] + [pltpu.SemaphoreType.DMA((2,))] + wide[:2] + [pltpu.SemaphoreType.DMA((2,))],
        compiler_params=params,
        name="apply",
    )(me, received, other, *kept, x, g)
    part = part + swapped(give)
    for axis, stride in (("seq", 1), ("tm", 8), ("tm", 2)):
        part = summed_by_four(part, axis, stride)
    scale = 1.0 / math.sqrt(lax.axis_size("seq") * lax.axis_size("tm") * T)
    grad_input, grad_hidden, grad_bias = pl.pallas_call(
        functools.partial(finish_kernel, scale=scale),
        out_shape=(shape(H, 192), shape(H, 192), shape(2, 128)),
        in_specs=[smem, vmem, vmem],
        out_specs=[vmem] * 3,
        compiler_params=params,
        name="finish",
    )(me, part, swapped(part))
    grad_bias = grad_bias.reshape(256)
    return (
        jnp.swapaxes(states, 0, 1)[None], jnp.swapaxes(adjoint, 0, 1)[None],
        grad_input, grad_hidden, grad_bias,
    )


def solution(mesh):
    return jax.shard_map(
        per_device,
        mesh=mesh,
        in_specs=(P("seq", "tm", None), P("seq", "tm", None), P("seq", "tm", None), P(), P(), P()),
        out_specs=(P("seq", "tm", None), P("seq", "tm", None), P(), P(), P()),
        check_vma=False,
    )
```

```python
import functools
import math

import jax
import jax.numpy as jnp
from jax import lax
from jax.experimental import pallas as pl
from jax.experimental.pallas import tpu as pltpu
from jax.sharding import PartitionSpec as P

F32 = jnp.float32
BF16 = jnp.bfloat16
HIGHEST = lax.Precision.HIGHEST
H = 64
T = 256
RUN = 16
PAIRS = 8
DEV = 32
HALF = DEV // 2
TILE = 40
GROUP = 2
PART = 104
VMEM_LIMIT = 48 * 1024 * 1024


def dot(a, b, dims=((1,), (0,))):
    return lax.dot_general(a, b, (dims, ((), ())), precision=HIGHEST, preferred_element_type=F32)


def bdot(a, b):
    return jnp.dot(a, b, preferred_element_type=F32)


def iota(shape, axis):
    return lax.broadcasted_iota(jnp.int32, shape, axis)


def split(a):
    high = a.astype(BF16)
    return high, (a - high.astype(F32)).astype(BF16)


def sigmoid(a):
    return 1.0 / (1.0 + jnp.exp(-a))


def doubled(block):
    zero = jnp.zeros_like(block)
    return jnp.concatenate(
        [jnp.concatenate([block, zero], axis=1), jnp.concatenate([zero, block], axis=1)], axis=0
    )


def side_weights(wh):
    n, r, z = [split(doubled(wh[:, k:k + H])) for k in (128, 0, 64)]
    zero = jnp.zeros((128, 128), BF16)
    top = jnp.concatenate([n[0], r[0], z[0], n[1]], axis=1)
    bottom = jnp.concatenate([n[0], r[0], z[0], zero], axis=1)
    return jnp.concatenate([top, bottom], axis=0), jnp.concatenate([r[1], z[1]], axis=1)


def halves(value):
    return jnp.concatenate(split(value), axis=1)


def gates_of(first, second):
    return (
        first[:, :128] + first[:, 384:], first[:, 128:256] + second[:, :128],
        first[:, 256:384] + second[:, 128:],
    )


def backward_weights(wh):
    tall = jnp.concatenate([doubled(wh[:, k:k + H].T) for k in (128, 0, 64)], axis=0)
    return jnp.concatenate(split(tall), axis=1)


def stacked(value):
    high = value.astype(BF16).astype(F32)
    return jnp.concatenate([high, value - high], axis=0).astype(BF16)


def narrow_gates(value, w1_ref, w2_ref):
    rows = value.shape[0]
    weights = jnp.concatenate([w1_ref[:128, :], w2_ref[...]], axis=1)
    out = bdot(stacked(value), weights)
    high, low = out[:rows], out[rows:]
    n = high[:, :128] + high[:, 384:512] + low[:, :128]
    r = high[:, 128:256] + high[:, 512:640] + low[:, 128:256]
    z = high[:, 256:384] + high[:, 640:] + low[:, 256:384]
    return n, r, z


def pulled(mixed, wt_ref):
    rows = mixed.shape[0]
    out = bdot(stacked(mixed), wt_ref[...])
    return out[:rows, :128] + out[rows:, :128] + out[:rows, 128:]


def to_row(column, offset):
    hit = iota((H, 128), 1) == iota((H, 128), 0) + offset
    return jnp.sum(jnp.where(hit, column, 0.0), axis=0, keepdims=True)


def gate_terms(gi_r, gi_z, gi_n, gh_r, gh_z, gh_n, bias_h, prev):
    reset = sigmoid(gi_r + gh_r)
    update = sigmoid(gi_z + gh_z)
    keep = sigmoid(-(gi_z + gh_z))
    hsum = gh_n + bias_h
    cand = jnp.tanh(gi_n + reset * hsum)
    squash = keep * (1.0 - cand * cand)
    p = squash * reset
    q = squash * hsum * reset * (1.0 - reset)
    w = (prev - cand) * update * keep
    shift = keep * cand - p * gh_n - q * gh_r - w * gh_z
    return squash, p, q, w, update, shift


def packed(a):
    return jnp.concatenate([a[:, :128], a[:, 128:]], axis=0).T


def combine(earlier, later):
    row, lane = iota((72, 128), 0), iota((72, 128), 1)
    out = bdot(stacked(earlier[:, :H]), jnp.concatenate(split(later[:H, :]), axis=1))
    product = out[:72, :128] + out[72:, :128] + out[:72, 128:]
    return (
        product
        + jnp.where((lane == H) & (row < H), earlier, 0.0)
        + jnp.where((row == H) & (lane < H), later, 0.0)
    )


def fetch(pairs, sems):
    copies = [pltpu.make_async_copy(a, b, sems.at[k]) for k, (a, b) in enumerate(pairs)]
    for copy in copies:
        copy.start()
    return copies


def blocks_kernel(
    x_hbm, g_hbm, c_hbm, wi_hbm, wh_hbm, bias_hbm,
    send_ref, aug_ref, sup_ref, pk_ref, tl_ref, w1_ref, w2_ref, wt_ref, hb_ref,
    y_ref, z_ref, b_ref, lhs_ref,
    x_ref, g_ref, c_ref, wi_ref, wh_ref, bias_ref, sems,
):
    for copy in fetch(
        [(wh_hbm, wh_ref), (g_hbm, g_ref), (wi_hbm, wi_ref), (x_hbm, x_ref), (bias_hbm, bias_ref),
         (c_hbm, c_ref)], sems,
    ):
        copy.wait()
    wh = wh_ref[...]
    w1_ref[...], w2_ref[...] = side_weights(wh)
    wt_ref[...] = backward_weights(wh)
    hb = jnp.broadcast_to(bias_ref[1:2, :], (8, 128))
    hb_ref[...] = jnp.where(iota((8, 128), 1) < H, pltpu.roll(hb, H, 1), hb)
    guess = g_ref[...]
    prev = pltpu.roll(guess, 1, 1)
    gi = dot(wi_ref[...], x_ref[...], ((0,), (0,)))
    gh = dot(wh, prev, ((0,), (0,)))
    bias0 = jnp.broadcast_to(bias_ref[0:1, :], (128, 128)).T
    bias1 = jnp.broadcast_to(bias_ref[1:2, :], (128, 128)).T
    bias0 = jnp.concatenate([bias0, bias0], axis=1)
    bias1 = jnp.concatenate([bias1, bias1], axis=1)
    gi_r = gi[:64] + bias0[:64]
    gi_z = gi[64:128] + bias0[64:]
    gi_n = gi[128:] + bias1[:64]
    squash, p, q, w, u, shift = gate_terms(
        gi_r, gi_z, gi_n, gh[:64], gh[64:128], gh[128:], bias1[64:], prev
    )
    tl_ref[0], tl_ref[1], tl_ref[2], tl_ref[3] = squash, p, q, w
    first = iota((H, T), 1) == 0
    pk_ref[0] = packed(jnp.where(first, 0.0, p))
    pk_ref[1] = packed(jnp.where(first, 0.0, q))
    pk_ref[2] = packed(jnp.where(first, 0.0, w))
    pk_ref[3] = packed(jnp.where(first, 1.0, u))
    pk_ref[4] = packed(jnp.where(first, 0.0, shift))
    pk_ref[5] = packed(c_ref[...])

    lane64 = iota((H, 128), 1)
    low64 = lane64 < H
    eye2 = jnp.where((lane64 == iota((H, 128), 0)) | (lane64 == iota((H, 128), 0) + H), 1.0, 0.0)
    wn2 = jnp.concatenate([wh[:, 128:192], wh[:, 128:192]], axis=1)
    wr2 = jnp.concatenate([wh[:, :64], wh[:, :64]], axis=1)
    wz2 = jnp.concatenate([wh[:, 64:128], wh[:, 64:128]], axis=1)

    def rows(k, step):
        return pk_ref[k, pl.ds(step, PAIRS, stride=RUN), :]

    def put(c, value, cot):
        y_ref[c] = value
        lhs_ref[c * H:(c + 1) * H, :] = halves(value)
        return value * cot

    def put_b(value):
        b_ref[...] = value
        lhs_ref[512:528, :] = halves(jnp.concatenate([value, jnp.zeros_like(value)], axis=0))

    p0, q0, w0, u0, s0, c0 = [rows(k, 0) for k in range(6)]
    for c in range(PAIRS):
        value = (
            p0[c:c + 1] * wn2 + q0[c:c + 1] * wr2 + w0[c:c + 1] * wz2 + u0[c:c + 1] * eye2
        )
        z_ref[c] = put(c, value, c0[c:c + 1])
    put_b(s0)

    def step(l, carry):
        p1, q1, w1, u1, s1, c1 = [rows(k, l) for k in range(6)]
        for c in range(PAIRS):
            if c % GROUP == 0:
                lhs = lhs_ref[c * H:(c + GROUP) * H, :]
                first, second = bdot(lhs, w1_ref[...]), bdot(lhs[:, :128], w2_ref[...])
            part = slice((c % GROUP) * H, (c % GROUP + 1) * H)
            n, r, z = gates_of(first[part], second[part])
            value = (
                u1[c:c + 1] * y_ref[c] + p1[c:c + 1] * n + q1[c:c + 1] * r + w1[c:c + 1] * z
            )
            z_ref[c] += put(c, value, c1[c:c + 1])
        lhs = lhs_ref[512:528, :]
        first, second = bdot(lhs, w1_ref[...]), bdot(lhs[:, :128], w2_ref[...])
        n, r, z = gates_of(first[:8], second[:8])
        put_b(u1 * b_ref[...] + p1 * n + q1 * r + w1 * z + s1)
        return carry

    lax.fori_loop(1, RUN, step, 0, unroll=True)

    low8 = iota((8, 128), 1) < H
    top8 = iota((8, 128), 0) == 0
    bs = b_ref[...]
    for c in range(PAIRS):
        y = y_ref[c]
        z = z_ref[c]
        offs = jnp.broadcast_to(bs[c:c + 1], (8, 128))
        for part in range(2):
            if part:
                y, z, offs = pltpu.roll(y, H, 1), pltpu.roll(z, H, 1), pltpu.roll(offs, H, 1)
            col = jnp.sum(jnp.where(low64, z, 0.0), axis=1, keepdims=True)
            n = c + part * PAIRS
            aug_ref[n, 0:64, :] = jnp.where(low64, y, jnp.where(lane64 == H, col, 0.0))
            aug_ref[n, 64:72, :] = jnp.where(low8 & top8, offs, 0.0)
    sups = []
    for k in range(4):
        left = combine(aug_ref[4 * k], aug_ref[4 * k + 1])
        right = combine(aug_ref[4 * k + 2], aug_ref[4 * k + 3])
        sups.append(combine(left, right))
        sup_ref[k] = sups[-1]
    total = combine(combine(sups[0], sups[1]), combine(sups[2], sups[3]))

    low32 = iota((32, 128), 1) < H
    body = jnp.where(low32, total[:32], pltpu.roll(total[32:64], H, 1))
    col = jnp.sum(jnp.where(lane64 == H, total[:64], 0.0), axis=1, keepdims=True)
    row_bc = jnp.where(low8[:1], total[64:65], 0.0) + to_row(col, H)
    last = jnp.sum(jnp.where(lane64 == 127, guess[:, 128:], 0.0), axis=1, keepdims=True)

    def head(a):
        return jnp.sum(jnp.where(lane64 == 0, a[:, :128], 0.0), axis=1, keepdims=True)

    row_gr = to_row(last, 0) + to_row(head(gi_r), H)
    row_zn = to_row(head(gi_z), 0) + to_row(head(gi_n), H)
    row8 = iota((8, 128), 0)
    tail = jnp.where(row8 == 0, row_bc, jnp.where(row8 == 1, row_gr, jnp.where(row8 == 2, row_zn, 0.0)))
    for k in range(HALF):
        send_ref[k, 0:32, :] = body
        send_ref[k, 32:40, :] = tail


def apply_kernel(
    me_ref, own_ref, other_ref, aug_ref, sup_ref, pk_ref, tl_ref, w1_ref, w2_ref, wt_ref, hb_ref,
    x_hbm, g_hbm,
    state_hbm, adj_hbm, keep_ref, give_ref,
    lhs_ref, z_ref, zt_ref, row_ref, bnd_ref, st_ref, lam_ref, x_ref, g_ref, sems,
    state_ref, adj_ref, out_sems,
):
    copies = fetch([(g_hbm, g_ref), (x_hbm, x_ref)], sems)
    me = me_ref[0]
    core = me % 2
    for k in range(3):
        row_ref[k, pl.ds(core, HALF, stride=2), :] = own_ref[:, 32 + k, :]
        row_ref[k, pl.ds(1 - core, HALF, stride=2), :] = other_ref[:, 32 + k, :]
    bc, gr, zn = row_ref[0], row_ref[1], row_ref[2]
    low16 = iota((HALF, 128), 1) < H

    def pair_low(a):
        return jnp.where(low16, a[:HALF], pltpu.roll(a[HALF:], H, 1))

    def pair_high(a):
        return jnp.where(low16, pltpu.roll(a[:HALF], H, 1), a[HALF:])

    gr_next = pltpu.roll(gr, DEV - 1, 0)
    zn_next = pltpu.roll(zn, DEV - 1, 0)
    prev = jnp.where((iota((HALF, 128), 0) == HALF - 1) & ~low16, 0.0, pair_low(gr))
    n, r, z = narrow_gates(prev, w1_ref, w2_ref)
    terms = gate_terms(
        pair_high(gr_next), pair_low(zn_next), pair_high(zn_next), r, z, n, hb_ref[0:1, :], prev
    )
    for k in range(6):
        bnd_ref[k] = terms[k]
    bnd_ref[6] = prev
    squash, p, q, w, u, shift = terms

    lane64 = iota((H, 128), 1)
    row64 = iota((H, 128), 0)
    low32 = iota((32, 128), 1) < H
    for ref, side in ((own_ref, core), (other_ref, 1 - core)):
        for k in range(HALF // 2):
            a, b = ref[k, 0:32, :], ref[k + HALF // 2, 0:32, :]
            top = jnp.where(low32, a, pltpu.roll(b, H, 1))
            bottom = jnp.where(low32, pltpu.roll(a, H, 1), b)
            value = jnp.concatenate([top, bottom], axis=0)
            z_ref[2 * k + side] = value
            start = pl.multiple_of((2 * k + side) * H, H)
            lhs_ref[pl.ds(start, H), :] = halves(value)
    offs = pair_low(bc)
    lhs_ref[HALF * H:, :] = halves(offs)
    for k in range(HALF):
        if k % GROUP == 0:
            lhs = lhs_ref[k * H:(k + GROUP) * H, :]
            first, second = bdot(lhs, w1_ref[...]), bdot(lhs[:, :128], w2_ref[...])
        part = slice((k % GROUP) * H, (k % GROUP + 1) * H)
        n, r, z = gates_of(first[part], second[part])
        value = u[k:k + 1] * z_ref[k] + p[k:k + 1] * n + q[k:k + 1] * r + w[k:k + 1] * z
        z_ref[k] = value
        if k % 2:
            zt_ref[k // 2] = jnp.concatenate([value, pltpu.roll(value, H, 1)], axis=0).T[:H]
    lhs = lhs_ref[HALF * H:, :]
    n, r, z = gates_of(bdot(lhs, w1_ref[...]), bdot(lhs[:, :128], w2_ref[...]))
    fwd_rows = u * offs + p * n + q * r + w * z + shift
    bwd_rows = pair_high(bc)
    empty = jnp.zeros((128 - HALF, 128), F32)
    fwd_cols = jnp.concatenate([fwd_rows, empty], axis=0).T
    bwd_cols = jnp.concatenate([bwd_rows, empty], axis=0).T

    lane1 = iota((1, 128), 1)
    low1 = lane1 < H
    eye_a = lane64 == row64
    eye_b = lane64 == row64 + H
    shift_last = shift[HALF - 1:HALF, :]
    x_col = jnp.sum(jnp.where(eye_b, shift_last, 0.0), axis=1, keepdims=True)
    lam_row = jnp.where(low1, 0.0, bwd_rows[HALF - 1:HALF, :])
    zero_col, zero_row = jnp.zeros((H, 1), F32), jnp.zeros((1, 128), F32)
    x_keep = jnp.where(me == 0, x_col, zero_col)
    lam_keep = zero_col
    x_rows, lam_rows = zero_row, jnp.where(me + 1 == DEV - 1, lam_row, zero_row)

    def half(k, row):
        return jnp.where(low1, row, 0.0) if k < HALF else jnp.where(low1, 0.0, row)

    def side_cols(cols, k):
        return jnp.where(lane64 == k % HALF, cols[:H] if k < HALF else cols[H:], 0.0)

    for i in range(DEV - 1):
        k, m = i, i % HALF
        if k % 2 == 0:
            x_row = half(k, jnp.sum(x_col * z_ref[m], axis=0, keepdims=True) + fwd_rows[m:m + 1])
            x_rows = jnp.where(me == k + 1, x_row, x_rows)
        else:
            x_col = jnp.sum(zt_ref[m // 2] * x_row + side_cols(fwd_cols, k), axis=1, keepdims=True)
            x_keep = jnp.where(me == k + 1, x_col, x_keep)
        k = DEV - 2 - i
        m = k % HALF
        if k % 2 == 0:
            lam_col = jnp.sum(z_ref[m] * lam_row + side_cols(bwd_cols, k), axis=1, keepdims=True)
            lam_keep = jnp.where(me + 1 == k, lam_col, lam_keep)
        else:
            lam_row = half(
                k, jnp.sum(lam_col * zt_ref[m // 2], axis=0, keepdims=True) + bwd_rows[m:m + 1]
            )
            lam_rows = jnp.where(me + 1 == k, lam_row, lam_rows)

    def settled(rows, column):
        row = jnp.where(low1, rows, 0.0) + jnp.where(low1, pltpu.roll(rows, H, 1), 0.0)
        return row + jnp.sum(jnp.where(eye_a, column, 0.0), axis=0, keepdims=True)

    x = settled(x_rows, x_keep)
    lam = settled(lam_rows, lam_keep)

    def boundary(k, index):
        row = bnd_ref[k, pl.ds(index % HALF, 1), :]
        return jnp.where(low1, jnp.where(index >= HALF, pltpu.roll(row, H, 1), row), 0.0)

    lam8 = jnp.broadcast_to(lam, (8, 128))
    mixed = jnp.concatenate([lam8 * boundary(k, me) for k in (1, 2, 3)], axis=1)
    carry = (pulled(mixed, wt_ref) + lam8 * boundary(4, me))[0:1]

    row72 = iota((72, 128), 0)
    eye72 = iota((72, 128), 1) == row72
    one = lane1 == H

    def ahead(maps, x):
        col = jnp.sum(jnp.where(eye72, x, 0.0), axis=1, keepdims=True)
        return jnp.where(one, 1.0, jnp.sum(col * maps, axis=0, keepdims=True))

    def back(maps, lam):
        col = jnp.sum(maps[:H] * lam, axis=1, keepdims=True)
        return jnp.where(one, 1.0, jnp.sum(jnp.where(eye_a, col, 0.0), axis=0, keepdims=True))

    starts = [jnp.where(one, 1.0, x)]
    for k in range(3):
        starts.append(ahead(sup_ref[k], starts[-1]))
    ends = [jnp.where(one, 1.0, carry)]
    for k in (3, 2, 1):
        ends.append(back(sup_ref[k], ends[-1]))
    ends = ends[::-1]
    state_rows, carry_rows = [None] * 16, [None] * 16
    for k in range(4):
        value, lam = starts[k], ends[k]
        for j in range(4):
            state_rows[4 * k + j] = value
            carry_rows[4 * k + 3 - j] = lam
            if j < 3:
                value = ahead(aug_ref[4 * k + j], value)
                lam = back(aug_ref[4 * k + 3 - j], lam)

    def gather(items):
        left = jnp.concatenate(items[:8], axis=0)
        right = jnp.concatenate(items[8:], axis=0)
        return jnp.where(iota((8, 128), 1) < H, left, pltpu.roll(right, H, 1))

    def rows(k, step):
        return pk_ref[k, pl.ds(step, PAIRS, stride=RUN), :]

    state, kappa = gather(state_rows), gather(carry_rows)
    for i in range(RUN):
        j = RUN - 1 - i
        n, r, z = narrow_gates(state, w1_ref, w2_ref)
        lam = rows(5, j) + kappa
        lam_ref[pl.ds(j, PAIRS, stride=RUN), :] = lam
        mixed = jnp.concatenate([lam * rows(0, j), lam * rows(1, j), lam * rows(2, j)], axis=1)
        kappa = pulled(mixed, wt_ref) + lam * rows(3, j)
        state = rows(3, i) * state + rows(0, i) * n + rows(1, i) * r + rows(2, i) * z + rows(4, i)
        st_ref[pl.ds(i, PAIRS, stride=RUN), :] = state

    states = st_ref[...].T
    state_ref[:, :128] = states[:H]
    state_ref[:, 128:] = states[H:]
    lams = lam_ref[...].T
    lams = jnp.concatenate([lams[:H], lams[H:]], axis=1)
    adj_ref[...] = lams
    results = fetch([(state_ref, state_hbm), (adj_ref, adj_hbm)], out_sems)

    before = (me + DEV - 1) % DEV
    first = iota((H, T), 1) == 0

    def with_first(a, k):
        col = jnp.sum(jnp.where(eye_a, boundary(k, before), 0.0), axis=1, keepdims=True)
        return jnp.where(first, col, a)

    for copy in copies:
        copy.wait()
    squash, p, q, w = [with_first(tl_ref[k], k) for k in range(4)]
    prev = with_first(pltpu.roll(g_ref[...], 1, 1), 6)
    left = jnp.concatenate([x_ref[...], prev, jnp.ones((8, T), F32)], axis=0)
    right = jnp.concatenate([lams * q, lams * w, lams * squash, lams * p], axis=0)
    sums = dot(left, right, ((1,), (1,)))
    row8 = iota((8, 128), 0)
    biases = jnp.where(
        row8 == 0, sums[128:136, :128], jnp.where(row8 == 1, sums[128:136, 128:], 0.0)
    )
    last = jnp.where(lane64 < H, sums[:64, 128:], sums[64:128, 128:])
    first_half = sums[:PART, :128]
    second_half = jnp.concatenate([sums[PART:128, :128], last, biases, jnp.zeros((8, 128), F32)], axis=0)
    keep_ref[...] = jnp.where(core == 0, first_half, second_half)
    give_ref[...] = jnp.where(core == 0, second_half, first_half)
    for copy in results:
        copy.wait()


def finish_kernel(me_ref, own_ref, other_ref, gin_ref, ghid_ref, gbias_ref, *, scale):
    core = me_ref[0] % 2
    own, other = own_ref[...] * scale, other_ref[...] * scale
    whole = jnp.concatenate(
        [jnp.where(core == 0, own, other), jnp.where(core == 0, other, own)], axis=0
    )
    gin_ref[:, :128] = whole[:64]
    gin_ref[:, 128:] = whole[128:192, :64]
    ghid_ref[:, :128] = whole[64:128]
    ghid_ref[:, 128:] = whole[128:192, 64:]
    gbias_ref[...] = whole[192:194]


def shape(*dims):
    return jax.ShapeDtypeStruct(dims, F32)


def swapped(a):
    return lax.ppermute(a, "tm", [(k, k ^ 1) for k in range(DEV)])


def summed_by_four(a, axis, stride):
    count = lax.axis_size(axis)
    first, second, third = [
        lax.ppermute(a, axis, [(k, k ^ (step * stride)) for k in range(count)]) for step in (1, 2, 3)
    ]
    return lax.optimization_barrier((first + third) + (a + second))


def per_device(inputs, guess, cotangent, w_input, w_hidden, bias):
    x = jnp.swapaxes(inputs[0], 0, 1)
    g = jnp.swapaxes(guess[0], 0, 1)
    c = jnp.swapaxes(cotangent[0], 0, 1)
    bias2 = bias.reshape(2, 128)
    x, g, c, w_input, w_hidden, bias2 = [
        pltpu.with_memory_space_constraint(a, pltpu.HBM)
        for a in (x, g, c, w_input, w_hidden, bias2)
    ]
    vmem = pl.BlockSpec(memory_space=pltpu.VMEM)
    hbm = pl.BlockSpec(memory_space=pltpu.HBM)
    smem = pl.BlockSpec(memory_space=pltpu.SMEM)
    wide = [pltpu.VMEM((H, T), F32)] * 3
    params = pltpu.CompilerParams(vmem_limit_bytes=VMEM_LIMIT)
    send, *kept = pl.pallas_call(
        blocks_kernel,
        out_shape=(
            shape(HALF, TILE, 128), shape(16, 72, 128), shape(4, 72, 128),
            shape(6, 128, 128), shape(4, H, T),
            jax.ShapeDtypeStruct((256, 512), BF16), jax.ShapeDtypeStruct((128, 256), BF16),
            jax.ShapeDtypeStruct((384, 256), BF16), shape(8, 128),
        ),
        in_specs=[hbm] * 6,
        out_specs=[vmem] * 9,
        scratch_shapes=[
            pltpu.VMEM((PAIRS, H, 128), F32),
            pltpu.VMEM((PAIRS, H, 128), F32),
            pltpu.VMEM((8, 128), F32),
            pltpu.VMEM((528, 256), BF16),
        ] + wide + [
            pltpu.VMEM((H, 192), F32),
            pltpu.VMEM((H, 192), F32),
            pltpu.VMEM((2, 128), F32),
            pltpu.SemaphoreType.DMA((6,)),
        ],
        compiler_params=params,
        name="blocks",
    )(x, g, c, w_input, w_hidden, bias2)
    groups = [[2 * k + core for k in range(HALF)] for core in range(2)]
    received = lax.all_to_all(send, "tm", 0, 0, axis_index_groups=groups)
    other = swapped(received)
    me = lax.axis_index("tm").astype(jnp.int32).reshape(1)
    states, adjoint, part, give = pl.pallas_call(
        apply_kernel,
        out_shape=(shape(H, T), shape(H, T), shape(PART, 128), shape(PART, 128)),
        in_specs=[smem] + [vmem] * 10 + [hbm] * 2,
        out_specs=[hbm] * 2 + [vmem] * 2,
        scratch_shapes=[
            pltpu.VMEM((HALF * H + 16, 256), BF16),
            pltpu.VMEM((HALF, H, 128), F32),
            pltpu.VMEM((HALF // 2, H, 128), F32),
            pltpu.VMEM((3, DEV, 128), F32),
            pltpu.VMEM((7, HALF, 128), F32),
            pltpu.VMEM((128, 128), F32),
            pltpu.VMEM((128, 128), F32),
        ] + wide[:2] + [pltpu.SemaphoreType.DMA((2,))] + wide[:2] + [pltpu.SemaphoreType.DMA((2,))],
        compiler_params=params,
        name="apply",
    )(me, received, other, *kept, x, g)
    part = part + swapped(give)
    for axis, stride in (("seq", 1), ("tm", 8), ("tm", 2)):
        part = summed_by_four(part, axis, stride)
    scale = 1.0 / math.sqrt(lax.axis_size("seq") * lax.axis_size("tm") * T)
    grad_input, grad_hidden, grad_bias = pl.pallas_call(
        functools.partial(finish_kernel, scale=scale),
        out_shape=(shape(H, 192), shape(H, 192), shape(2, 128)),
        in_specs=[smem, vmem, vmem],
        out_specs=[vmem] * 3,
        compiler_params=params,
        name="finish",
    )(me, part, swapped(part))
    grad_bias = grad_bias.reshape(256)
    return (
        jnp.swapaxes(states, 0, 1)[None], jnp.swapaxes(adjoint, 0, 1)[None],
        grad_input, grad_hidden, grad_bias,
    )


def solution(mesh):
    return jax.shard_map(
        per_device,
        mesh=mesh,
        in_specs=(P("seq", "tm", None), P("seq", "tm", None), P("seq", "tm", None), P(), P(), P()),
        out_specs=(P("seq", "tm", None), P("seq", "tm", None), P(), P(), P()),
        check_vma=False,
    )
```

```python
import functools
import math

import jax
import jax.numpy as jnp
from jax import lax
from jax.experimental import pallas as pl
from jax.experimental.pallas import tpu as pltpu
from jax.sharding import PartitionSpec as P

F32 = jnp.float32
BF16 = jnp.bfloat16
HIGHEST = lax.Precision.HIGHEST
H = 64
T = 256
RUN = 16
PAIRS = 8
DEV = 32
HALF = DEV // 2
TILE = 40
GROUP = 2
PART = 104
VMEM_LIMIT = 48 * 1024 * 1024


def dot(a, b, dims=((1,), (0,))):
    return lax.dot_general(a, b, (dims, ((), ())), precision=HIGHEST, preferred_element_type=F32)


def bdot(a, b):
    return jnp.dot(a, b, preferred_element_type=F32)


def gate_dot(weights, columns):
    tall = stacked(weights.T)
    wide = jnp.concatenate(split(columns), axis=1)
    out = bdot(tall, wide)
    return out[:192, :T] + out[192:, :T] + out[:192, T:]


def iota(shape, axis):
    return lax.broadcasted_iota(jnp.int32, shape, axis)


def split(a):
    high = a.astype(BF16)
    return high, (a - high.astype(F32)).astype(BF16)


def sigmoid(a):
    return 1.0 / (1.0 + jnp.exp(-a))


def doubled(block):
    zero = jnp.zeros_like(block)
    return jnp.concatenate(
        [jnp.concatenate([block, zero], axis=1), jnp.concatenate([zero, block], axis=1)], axis=0
    )


def side_weights(wh):
    n, r, z = [split(doubled(wh[:, k:k + H])) for k in (128, 0, 64)]
    zero = jnp.zeros((128, 128), BF16)
    top = jnp.concatenate([n[0], r[0], z[0], n[1]], axis=1)
    bottom = jnp.concatenate([n[0], r[0], z[0], zero], axis=1)
    return jnp.concatenate([top, bottom], axis=0), jnp.concatenate([r[1], z[1]], axis=1)


def halves(value):
    return jnp.concatenate(split(value), axis=1)


def gates_of(first, second):
    return (
        first[:, :128] + first[:, 384:], first[:, 128:256] + second[:, :128],
        first[:, 256:384] + second[:, 128:],
    )


def backward_weights(wh):
    tall = jnp.concatenate([doubled(wh[:, k:k + H].T) for k in (128, 0, 64)], axis=0)
    return jnp.concatenate(split(tall), axis=1)


def stacked(value):
    high = value.astype(BF16).astype(F32)
    return jnp.concatenate([high, value - high], axis=0).astype(BF16)


def narrow_gates(value, w1_ref, w2_ref):
    rows = value.shape[0]
    weights = jnp.concatenate([w1_ref[:128, :], w2_ref[...]], axis=1)
    out = bdot(stacked(value), weights)
    high, low = out[:rows], out[rows:]
    n = high[:, :128] + high[:, 384:512] + low[:, :128]
    r = high[:, 128:256] + high[:, 512:640] + low[:, 128:256]
    z = high[:, 256:384] + high[:, 640:] + low[:, 256:384]
    return n, r, z


def pulled(mixed, wt_ref):
    rows = mixed.shape[0]
    out = bdot(stacked(mixed), wt_ref[...])
    return out[:rows, :128] + out[rows:, :128] + out[:rows, 128:]


def to_row(column, offset):
    hit = iota((H, 128), 1) == iota((H, 128), 0) + offset
    return jnp.sum(jnp.where(hit, column, 0.0), axis=0, keepdims=True)


def gate_terms(gi_r, gi_z, gi_n, gh_r, gh_z, gh_n, bias_h, prev):
    reset = sigmoid(gi_r + gh_r)
    update = sigmoid(gi_z + gh_z)
    keep = sigmoid(-(gi_z + gh_z))
    hsum = gh_n + bias_h
    cand = jnp.tanh(gi_n + reset * hsum)
    squash = keep * (1.0 - cand * cand)
    p = squash * reset
    q = squash * hsum * reset * (1.0 - reset)
    w = (prev - cand) * update * keep
    shift = keep * cand - p * gh_n - q * gh_r - w * gh_z
    return squash, p, q, w, update, shift


def packed(a):
    return jnp.concatenate([a[:, :128], a[:, 128:]], axis=0).T


def combine(earlier, later):
    row, lane = iota((72, 128), 0), iota((72, 128), 1)
    out = bdot(stacked(earlier[:, :H]), jnp.concatenate(split(later[:H, :]), axis=1))
    product = out[:72, :128] + out[72:, :128] + out[:72, 128:]
    return (
        product
        + jnp.where((lane == H) & (row < H), earlier, 0.0)
        + jnp.where((row == H) & (lane < H), later, 0.0)
    )


def fetch(pairs, sems):
    copies = [pltpu.make_async_copy(a, b, sems.at[k]) for k, (a, b) in enumerate(pairs)]
    for copy in copies:
        copy.start()
    return copies


def blocks_kernel(
    x_hbm, g_hbm, c_hbm, wi_hbm, wh_hbm, bias_hbm,
    send_ref, aug_ref, sup_ref, pk_ref, tl_ref, w1_ref, w2_ref, wt_ref, hb_ref,
    y_ref, z_ref, b_ref, lhs_ref,
    x_ref, g_ref, c_ref, wi_ref, wh_ref, bias_ref, sems,
):
    for copy in fetch(
        [(wh_hbm, wh_ref), (g_hbm, g_ref), (wi_hbm, wi_ref), (x_hbm, x_ref), (bias_hbm, bias_ref),
         (c_hbm, c_ref)], sems,
    ):
        copy.wait()
    wh = wh_ref[...]
    w1_ref[...], w2_ref[...] = side_weights(wh)
    wt_ref[...] = backward_weights(wh)
    hb = jnp.broadcast_to(bias_ref[1:2, :], (8, 128))
    hb_ref[...] = jnp.where(iota((8, 128), 1) < H, pltpu.roll(hb, H, 1), hb)
    guess = g_ref[...]
    prev = pltpu.roll(guess, 1, 1)
    gi = gate_dot(wi_ref[...], x_ref[...])
    gh = gate_dot(wh, prev)
    bias0 = jnp.broadcast_to(bias_ref[0:1, :], (128, 128)).T
    bias1 = jnp.broadcast_to(bias_ref[1:2, :], (128, 128)).T
    bias0 = jnp.concatenate([bias0, bias0], axis=1)
    bias1 = jnp.concatenate([bias1, bias1], axis=1)
    gi_r = gi[:64] + bias0[:64]
    gi_z = gi[64:128] + bias0[64:]
    gi_n = gi[128:] + bias1[:64]
    squash, p, q, w, u, shift = gate_terms(
        gi_r, gi_z, gi_n, gh[:64], gh[64:128], gh[128:], bias1[64:], prev
    )
    tl_ref[0], tl_ref[1], tl_ref[2], tl_ref[3] = squash, p, q, w
    first = iota((H, T), 1) == 0
    pk_ref[0] = packed(jnp.where(first, 0.0, p))
    pk_ref[1] = packed(jnp.where(first, 0.0, q))
    pk_ref[2] = packed(jnp.where(first, 0.0, w))
    pk_ref[3] = packed(jnp.where(first, 1.0, u))
    pk_ref[4] = packed(jnp.where(first, 0.0, shift))
    pk_ref[5] = packed(c_ref[...])

    lane64 = iota((H, 128), 1)
    low64 = lane64 < H
    eye2 = jnp.where((lane64 == iota((H, 128), 0)) | (lane64 == iota((H, 128), 0) + H), 1.0, 0.0)
    wn2 = jnp.concatenate([wh[:, 128:192], wh[:, 128:192]], axis=1)
    wr2 = jnp.concatenate([wh[:, :64], wh[:, :64]], axis=1)
    wz2 = jnp.concatenate([wh[:, 64:128], wh[:, 64:128]], axis=1)

    def rows(k, step):
        return pk_ref[k, pl.ds(step, PAIRS, stride=RUN), :]

    def put(c, value, cot):
        y_ref[c] = value
        lhs_ref[c * H:(c + 1) * H, :] = halves(value)
        return value * cot

    def put_b(value):
        b_ref[...] = value
        lhs_ref[512:528, :] = halves(jnp.concatenate([value, jnp.zeros_like(value)], axis=0))

    p0, q0, w0, u0, s0, c0 = [rows(k, 0) for k in range(6)]
    for c in range(PAIRS):
        value = (
            p0[c:c + 1] * wn2 + q0[c:c + 1] * wr2 + w0[c:c + 1] * wz2 + u0[c:c + 1] * eye2
        )
        z_ref[c] = put(c, value, c0[c:c + 1])
    put_b(s0)

    def step(l, carry):
        p1, q1, w1, u1, s1, c1 = [rows(k, l) for k in range(6)]
        for c in range(PAIRS):
            if c % GROUP == 0:
                lhs = lhs_ref[c * H:(c + GROUP) * H, :]
                first, second = bdot(lhs, w1_ref[...]), bdot(lhs[:, :128], w2_ref[...])
            part = slice((c % GROUP) * H, (c % GROUP + 1) * H)
            n, r, z = gates_of(first[part], second[part])
            value = (
                u1[c:c + 1] * y_ref[c] + p1[c:c + 1] * n + q1[c:c + 1] * r + w1[c:c + 1] * z
            )
            z_ref[c] += put(c, value, c1[c:c + 1])
        lhs = lhs_ref[512:528, :]
        first, second = bdot(lhs, w1_ref[...]), bdot(lhs[:, :128], w2_ref[...])
        n, r, z = gates_of(first[:8], second[:8])
        put_b(u1 * b_ref[...] + p1 * n + q1 * r + w1 * z + s1)
        return carry

    lax.fori_loop(1, RUN, step, 0, unroll=True)

    low8 = iota((8, 128), 1) < H
    top8 = iota((8, 128), 0) == 0
    bs = b_ref[...]
    for c in range(PAIRS):
        y = y_ref[c]
        z = z_ref[c]
        offs = jnp.broadcast_to(bs[c:c + 1], (8, 128))
        for part in range(2):
            if part:
                y, z, offs = pltpu.roll(y, H, 1), pltpu.roll(z, H, 1), pltpu.roll(offs, H, 1)
            col = jnp.sum(jnp.where(low64, z, 0.0), axis=1, keepdims=True)
            n = c + part * PAIRS
            aug_ref[n, 0:64, :] = jnp.where(low64, y, jnp.where(lane64 == H, col, 0.0))
            aug_ref[n, 64:72, :] = jnp.where(low8 & top8, offs, 0.0)
    sups = []
    for k in range(4):
        left = combine(aug_ref[4 * k], aug_ref[4 * k + 1])
        right = combine(aug_ref[4 * k + 2], aug_ref[4 * k + 3])
        sups.append(combine(left, right))
        sup_ref[k] = sups[-1]
    total = combine(combine(sups[0], sups[1]), combine(sups[2], sups[3]))

    low32 = iota((32, 128), 1) < H
    body = jnp.where(low32, total[:32], pltpu.roll(total[32:64], H, 1))
    col = jnp.sum(jnp.where(lane64 == H, total[:64], 0.0), axis=1, keepdims=True)
    row_bc = jnp.where(low8[:1], total[64:65], 0.0) + to_row(col, H)
    last = jnp.sum(jnp.where(lane64 == 127, guess[:, 128:], 0.0), axis=1, keepdims=True)

    def head(a):
        return jnp.sum(jnp.where(lane64 == 0, a[:, :128], 0.0), axis=1, keepdims=True)

    row_gr = to_row(last, 0) + to_row(head(gi_r), H)
    row_zn = to_row(head(gi_z), 0) + to_row(head(gi_n), H)
    row8 = iota((8, 128), 0)
    tail = jnp.where(row8 == 0, row_bc, jnp.where(row8 == 1, row_gr, jnp.where(row8 == 2, row_zn, 0.0)))
    for k in range(HALF):
        send_ref[k, 0:32, :] = body
        send_ref[k, 32:40, :] = tail


def apply_kernel(
    me_ref, own_ref, other_ref, aug_ref, sup_ref, pk_ref, tl_ref, w1_ref, w2_ref, wt_ref, hb_ref,
    x_hbm, g_hbm,
    state_hbm, adj_hbm, keep_ref, give_ref,
    lhs_ref, z_ref, zt_ref, row_ref, bnd_ref, st_ref, lam_ref, x_ref, g_ref, sems,
    state_ref, adj_ref, out_sems,
):
    copies = fetch([(g_hbm, g_ref), (x_hbm, x_ref)], sems)
    me = me_ref[0]
    core = me % 2
    for k in range(3):
        row_ref[k, pl.ds(core, HALF, stride=2), :] = own_ref[:, 32 + k, :]
        row_ref[k, pl.ds(1 - core, HALF, stride=2), :] = other_ref[:, 32 + k, :]
    bc, gr, zn = row_ref[0], row_ref[1], row_ref[2]
    low16 = iota((HALF, 128), 1) < H

    def pair_low(a):
        return jnp.where(low16, a[:HALF], pltpu.roll(a[HALF:], H, 1))

    def pair_high(a):
        return jnp.where(low16, pltpu.roll(a[:HALF], H, 1), a[HALF:])

    gr_next = pltpu.roll(gr, DEV - 1, 0)
    zn_next = pltpu.roll(zn, DEV - 1, 0)
    prev = jnp.where((iota((HALF, 128), 0) == HALF - 1) & ~low16, 0.0, pair_low(gr))
    n, r, z = narrow_gates(prev, w1_ref, w2_ref)
    terms = gate_terms(
        pair_high(gr_next), pair_low(zn_next), pair_high(zn_next), r, z, n, hb_ref[0:1, :], prev
    )
    for k in range(6):
        bnd_ref[k] = terms[k]
    bnd_ref[6] = prev
    squash, p, q, w, u, shift = terms

    lane64 = iota((H, 128), 1)
    row64 = iota((H, 128), 0)
    low32 = iota((32, 128), 1) < H
    for ref, side in ((own_ref, core), (other_ref, 1 - core)):
        for k in range(HALF // 2):
            a, b = ref[k, 0:32, :], ref[k + HALF // 2, 0:32, :]
            top = jnp.where(low32, a, pltpu.roll(b, H, 1))
            bottom = jnp.where(low32, pltpu.roll(a, H, 1), b)
            value = jnp.concatenate([top, bottom], axis=0)
            z_ref[2 * k + side] = value
            start = pl.multiple_of((2 * k + side) * H, H)
            lhs_ref[pl.ds(start, H), :] = halves(value)
    offs = pair_low(bc)
    lhs_ref[HALF * H:, :] = halves(offs)
    for k in range(HALF):
        if k % GROUP == 0:
            lhs = lhs_ref[k * H:(k + GROUP) * H, :]
            first, second = bdot(lhs, w1_ref[...]), bdot(lhs[:, :128], w2_ref[...])
        part = slice((k % GROUP) * H, (k % GROUP + 1) * H)
        n, r, z = gates_of(first[part], second[part])
        value = u[k:k + 1] * z_ref[k] + p[k:k + 1] * n + q[k:k + 1] * r + w[k:k + 1] * z
        z_ref[k] = value
        if k % 2:
            zt_ref[k // 2] = jnp.concatenate([value, pltpu.roll(value, H, 1)], axis=0).T[:H]
    lhs = lhs_ref[HALF * H:, :]
    n, r, z = gates_of(bdot(lhs, w1_ref[...]), bdot(lhs[:, :128], w2_ref[...]))
    fwd_rows = u * offs + p * n + q * r + w * z + shift
    bwd_rows = pair_high(bc)
    empty = jnp.zeros((128 - HALF, 128), F32)
    fwd_cols = jnp.concatenate([fwd_rows, empty], axis=0).T
    bwd_cols = jnp.concatenate([bwd_rows, empty], axis=0).T

    lane1 = iota((1, 128), 1)
    low1 = lane1 < H
    eye_a = lane64 == row64
    eye_b = lane64 == row64 + H
    shift_last = shift[HALF - 1:HALF, :]
    x_col = jnp.sum(jnp.where(eye_b, shift_last, 0.0), axis=1, keepdims=True)
    lam_row = jnp.where(low1, 0.0, bwd_rows[HALF - 1:HALF, :])
    zero_col, zero_row = jnp.zeros((H, 1), F32), jnp.zeros((1, 128), F32)
    x_keep = jnp.where(me == 0, x_col, zero_col)
    lam_keep = zero_col
    x_rows, lam_rows = zero_row, jnp.where(me + 1 == DEV - 1, lam_row, zero_row)

    def half(k, row):
        return jnp.where(low1, row, 0.0) if k < HALF else jnp.where(low1, 0.0, row)

    def side_cols(cols, k):
        return jnp.where(lane64 == k % HALF, cols[:H] if k < HALF else cols[H:], 0.0)

    for i in range(DEV - 1):
        k, m = i, i % HALF
        if k % 2 == 0:
            x_row = half(k, jnp.sum(x_col * z_ref[m], axis=0, keepdims=True) + fwd_rows[m:m + 1])
            x_rows = jnp.where(me == k + 1, x_row, x_rows)
        else:
            x_col = jnp.sum(zt_ref[m // 2] * x_row + side_cols(fwd_cols, k), axis=1, keepdims=True)
            x_keep = jnp.where(me == k + 1, x_col, x_keep)
        k = DEV - 2 - i
        m = k % HALF
        if k % 2 == 0:
            lam_col = jnp.sum(z_ref[m] * lam_row + side_cols(bwd_cols, k), axis=1, keepdims=True)
            lam_keep = jnp.where(me + 1 == k, lam_col, lam_keep)
        else:
            lam_row = half(
                k, jnp.sum(lam_col * zt_ref[m // 2], axis=0, keepdims=True) + bwd_rows[m:m + 1]
            )
            lam_rows = jnp.where(me + 1 == k, lam_row, lam_rows)

    def settled(rows, column):
        row = jnp.where(low1, rows, 0.0) + jnp.where(low1, pltpu.roll(rows, H, 1), 0.0)
        return row + jnp.sum(jnp.where(eye_a, column, 0.0), axis=0, keepdims=True)

    x = settled(x_rows, x_keep)
    lam = settled(lam_rows, lam_keep)

    def boundary(k, index):
        row = bnd_ref[k, pl.ds(index % HALF, 1), :]
        return jnp.where(low1, jnp.where(index >= HALF, pltpu.roll(row, H, 1), row), 0.0)

    lam8 = jnp.broadcast_to(lam, (8, 128))
    mixed = jnp.concatenate([lam8 * boundary(k, me) for k in (1, 2, 3)], axis=1)
    carry = (pulled(mixed, wt_ref) + lam8 * boundary(4, me))[0:1]

    row72 = iota((72, 128), 0)
    eye72 = iota((72, 128), 1) == row72
    one = lane1 == H

    def ahead(maps, x):
        col = jnp.sum(jnp.where(eye72, x, 0.0), axis=1, keepdims=True)
        return jnp.where(one, 1.0, jnp.sum(col * maps, axis=0, keepdims=True))

    def back(maps, lam):
        col = jnp.sum(maps[:H] * lam, axis=1, keepdims=True)
        return jnp.where(one, 1.0, jnp.sum(jnp.where(eye_a, col, 0.0), axis=0, keepdims=True))

    starts = [jnp.where(one, 1.0, x)]
    for k in range(3):
        starts.append(ahead(sup_ref[k], starts[-1]))
    ends = [jnp.where(one, 1.0, carry)]
    for k in (3, 2, 1):
        ends.append(back(sup_ref[k], ends[-1]))
    ends = ends[::-1]
    state_rows, carry_rows = [None] * 16, [None] * 16
    for k in range(4):
        value, lam = starts[k], ends[k]
        for j in range(4):
            state_rows[4 * k + j] = value
            carry_rows[4 * k + 3 - j] = lam
            if j < 3:
                value = ahead(aug_ref[4 * k + j], value)
                lam = back(aug_ref[4 * k + 3 - j], lam)

    def gather(items):
        left = jnp.concatenate(items[:8], axis=0)
        right = jnp.concatenate(items[8:], axis=0)
        return jnp.where(iota((8, 128), 1) < H, left, pltpu.roll(right, H, 1))

    def rows(k, step):
        return pk_ref[k, pl.ds(step, PAIRS, stride=RUN), :]

    state, kappa = gather(state_rows), gather(carry_rows)
    for i in range(RUN):
        j = RUN - 1 - i
        n, r, z = narrow_gates(state, w1_ref, w2_ref)
        lam = rows(5, j) + kappa
        lam_ref[pl.ds(j, PAIRS, stride=RUN), :] = lam
        mixed = jnp.concatenate([lam * rows(0, j), lam * rows(1, j), lam * rows(2, j)], axis=1)
        kappa = pulled(mixed, wt_ref) + lam * rows(3, j)
        state = rows(3, i) * state + rows(0, i) * n + rows(1, i) * r + rows(2, i) * z + rows(4, i)
        st_ref[pl.ds(i, PAIRS, stride=RUN), :] = state

    states = st_ref[...].T
    state_ref[:, :128] = states[:H]
    state_ref[:, 128:] = states[H:]
    lams = lam_ref[...].T
    lams = jnp.concatenate([lams[:H], lams[H:]], axis=1)
    adj_ref[...] = lams
    results = fetch([(state_ref, state_hbm), (adj_ref, adj_hbm)], out_sems)

    before = (me + DEV - 1) % DEV
    first = iota((H, T), 1) == 0

    def with_first(a, k):
        col = jnp.sum(jnp.where(eye_a, boundary(k, before), 0.0), axis=1, keepdims=True)
        return jnp.where(first, col, a)

    for copy in copies:
        copy.wait()
    squash, p, q, w = [with_first(tl_ref[k], k) for k in range(4)]
    prev = with_first(pltpu.roll(g_ref[...], 1, 1), 6)
    left = jnp.concatenate([x_ref[...], prev, jnp.ones((8, T), F32)], axis=0)
    right = jnp.concatenate([lams * q, lams * w, lams * squash, lams * p], axis=0)
    sums = dot(left, right, ((1,), (1,)))
    row8 = iota((8, 128), 0)
    biases = jnp.where(
        row8 == 0, sums[128:136, :128], jnp.where(row8 == 1, sums[128:136, 128:], 0.0)
    )
    last = jnp.where(lane64 < H, sums[:64, 128:], sums[64:128, 128:])
    first_half = sums[:PART, :128]
    second_half = jnp.concatenate([sums[PART:128, :128], last, biases, jnp.zeros((8, 128), F32)], axis=0)
    keep_ref[...] = jnp.where(core == 0, first_half, second_half)
    give_ref[...] = jnp.where(core == 0, second_half, first_half)
    for copy in results:
        copy.wait()


def finish_kernel(me_ref, own_ref, other_ref, gin_ref, ghid_ref, gbias_ref, *, scale):
    core = me_ref[0] % 2
    own, other = own_ref[...] * scale, other_ref[...] * scale
    whole = jnp.concatenate(
        [jnp.where(core == 0, own, other), jnp.where(core == 0, other, own)], axis=0
    )
    gin_ref[:, :128] = whole[:64]
    gin_ref[:, 128:] = whole[128:192, :64]
    ghid_ref[:, :128] = whole[64:128]
    ghid_ref[:, 128:] = whole[128:192, 64:]
    gbias_ref[...] = whole[192:194]


def shape(*dims):
    return jax.ShapeDtypeStruct(dims, F32)


def swapped(a):
    return lax.ppermute(a, "tm", [(k, k ^ 1) for k in range(DEV)])


def summed_by_four(a, axis, stride):
    count = lax.axis_size(axis)
    first, second, third = [
        lax.ppermute(a, axis, [(k, k ^ (step * stride)) for k in range(count)]) for step in (1, 2, 3)
    ]
    return lax.optimization_barrier((first + third) + (a + second))


def per_device(inputs, guess, cotangent, w_input, w_hidden, bias):
    x = jnp.swapaxes(inputs[0], 0, 1)
    g = jnp.swapaxes(guess[0], 0, 1)
    c = jnp.swapaxes(cotangent[0], 0, 1)
    bias2 = bias.reshape(2, 128)
    x, g, c, w_input, w_hidden, bias2 = [
        pltpu.with_memory_space_constraint(a, pltpu.HBM)
        for a in (x, g, c, w_input, w_hidden, bias2)
    ]
    vmem = pl.BlockSpec(memory_space=pltpu.VMEM)
    hbm = pl.BlockSpec(memory_space=pltpu.HBM)
    smem = pl.BlockSpec(memory_space=pltpu.SMEM)
    wide = [pltpu.VMEM((H, T), F32)] * 3
    params = pltpu.CompilerParams(vmem_limit_bytes=VMEM_LIMIT)
    send, *kept = pl.pallas_call(
        blocks_kernel,
        out_shape=(
            shape(HALF, TILE, 128), shape(16, 72, 128), shape(4, 72, 128),
            shape(6, 128, 128), shape(4, H, T),
            jax.ShapeDtypeStruct((256, 512), BF16), jax.ShapeDtypeStruct((128, 256), BF16),
            jax.ShapeDtypeStruct((384, 256), BF16), shape(8, 128),
        ),
        in_specs=[hbm] * 6,
        out_specs=[vmem] * 9,
        scratch_shapes=[
            pltpu.VMEM((PAIRS, H, 128), F32),
            pltpu.VMEM((PAIRS, H, 128), F32),
            pltpu.VMEM((8, 128), F32),
            pltpu.VMEM((528, 256), BF16),
        ] + wide + [
            pltpu.VMEM((H, 192), F32),
            pltpu.VMEM((H, 192), F32),
            pltpu.VMEM((2, 128), F32),
            pltpu.SemaphoreType.DMA((6,)),
        ],
        compiler_params=params,
        name="blocks",
    )(x, g, c, w_input, w_hidden, bias2)
    groups = [[2 * k + core for k in range(HALF)] for core in range(2)]
    received = lax.all_to_all(send, "tm", 0, 0, axis_index_groups=groups)
    other = swapped(received)
    me = lax.axis_index("tm").astype(jnp.int32).reshape(1)
    states, adjoint, part, give = pl.pallas_call(
        apply_kernel,
        out_shape=(shape(H, T), shape(H, T), shape(PART, 128), shape(PART, 128)),
        in_specs=[smem] + [vmem] * 10 + [hbm] * 2,
        out_specs=[hbm] * 2 + [vmem] * 2,
        scratch_shapes=[
            pltpu.VMEM((HALF * H + 16, 256), BF16),
            pltpu.VMEM((HALF, H, 128), F32),
            pltpu.VMEM((HALF // 2, H, 128), F32),
            pltpu.VMEM((3, DEV, 128), F32),
            pltpu.VMEM((7, HALF, 128), F32),
            pltpu.VMEM((128, 128), F32),
            pltpu.VMEM((128, 128), F32),
        ] + wide[:2] + [pltpu.SemaphoreType.DMA((2,))] + wide[:2] + [pltpu.SemaphoreType.DMA((2,))],
        compiler_params=params,
        name="apply",
    )(me, received, other, *kept, x, g)
    part = part + swapped(give)
    for axis, stride in (("seq", 1), ("tm", 8), ("tm", 2)):
        part = summed_by_four(part, axis, stride)
    scale = 1.0 / math.sqrt(lax.axis_size("seq") * lax.axis_size("tm") * T)
    grad_input, grad_hidden, grad_bias = pl.pallas_call(
        functools.partial(finish_kernel, scale=scale),
        out_shape=(shape(H, 192), shape(H, 192), shape(2, 128)),
        in_specs=[smem, vmem, vmem],
        out_specs=[vmem] * 3,
        compiler_params=params,
        name="finish",
    )(me, part, swapped(part))
    grad_bias = grad_bias.reshape(256)
    return (
        jnp.swapaxes(states, 0, 1)[None], jnp.swapaxes(adjoint, 0, 1)[None],
        grad_input, grad_hidden, grad_bias,
    )


def solution(mesh):
    return jax.shard_map(
        per_device,
        mesh=mesh,
        in_specs=(P("seq", "tm", None), P("seq", "tm", None), P("seq", "tm", None), P(), P(), P()),
        out_specs=(P("seq", "tm", None), P("seq", "tm", None), P(), P(), P()),
        check_vma=False,
    )
```
